512 devices in a mesh: resp: 16 (over y_hi, x), head: 4 (over y_lo, core), grp: 8 (over z).
Axes of the slice: x: 4, y: 8 (y_hi: 4, y_lo: 2; y = y_hi * 2 + y_lo), z: 8, core: 2. Of those that a mesh axis runs over, the one named last changes fastest.
Arguments:
- q_prompt: bfloat16 [8, 1024, 32, 128], P('grp', 'resp', 'head'), may hold values from -6 to 6
- q_resp: bfloat16 [8, 16, 128, 32, 128], P('grp', 'resp', None, 'head'), may hold values from -6 to 6
- kv_prompt: bfloat16 [8, 2, 1024, 4, 128], P('grp', None, 'resp', 'head'), may hold values from -6 to 6
- kv_resp: bfloat16 [8, 16, 2, 128, 4, 128], P('grp', 'resp', None, None, 'head'), may hold values from -6 to 6
- dout_prompt: bfloat16 [8, 1024, 32, 128], P('grp', 'resp', 'head'), may hold values from -21 to 21
- dout_resp: bfloat16 [8, 16, 128, 32, 128], P('grp', 'resp', None, 'head'), may hold values from -21 to 21
- q_gain: float32 [128], replicated, may hold values from 0.1 to 1.9
- k_gain: float32 [128], replicated, may hold values from 0.1 to 1.9
- resp_len: int32 [8, 16], P('grp', 'resp'), may hold values from 16 to 128, as said below
- prompt_len: int32 [8], P('grp'), may hold values from 512 to 1024, as said below
Outputs:
- dq_prompt: bfloat16 [8, 1024, 32, 128], P('grp', 'resp', 'head')
- dq_resp: bfloat16 [8, 16, 128, 32, 128], P('grp', 'resp', None, 'head')
- dkv_prompt: bfloat16 [8, 2, 1024, 4, 128], P('grp', None, 'resp', 'head')
- dkv_resp: bfloat16 [8, 16, 2, 128, 4, 128], P('grp', 'resp', None, None, 'head')
- gain_grads: float32 [2, 128], replicated
The draws below stay inside these ranges and needn't reach their ends.
Inputs may be any that keep to these rules, and one draw needn't show every extreme that they name: `resp_len`: in every group some response uses all 128 positions. `prompt_len`: some group uses all 1024 prompt positions.
All inputs are finite; a program needn't handle non-finite values.
Results may differ from the reference program's by a relative error of at most 0.0098.
Values may be sent and summed in bfloat16 or wider, within the bound.
A program may use at most 64 MiB of HBM per device.

```python
import jax
import jax.numpy as jnp
from jax import lax

HD = 128
PL = 64
R = 128
KVH = 4
QH = 32
P_SIZE = 1024
RESPS = 16
GROUPS = 8


def rising_scale(group_place, shard_place):
    return (1.0 + 2.0 * group_place) * (1.0 + 2.0 * shard_place) / 3.0


def rough_base(key, shape):
    first_key = jax.random.fold_in(key, 0)
    return jnp.clip(jax.random.normal(first_key, shape, jnp.float32), -5.0, 5.0)


def draw_dout_prompt(key, part):
    key = jax.random.fold_in(key, 11)
    shape = (GROUPS, P_SIZE, QH, HD)
    group_place = jnp.arange(GROUPS, dtype=jnp.float32) / max(GROUPS - 1, 1)
    shard_place = (jnp.arange(P_SIZE, dtype=jnp.int32) // PL).astype(jnp.float32) / max(RESPS - 1, 1)
    factor = rising_scale(group_place[:, None], shard_place[None, :])[:, :, None, None]
    return (rough_base(key, shape) * factor).astype(jnp.bfloat16)


def draw_dout_resp(key, part):
    key = jax.random.fold_in(key, 17)
    shape = (GROUPS, RESPS, R, QH, HD)
    group_place = jnp.arange(GROUPS, dtype=jnp.float32) / max(GROUPS - 1, 1)
    shard_place = jnp.arange(RESPS, dtype=jnp.float32) / max(RESPS - 1, 1)
    factor = rising_scale(group_place[:, None], shard_place[None, :])[:, :, None, None, None]
    return (rough_base(key, shape) * factor).astype(jnp.bfloat16)


def draw_resp_len(key, part):
    key = jax.random.fold_in(key, 23)
    first_key, second_key = jax.random.split(key)
    lengths = jax.random.randint(first_key, (GROUPS, RESPS), R // 8, R + 1)
    chosen = jax.random.randint(second_key, (GROUPS, 1), 0, RESPS)
    places = jnp.arange(RESPS, dtype=jnp.int32)[None, :]
    return jnp.where(places == chosen, R, lengths).astype(jnp.int32)


def draw_prompt_len(key, part):
    key = jax.random.fold_in(key, 31)
    first_key, second_key = jax.random.split(key)
    lengths = jax.random.randint(first_key, (GROUPS,), P_SIZE // 2, P_SIZE + 1)
    chosen = jax.random.randint(second_key, (), 0, GROUPS)
    places = jnp.arange(GROUPS, dtype=jnp.int32)
    return jnp.where(places == chosen, P_SIZE, lengths).astype(jnp.int32)


def block_scale(key, dims, shards, low, high):
    level = 1.0
    for axis_at, parts in shards:
        draws = jax.random.uniform(jax.random.fold_in(jax.random.fold_in(key, 6), axis_at), (parts,), jnp.float32, low / len(shards), high / len(shards))
        level = level * jnp.repeat(jnp.exp(draws), dims[axis_at] // parts).reshape((-1,) + (1,) * (len(dims) - 1 - axis_at))
    return level


def bell_draw(rng, shape, scale, reach, cuts=(), kind=jnp.bfloat16):
    level = block_scale(rng, shape, cuts, -0.22, 0.18) if cuts else 1.0
    drawn = jax.random.normal(rng, shape, jnp.float32) * scale * level
    return jnp.minimum(jnp.maximum(drawn, -reach), reach).astype(kind)


def setup_inputs(seed: int = 0) -> dict:
    splits = jax.random.split(jax.random.key(seed), 11)
    q_prompt = bell_draw(splits[0], (GROUPS, P_SIZE, QH, HD), 1.0, 6.0, ((0, 8), (1, 16), (2, 4)))
    q_resp = bell_draw(splits[1], (GROUPS, RESPS, R, QH, HD), 1.0, 6.0, ((0, 8), (1, 16), (3, 4)))
    kv_prompt = bell_draw(splits[2], (GROUPS, 2, P_SIZE, KVH, HD), 1.0, 6.0, ((0, 8), (2, 16), (3, 4)))
    kv_resp = bell_draw(splits[3], (GROUPS, RESPS, 2, R, KVH, HD), 1.0, 6.0, ((0, 8), (1, 16), (4, 4)))
    dout_prompt = draw_dout_prompt(jax.random.fold_in(splits[10], 71), 0)
    dout_resp = draw_dout_resp(jax.random.fold_in(splits[10], 71), 0)
    q_gain = jnp.clip(1.0 + 0.18 * jax.random.normal(splits[6], (HD,), jnp.float32), 0.1, 1.9)
    k_gain = jnp.clip(1.0 + 0.18 * jax.random.normal(splits[7], (HD,), jnp.float32), 0.1, 1.9)
    resp_len = draw_resp_len(jax.random.fold_in(splits[10], 71), 0)
    prompt_len = draw_prompt_len(jax.random.fold_in(splits[10], 71), 0)
    return {"q_prompt": q_prompt, "q_resp": q_resp, "kv_prompt": kv_prompt, "kv_resp": kv_resp, "dout_prompt": dout_prompt, "dout_resp": dout_resp, "q_gain": q_gain, "k_gain": k_gain, "resp_len": resp_len, "prompt_len": prompt_len}


EPSILON = 1e-06

def normed(values_in, gain):
    floats = values_in.astype(jnp.float32)
    inverse = lax.rsqrt(lax.optimization_barrier(jnp.mean(floats * floats, axis=-1, keepdims=True)) + EPSILON)
    unit_rows = floats * inverse
    return ((unit_rows * gain).astype(jnp.bfloat16), unit_rows, inverse)

def norm_back(grad_normed, unit_rows, inverse, gain):
    grad_unit = grad_normed * gain
    return inverse * (grad_unit - unit_rows * lax.optimization_barrier(jnp.mean(grad_unit * unit_rows, axis=-1, keepdims=True)))

def block_grads(queries, key_rows, value_rows, douts, allowed):
    scale = queries.shape[-1] ** (-0.5)
    query_f = queries.astype(jnp.float32)
    key_f = key_rows.astype(jnp.float32)
    value_f = value_rows.astype(jnp.float32)
    dout_f = douts.astype(jnp.float32)
    scores = jnp.einsum('hqd,kd->hqk', query_f, key_f) * scale
    raw_weights = jnp.where(allowed[None], jnp.exp(scores), jnp.zeros_like(scores))
    weights = raw_weights / lax.optimization_barrier(jnp.sum(raw_weights, axis=-1, keepdims=True))
    weights_b = weights.astype(jnp.bfloat16)
    weights_f = weights_b.astype(jnp.float32)
    output = jnp.einsum('hqk,kd->hqd', weights_f, value_f)
    delta = lax.optimization_barrier(jnp.sum(dout_f * output, axis=-1, keepdims=True))
    grad_probs = jnp.einsum('hqd,kd->hqk', dout_f, value_f)
    grad_scores = (weights * (grad_probs - delta)).astype(jnp.bfloat16).astype(jnp.float32)
    grad_query = jnp.einsum('hqk,kd->hqd', grad_scores, key_f) * scale
    grad_key = jnp.einsum('hqk,hqd->kd', grad_scores, query_f) * scale
    grad_value = jnp.einsum('hqk,hqd->kd', weights_f, dout_f)
    return (grad_query, grad_key, grad_value)

def heads_of(values_in, head_index, group_heads):
    lower = head_index * group_heads
    return jnp.transpose(values_in[:, lower:lower + group_heads], (1, 0, 2))

def reference(q_prompt, q_resp, kv_prompt, kv_resp, dout_prompt, dout_resp, q_gain, k_gain, resp_len, prompt_len):

    def one_group(entries):
        query_in, kv_in, query_resp, kv_resp_in, dout_in, dout_resp_in, lengths, prompt_limit = entries
        prompt_total = query_in.shape[0]
        length = query_resp.shape[1]
        kv_heads = kv_in.shape[2]
        group_heads = query_in.shape[1] // kv_heads
        query_p, unit_qp, inverse_qp = normed(query_in, q_gain)
        key_p, unit_kp, inverse_kp = normed(kv_in[0], k_gain)
        values_p = kv_in[1]
        places = jnp.arange(prompt_total, dtype=jnp.int32)
        allow_pp = (places[None, :] <= places[:, None]) & (places[None, :] < prompt_limit)
        douts_p = jnp.where((places < prompt_limit)[:, None, None], dout_in, jnp.zeros_like(dout_in))
        prompt_q, prompt_k, prompt_v = ([], [], [])
        for head_index in range(kv_heads):
            grad_query, grad_key, grad_value = block_grads(heads_of(query_p, head_index, group_heads), key_p[:, head_index], values_p[:, head_index], heads_of(douts_p, head_index, group_heads), allow_pp)
            prompt_q.append(grad_query)
            prompt_k.append(grad_key)
            prompt_v.append(grad_value)
        grad_qp = jnp.transpose(jnp.concatenate(prompt_q, axis=0), (1, 0, 2))
        grad_kp = jnp.stack(prompt_k, axis=1)
        grad_vp = jnp.stack(prompt_v, axis=1)
        steps_r = jnp.arange(length, dtype=jnp.int32)
        allow_r = jnp.concatenate([jnp.broadcast_to(places[None, :] < prompt_limit, (length, prompt_total)), steps_r[None, :] <= steps_r[:, None]], axis=1)

        def one_resp(pieces):
            query_one, kv_one, dout_one, resp_used = pieces
            query_r, unit_qr, inverse_qr = normed(query_one, q_gain)
            key_r, unit_kr, inverse_kr = normed(kv_one[0], k_gain)
            douts_r = jnp.where((steps_r < resp_used)[:, None, None], dout_one, jnp.zeros_like(dout_one))
            resp_q, resp_k, resp_v = ([], [], [])
            for head_index in range(kv_heads):
                keys_all = jnp.concatenate([key_p[:, head_index], key_r[:, head_index]], axis=0)
                values_all = jnp.concatenate([values_p[:, head_index], kv_one[1][:, head_index]], axis=0)
                grad_query, grad_key, grad_value = block_grads(heads_of(query_r, head_index, group_heads), keys_all, values_all, heads_of(douts_r, head_index, group_heads), allow_r)
                resp_q.append(grad_query)
                resp_k.append(grad_key)
                resp_v.append(grad_value)
            grad_qr = jnp.transpose(jnp.concatenate(resp_q, axis=0), (1, 0, 2))
            grad_kr = jnp.stack(resp_k, axis=1)
            grad_vr = jnp.stack(resp_v, axis=1)
            dq_one = norm_back(grad_qr, unit_qr, inverse_qr, q_gain).astype(jnp.bfloat16)
            dk_one = norm_back(grad_kr[prompt_total:], unit_kr, inverse_kr, k_gain).astype(jnp.bfloat16)
            dkv_one = jnp.stack([dk_one, grad_vr[prompt_total:].astype(jnp.bfloat16)])
            query_term = lax.optimization_barrier(jnp.sum(grad_qr * unit_qr, axis=(0, 1)))
            key_term = lax.optimization_barrier(jnp.sum(grad_kr[prompt_total:] * unit_kr, axis=(0, 1)))
            return (dq_one, dkv_one, grad_kr[:prompt_total], grad_vr[:prompt_total], query_term, key_term)
        results = lax.map(one_resp, (query_resp, kv_resp_in, dout_resp_in, lengths))
        grad_key_all = grad_kp + lax.optimization_barrier(jnp.sum(results[2], axis=0))
        grad_value_all = grad_vp + lax.optimization_barrier(jnp.sum(results[3], axis=0))
        dq_group = norm_back(grad_qp, unit_qp, inverse_qp, q_gain).astype(jnp.bfloat16)
        dk_group = norm_back(grad_key_all, unit_kp, inverse_kp, k_gain).astype(jnp.bfloat16)
        dkv_group = jnp.stack([dk_group, grad_value_all.astype(jnp.bfloat16)])
        query_term = lax.optimization_barrier(jnp.sum(grad_qp * unit_qp, axis=(0, 1))) + lax.optimization_barrier(jnp.sum(results[4], axis=0))
        key_term = lax.optimization_barrier(jnp.sum(grad_key_all * unit_kp, axis=(0, 1))) + lax.optimization_barrier(jnp.sum(results[5], axis=0))
        return (dq_group, results[0], dkv_group, results[1], query_term, key_term)
    outputs = lax.map(one_group, (q_prompt, kv_prompt, q_resp, kv_resp, dout_prompt, dout_resp, resp_len, prompt_len))
    gain_grads = jnp.stack([lax.optimization_barrier(jnp.sum(outputs[4], axis=0)), lax.optimization_barrier(jnp.sum(outputs[5], axis=0))])
    return (outputs[0], outputs[1], outputs[2], outputs[3], gain_grads)
```

```python
import functools
import math

import jax
import jax.numpy as jnp
from jax import lax
from jax.experimental import pallas as pl
from jax.experimental.pallas import tpu as pltpu
from jax.sharding import PartitionSpec as P

EPSILON = 1e-06
MESH = pl.DeviceIdType.MESH
HD = 128
BF = jnp.bfloat16
F32 = jnp.float32
NX = 4
NY = 4
TILE = 256
NT = (((1,), (1,)), ((), ()))
NN = (((1,), (0,)), ((), ()))


def dot(lhs, rhs, dims=NN):
    return lax.dot_general(lhs, rhs, dims, preferred_element_type=F32)


def order(step):
    return step + step // 2 - 2 * (step // 3)


def kernel(
    qr_in,
    qp_in,
    kvp_in,
    kvr_in,
    dr_in,
    dp_in,
    qg_in,
    kg_in,
    rlen_in,
    plen_in,
    dqr_out,
    dqp_out,
    dkvp_out,
    dkvr_out,
    gains_out,
    qg_ref,
    kg_ref,
    rlen_ref,
    plen_ref,
    q_nat,
    d_nat,
    kvr,
    kall,
    unit_qt,
    inv_q,
    qnt,
    qn,
    dt,
    dst,
    delta_ref,
    gcol,
    kn_ref,
    knt_ref,
    uk_ref,
    vt1,
    knr,
    knrt,
    ukr,
    e_ref,
    er_ref,
    ol,
    gqt,
    sums,
    part,
    rx,
    own,
    ys,
    ry,
    kterm,
    gsend,
    grecv,
    dq_v,
    dkvp_v,
    dkvr_v,
    in_sem,
    out_sem,
    kv_recv,
    kvy_send,
    kvx_send,
    rx_recv,
    rx_send,
    ry_recv,
    ry_send,
    g_recv,
    g_send,
):
    resp = lax.axis_index("resp")
    head = lax.axis_index("head")
    grp = lax.axis_index("grp")
    yh = resp // NX
    x = lax.rem(resp, NX)
    yl = head // 2
    core = lax.rem(head, 2)
    ngrp = 8
    y8 = 2 * yh + yl
    rows_r = qr_in.shape[0]
    rows_p = qp_in.shape[0]
    rows = rows_r + rows_p
    tiles = rows // TILE
    tiles_r = rows_r // TILE
    scale = HD**-0.5
    exp_scale = scale * math.log2(math.e)

    def partner(stage, k):
        if stage == 0:
            return {"grp": lax.rem(grp + k, ngrp)}
        if stage == 1:
            to = lax.rem(y8 + k, 8)
            return {"resp": (to // 2) * NX + x, "head": lax.rem(to, 2) * 2 + core}
        to = lax.rem(2 * x + core + k, 8)
        return {"resp": yh * NX + to // 2, "head": yl * 2 + lax.rem(to, 2)}

    stage_at = (grp, y8, 2 * x + core)

    barrier = pltpu.get_barrier_semaphore()
    for stage in range(3):
        for k in range(1, 8):
            pl.semaphore_signal(
                barrier, inc=1, device_id=partner(stage, k), device_id_type=MESH
            )

    loads = [
        pltpu.make_async_copy(kvp_in, kall.at[resp], in_sem.at[0]),
        pltpu.make_async_copy(qr_in, q_nat.at[pl.ds(0, rows_r)], in_sem.at[1]),
        pltpu.make_async_copy(qp_in, q_nat.at[pl.ds(rows_r, rows_p)], in_sem.at[2]),
        pltpu.make_async_copy(kvr_in, kvr, in_sem.at[3]),
        pltpu.make_async_copy(dr_in, d_nat.at[pl.ds(0, rows_r)], in_sem.at[4]),
        pltpu.make_async_copy(dp_in, d_nat.at[pl.ds(rows_r, rows_p)], in_sem.at[5]),
        pltpu.make_async_copy(qg_in, qg_ref, in_sem.at[6]),
        pltpu.make_async_copy(kg_in, kg_ref, in_sem.at[7]),
        pltpu.make_async_copy(rlen_in, rlen_ref, in_sem.at[8]),
        pltpu.make_async_copy(plen_in, plen_ref, in_sem.at[9]),
    ]
    for load in loads:
        load.start()

    for load in loads[6:]:
        load.wait()
    plen = plen_ref[0]
    rlen = rlen_ref[0, 0]

    gcol[...] = jnp.broadcast_to(qg_ref[...], (TILE, HD)).T
    loads[1].wait()
    loads[2].wait()
    for n in range(tiles):
        sl = pl.ds(n * TILE, TILE)
        xt = q_nat[sl, :].T.astype(F32)
        inv = lax.rsqrt(jnp.mean(xt * xt, axis=0, keepdims=True) + EPSILON)
        ut = xt * inv
        unit_qt[:, sl] = ut
        inv_q[:, sl] = jnp.broadcast_to(inv, (8, TILE))
        qt = (ut * gcol[...]).astype(BF)
        qnt[:, sl] = qt
        qn[sl, :] = qt.T

    loads[0].wait()
    pl.semaphore_wait(barrier, 21)

    def y_copy(dy):
        to = lax.rem(yh + dy, NY) * NX + x
        return pltpu.make_async_remote_copy(
            src_ref=kall.at[resp],
            dst_ref=kall.at[resp],
            send_sem=kvy_send.at[dy - 1],
            recv_sem=kv_recv.at[resp],
            device_id={"resp": to},
            device_id_type=MESH,
        )

    def x_copy(step, dx):
        block = lax.rem(yh + order(step), NY) * NX + x
        return pltpu.make_async_remote_copy(
            src_ref=kall.at[block],
            dst_ref=kall.at[block],
            send_sem=kvx_send.at[step, dx - 1],
            recv_sem=kv_recv.at[block],
            device_id={"resp": yh * NX + lax.rem(x + dx, NX)},
            device_id_type=MESH,
        )

    def wait_block(block):
        pltpu.make_async_remote_copy(
            src_ref=kall.at[block],
            dst_ref=kall.at[block],
            send_sem=kvy_send.at[0],
            recv_sem=kv_recv.at[block],
            device_id={"resp": lax.rem(resp + 1, NX * NY)},
            device_id_type=MESH,
        ).wait_recv()

    for dy in (1, 3, 2):
        y_copy(dy).start()
    for dx in (1, 3, 2):
        x_copy(0, dx).start()

    loads[4].wait()
    loads[5].wait()
    for n in range(tiles):
        sl = pl.ds(n * TILE, TILE)
        lane = lax.broadcasted_iota(jnp.int32, (HD, TILE), 1) + n * TILE
        if n < tiles_r:
            keep = lane < rlen * 8
        else:
            keep = lane - rows_r < (plen - rows_p // 8 * resp) * 8
        dt[:, sl] = jnp.where(keep, d_nat[sl, :].T.astype(F32), 0.0)

    loads[3].wait()
    kf = kvr[0].astype(F32)
    inv_kr = lax.rsqrt(jnp.mean(kf * kf, axis=-1, keepdims=True) + EPSILON)
    ur = kf * inv_kr
    ukr[...] = ur
    kr = (ur * kg_ref[...]).astype(BF)
    knr[...] = kr
    knrt[...] = kr.T
    nkr = kr.shape[0]
    vt1[pl.ds(0, HD), pl.ds(0, nkr)] = kvr[1].T
    vt1[pl.ds(HD, 16), pl.ds(0, nkr)] = jnp.ones((16, nkr), BF)
    for n in range(tiles):
        sl = pl.ds(n * TILE, TILE)
        if n < tiles_r:
            s = dot(knr[...], qnt[:, sl])
            at = lax.broadcasted_iota(jnp.int32, s.shape, 0)
            lane = lax.broadcasted_iota(jnp.int32, s.shape, 1) + n * TILE
            e = jnp.where(at * 8 <= lane, jnp.exp2(s * exp_scale), 0.0).astype(BF)
            er_ref[:, sl] = e
            ol[:, sl] = dot(vt1[:, pl.ds(0, nkr)], e)
        else:
            ol[:, sl] = jnp.zeros((HD + 16, TILE), F32)

    def pass1(step, carry):
        chunk = lax.rem(yh + order(step), NY)

        @pl.when(step < NY - 1)
        def _():
            wait_block(lax.rem(yh + order(step + 1), NY) * NX + x)
            for dx in (1, 3, 2):
                x_copy(step + 1, dx).start()

        for dx in (1, 3, 2):
            wait_block(chunk * NX + lax.rem(x + dx, NX))

        n_keys = NX * kall.shape[2]
        at = lax.broadcasted_iota(jnp.int32, (n_keys, HD), 0) + chunk * n_keys
        k_raw = kall[pl.ds(chunk * NX, NX), 0].reshape(n_keys, HD).astype(F32)
        inv = lax.rsqrt(jnp.mean(k_raw * k_raw, axis=-1, keepdims=True) + EPSILON)
        unit = k_raw * inv
        uk_ref[step] = unit
        kf = unit * kg_ref[...]
        kn = kf.astype(BF)
        kn_ref[step] = kn
        knt_ref[step] = jnp.where(at < plen, kf, 0.0).astype(BF).T
        v = kall[pl.ds(chunk * NX, NX), 1].reshape(n_keys, HD).astype(F32)
        vt1[pl.ds(0, HD), :] = jnp.where(at < plen, v, 0.0).astype(BF).T
        lane = lax.broadcasted_iota(jnp.int32, (16, n_keys), 1) + chunk * n_keys
        vt1[pl.ds(HD, 16), :] = jnp.where(lane < plen, 1.0, 0.0).astype(BF)
        for n in range(tiles):
            sl = pl.ds(n * TILE, TILE)
            s = dot(kn, qnt[:, sl])
            e = jnp.exp2(s * exp_scale)
            if n >= tiles_r:
                key = lax.broadcasted_iota(jnp.int32, s.shape, 0)
                lane = lax.broadcasted_iota(jnp.int32, s.shape, 1) + (n * TILE - rows_r)
                ahead = resp * (rows_p // 8) - chunk * n_keys
                e = jnp.where((key - ahead) * 8 <= lane, e, 0.0)
            e = e.astype(BF)
            e_ref[step, :, sl] = e
            ol[:, sl] += dot(vt1[...], e)
        return carry

    lax.fori_loop(0, NY, pass1, 0)

    for n in range(tiles):
        sl = pl.ds(n * TILE, TILE)
        rl = 1.0 / ol[pl.ds(HD, 1), sl]
        ds = (dt[:, sl] * rl).astype(BF)
        dst[:, sl] = ds
        delta = rl * jnp.sum(ds.astype(F32) * ol[pl.ds(0, HD), sl], axis=0, keepdims=True)
        delta_ref[:, sl] = jnp.broadcast_to(delta, (8, TILE))
        gqt[:, sl] = jnp.zeros((HD, TILE), F32)
    kterm[...] = jnp.zeros((8, HD), F32)

    def x_sum(step, dx):
        return pltpu.make_async_remote_copy(
            src_ref=part.at[step, lax.rem(x + dx, NX)],
            dst_ref=rx.at[step, dx - 1],
            send_sem=rx_send.at[step, dx - 1],
            recv_sem=rx_recv.at[step, dx - 1],
            device_id={"resp": yh * NX + lax.rem(x + dx, NX)},
            device_id_type=MESH,
        )

    def y_sum(step):
        dy = order(step)
        return pltpu.make_async_remote_copy(
            src_ref=ys.at[step],
            dst_ref=ry.at[dy - 1],
            send_sem=ry_send.at[step],
            recv_sem=ry_recv.at[dy - 1],
            device_id={"resp": lax.rem(yh + dy, NY) * NX + x},
            device_id_type=MESH,
        )

    def summed(step, which):
        total = own[step, which]
        for k in range(NX - 1):
            total = total + rx[step, k, which].astype(F32)
        return total

    span = kall.shape[2]

    def pass2(back, carry):
        step = NY - 1 - back
        chunk = lax.rem(yh + order(step), NY)
        n_keys = NX * span
        v = kall[pl.ds(chunk * NX, NX), 1].reshape(n_keys, HD)
        gk = jnp.zeros((n_keys, HD), F32)
        gv = jnp.zeros((n_keys, HD), F32)
        for n in range(tiles):
            sl = pl.ds(n * TILE, TILE)
            e = e_ref[step, :, sl]
            dp = dot(v, dst[:, sl])
            gs = (e.astype(F32) * (dp - delta_ref[pl.ds(0, 1), sl])).astype(BF)
            gk += dot(gs, qn[sl, :])
            gv += dot(e, dst[:, sl], NT)
            gqt[:, sl] += dot(knt_ref[step], gs)
        at = lax.broadcasted_iota(jnp.int32, (n_keys, HD), 0) + chunk * n_keys
        gk = jnp.where(at < plen, gk * scale, 0.0)
        gv = jnp.where(at < plen, gv, 0.0)
        kterm[...] += jnp.sum((gk * uk_ref[step]).reshape(n_keys // 8, 8, HD), axis=0)
        sums[0] = gk
        sums[1] = gv
        for which in range(2):
            for k in range(NX):
                part[step, k, which] = sums[which, pl.ds(k * span, span)].astype(BF)
            own[step, which] = sums[which, pl.ds(x * span, span)]
        for dx in (2, 1, 3):
            x_sum(step, dx).start()

        @pl.when(back == 0)
        def _():
            gkr = jnp.zeros((nkr, HD), F32)
            gvr = jnp.zeros((nkr, HD), F32)
            for n in range(tiles_r):
                sl = pl.ds(n * TILE, TILE)
                e = er_ref[:, sl]
                dp = dot(kvr[1], dst[:, sl])
                gs = (e.astype(F32) * (dp - delta_ref[pl.ds(0, 1), sl])).astype(BF)
                gkr += dot(gs, qn[sl, :])
                gvr += dot(e, dst[:, sl], NT)
                gqt[:, sl] += dot(knrt[...], gs)
            gkr = gkr * scale
            ur = ukr[...]
            kterm[...] += jnp.sum((gkr * ur).reshape(nkr // 8, 8, HD), axis=0)
            kf = kvr[0].astype(F32)
            inv = lax.rsqrt(jnp.mean(kf * kf, axis=-1, keepdims=True) + EPSILON)
            gu = gkr * kg_ref[...]
            dk = inv * (gu - ur * jnp.mean(gu * ur, axis=-1, keepdims=True))
            dkvr_v[0] = dk.astype(BF)
            dkvr_v[1] = gvr.astype(BF)

        @pl.when(back > 0)
        def _():
            before = step + 1
            for dx in (2, 1, 3):
                x_sum(before, dx).wait_recv()
            for which in range(2):
                ys[before, which] = summed(before, which).astype(BF)
            y_sum(before).start()

        return carry

    lax.fori_loop(0, NY, pass2, 0)

    stores = [
        pltpu.make_async_copy(dkvr_v, dkvr_out, out_sem.at[0]),
        pltpu.make_async_copy(dq_v.at[pl.ds(0, rows_r)], dqr_out, out_sem.at[1]),
        pltpu.make_async_copy(dq_v.at[pl.ds(rows_r, rows_p)], dqp_out, out_sem.at[2]),
        pltpu.make_async_copy(dkvp_v, dkvp_out, out_sem.at[3]),
        pltpu.make_async_copy(gsend.at[3, pl.ds(0, 2)], gains_out, out_sem.at[4]),
    ]
    stores[0].start()

    prod = jnp.zeros((HD, HD), F32)
    for n in range(rows // HD):
        sl = pl.ds(n * HD, HD)
        prod += gqt[:, sl] * unit_qt[:, sl]
    qterm = jnp.sum(prod.T, axis=0, keepdims=True) * scale
    key_sum = jnp.sum(kterm[...], axis=0, keepdims=True)
    which_row = lax.broadcasted_iota(jnp.int32, (8, HD), 0)
    gsend[0] = jnp.where(
        which_row == 0,
        jnp.broadcast_to(qterm, (8, HD)),
        jnp.where(which_row == 1, jnp.broadcast_to(key_sum, (8, HD)), 0.0),
    )

    def g_copy(stage, k):
        return pltpu.make_async_remote_copy(
            src_ref=gsend.at[stage],
            dst_ref=grecv.at[stage, stage_at[stage]],
            send_sem=g_send.at[stage, k - 1],
            recv_sem=g_recv.at[stage, k - 1],
            device_id=partner(stage, k),
            device_id_type=MESH,
        )

    def g_start(stage):
        for k in range(1, 8):
            g_copy(stage, k).start()
        grecv[stage, stage_at[stage]] = gsend[stage]

    def g_finish(stage):
        for k in range(1, 8):
            g_copy(stage, k).wait_recv()
        total = grecv[stage, 0]
        for k in range(1, 8):
            total = total + grecv[stage, k]
        gsend[stage + 1] = total

    g_start(0)

    for n in range(tiles):
        sl = pl.ds(n * TILE, TILE)
        ut = unit_qt[:, sl]
        gu = gqt[:, sl] * scale * gcol[...]
        back = inv_q[pl.ds(0, 1), sl] * (gu - ut * jnp.mean(gu * ut, axis=0, keepdims=True))
        dq_v[sl, :] = back.astype(BF).T
    stores[1].start()
    stores[2].start()

    g_finish(0)
    g_start(1)

    for dx in (2, 1, 3):
        x_sum(0, dx).wait_recv()

    g_finish(1)
    g_start(2)

    for step in range(1, NY):
        y_sum(step).wait_recv()
    totals = []
    for which in range(2):
        total = summed(0, which)
        for k in range(NY - 1):
            total = total + ry[k, which].astype(F32)
        totals.append(total)
    unit = uk_ref[0, pl.ds(x * span, span), :]
    kf = kall[resp, 0].astype(F32)
    inv = lax.rsqrt(jnp.mean(kf * kf, axis=-1, keepdims=True) + EPSILON)
    gu = totals[0] * kg_ref[...]
    dk = inv * (gu - unit * jnp.mean(gu * unit, axis=-1, keepdims=True))
    dkvp_v[0] = dk.astype(BF)
    dkvp_v[1] = totals[1].astype(BF)
    stores[3].start()

    g_finish(2)
    stores[4].start()

    for dy in (1, 3, 2):
        y_copy(dy).wait_send()
    for step in range(NY):
        for dx in (1, 3, 2):
            x_copy(step, dx).wait_send()
            x_sum(step, dx).wait_send()
    for step in range(1, NY):
        y_sum(step).wait_send()
    for stage in range(3):
        for k in range(1, 8):
            g_copy(stage, k).wait_send()
    for store in stores:
        store.wait()


def shards(
    q_prompt,
    q_resp,
    kv_prompt,
    kv_resp,
    dout_prompt,
    dout_resp,
    q_gain,
    k_gain,
    resp_len,
    prompt_len,
):
    span = q_prompt.shape[1]
    length = q_resp.shape[2]
    rows_r = length * 8
    rows_p = span * 8
    rows = rows_r + rows_p
    n_keys = NX * span
    any_spec = pl.BlockSpec(memory_space=pl.ANY)
    hbm = pl.BlockSpec(memory_space=pltpu.HBM)
    dma = pltpu.SemaphoreType.DMA
    out = pl.pallas_call(
        kernel,
        out_shape=(
            jax.ShapeDtypeStruct((rows_r, HD), BF),
            jax.ShapeDtypeStruct((rows_p, HD), BF),
            jax.ShapeDtypeStruct((2, span, HD), BF),
            jax.ShapeDtypeStruct((2, length, HD), BF),
            jax.ShapeDtypeStruct((2, HD), F32),
        ),
        in_specs=[hbm] * 10,
        out_specs=[any_spec] * 5,
        scratch_shapes=[
            pltpu.VMEM((1, HD), F32),
            pltpu.VMEM((1, HD), F32),
            pltpu.SMEM((1, 1), jnp.int32),
            pltpu.SMEM((1,), jnp.int32),
            pltpu.VMEM((rows, HD), BF),
            pltpu.VMEM((rows, HD), BF),
            pltpu.VMEM((2, length, HD), BF),
            pltpu.VMEM((NX * NY, 2, span, HD), BF),
            pltpu.VMEM((HD, rows), F32),
            pltpu.VMEM((8, rows), F32),
            pltpu.VMEM((HD, rows), BF),
            pltpu.VMEM((rows, HD), BF),
            pltpu.VMEM((HD, rows), F32),
            pltpu.VMEM((HD, rows), BF),
            pltpu.VMEM((8, rows), F32),
            pltpu.VMEM((HD, TILE), F32),
            pltpu.VMEM((NY, n_keys, HD), BF),
            pltpu.VMEM((NY, HD, n_keys), BF),
            pltpu.VMEM((NY, n_keys, HD), F32),
            pltpu.VMEM((HD + 16, n_keys), BF),
            pltpu.VMEM((length, HD), BF),
            pltpu.VMEM((HD, length), BF),
            pltpu.VMEM((length, HD), F32),
            pltpu.VMEM((NY, n_keys, rows), BF),
            pltpu.VMEM((length, rows_r), BF),
            pltpu.VMEM((HD + 16, rows), F32),
            pltpu.VMEM((HD, rows), F32),
            pltpu.VMEM((2, n_keys, HD), F32),
            pltpu.VMEM((NY, NX, 2, span, HD), BF),
            pltpu.VMEM((NY, NX - 1, 2, span, HD), BF),
            pltpu.VMEM((NY, 2, span, HD), F32),
            pltpu.VMEM((NY, 2, span, HD), BF),
            pltpu.VMEM((NY - 1, 2, span, HD), BF),
            pltpu.VMEM((8, HD), F32),
            pltpu.VMEM((4, 8, HD), F32),
            pltpu.VMEM((3, 8, 8, HD), F32),
            pltpu.VMEM((rows, HD), BF),
            pltpu.VMEM((2, span, HD), BF),
            pltpu.VMEM((2, length, HD), BF),
            dma((10,)),
            dma((5,)),
            dma((NX * NY,)),
            dma((NY - 1,)),
            dma((NY, NX - 1)),
            dma((NY, NX - 1)),
            dma((NY, NX - 1)),
            dma((NY - 1,)),
            dma((NY,)),
            dma((3, 7)),
            dma((3, 7)),
        ],
        compiler_params=pltpu.CompilerParams(
            collective_id=0, has_side_effects=True
        ),
        name="attention_grads",
    )(
        q_resp.reshape(rows_r, HD),
        q_prompt.reshape(rows_p, HD),
        kv_prompt.reshape(2, span, HD),
        kv_resp.reshape(2, length, HD),
        dout_resp.reshape(rows_r, HD),
        dout_prompt.reshape(rows_p, HD),
        q_gain.reshape(1, HD),
        k_gain.reshape(1, HD),
        resp_len,
        prompt_len,
    )
    return (
        out[1].reshape(q_prompt.shape),
        out[0].reshape(q_resp.shape),
        out[2].reshape(kv_prompt.shape),
        out[3].reshape(kv_resp.shape),
        out[4],
    )


def solution(mesh):
    return jax.shard_map(
        shards,
        mesh=mesh,
        in_specs=(
            P("grp", "resp", "head", None),
            P("grp", "resp", None, "head", None),
            P("grp", None, "resp", "head", None),
            P("grp", "resp", None, None, "head", None),
            P("grp", "resp", "head", None),
            P("grp", "resp", None, "head", None),
            P(),
            P(),
            P("grp", "resp"),
            P("grp"),
        ),
        out_specs=(
            P("grp", "resp", "head", None),
            P("grp", "resp", None, "head", None),
            P("grp", None, "resp", "head", None),
            P("grp", "resp", None, None, "head", None),
            P(),
        ),
        check_vma=False,
    )
```

```python
import functools
import math

import jax
import jax.numpy as jnp
from jax import lax
from jax.experimental import pallas as pl
from jax.experimental.pallas import tpu as pltpu
from jax.sharding import PartitionSpec as P

EPSILON = 1e-06
MESH = pl.DeviceIdType.MESH
HD = 128
BF = jnp.bfloat16
F32 = jnp.float32
NX = 4
NY = 4
TILE = 512
NT = (((1,), (1,)), ((), ()))
NN = (((1,), (0,)), ((), ()))


def dot(lhs, rhs, dims=NN):
    return lax.dot_general(lhs, rhs, dims, preferred_element_type=F32)


def order(step):
    return step + step // 2 - 2 * (step // 3)


def kernel(
    qr_in,
    qp_in,
    kvp_in,
    kvr_in,
    dr_in,
    dp_in,
    qg_in,
    kg_in,
    rlen_in,
    plen_in,
    dqr_out,
    dqp_out,
    dkvp_out,
    dkvr_out,
    gains_out,
    qg_ref,
    kg_ref,
    rlen_ref,
    plen_ref,
    q_nat,
    d_nat,
    kvr,
    kall,
    unit_qt,
    inv_q,
    qnt,
    qn,
    dt,
    dst,
    delta_ref,
    gcol,
    kn_ref,
    knt_ref,
    uk_ref,
    vt1,
    knr,
    knrt,
    ukr,
    e_ref,
    er_ref,
    ol,
    gqt,
    sums,
    part,
    rx,
    own,
    ys,
    ry,
    kterm,
    gsend,
    grecv,
    dq_v,
    dkvp_v,
    dkvr_v,
    in_sem,
    out_sem,
    kv_recv,
    kvy_send,
    kvx_send,
    rx_recv,
    rx_send,
    ry_recv,
    ry_send,
    g_recv,
    g_send,
):
    resp = lax.axis_index("resp")
    head = lax.axis_index("head")
    grp = lax.axis_index("grp")
    yh = resp // NX
    x = lax.rem(resp, NX)
    yl = head // 2
    core = lax.rem(head, 2)
    ngrp = 8
    y8 = 2 * yh + yl
    rows_r = qr_in.shape[0]
    rows_p = qp_in.shape[0]
    rows = rows_r + rows_p
    tiles = rows // TILE
    tiles_r = rows_r // TILE
    scale = HD**-0.5
    exp_scale = scale * math.log2(math.e)

    def partner(stage, k):
        if stage == 0:
            return {"grp": lax.rem(grp + k, ngrp)}
        if stage == 1:
            to = lax.rem(y8 + k, 8)
            return {"resp": (to // 2) * NX + x, "head": lax.rem(to, 2) * 2 + core}
        to = lax.rem(2 * x + core + k, 8)
        return {"resp": yh * NX + to // 2, "head": yl * 2 + lax.rem(to, 2)}

    stage_at = (grp, y8, 2 * x + core)

    barrier = pltpu.get_barrier_semaphore()
    for stage in range(3):
        for k in range(1, 8):
            pl.semaphore_signal(
                barrier, inc=1, device_id=partner(stage, k), device_id_type=MESH
            )

    loads = [
        pltpu.make_async_copy(kvp_in, kall.at[resp], in_sem.at[0]),
        pltpu.make_async_copy(qr_in, q_nat.at[pl.ds(0, rows_r)], in_sem.at[1]),
        pltpu.make_async_copy(qp_in, q_nat.at[pl.ds(rows_r, rows_p)], in_sem.at[2]),
        pltpu.make_async_copy(kvr_in, kvr, in_sem.at[3]),
        pltpu.make_async_copy(dr_in, d_nat.at[pl.ds(0, rows_r)], in_sem.at[4]),
        pltpu.make_async_copy(dp_in, d_nat.at[pl.ds(rows_r, rows_p)], in_sem.at[5]),
        pltpu.make_async_copy(qg_in, qg_ref, in_sem.at[6]),
        pltpu.make_async_copy(kg_in, kg_ref, in_sem.at[7]),
        pltpu.make_async_copy(rlen_in, rlen_ref, in_sem.at[8]),
        pltpu.make_async_copy(plen_in, plen_ref, in_sem.at[9]),
    ]
    for load in loads:
        load.start()

    loads[0].wait()
    pl.semaphore_wait(barrier, 21)

    def y_copy(dy):
        to = lax.rem(yh + dy, NY) * NX + x
        return pltpu.make_async_remote_copy(
            src_ref=kall.at[resp],
            dst_ref=kall.at[resp],
            send_sem=kvy_send.at[dy - 1],
            recv_sem=kv_recv.at[resp],
            device_id={"resp": to},
            device_id_type=MESH,
        )

    def x_copy(step, dx):
        block = lax.rem(yh + order(step), NY) * NX + x
        return pltpu.make_async_remote_copy(
            src_ref=kall.at[block],
            dst_ref=kall.at[block],
            send_sem=kvx_send.at[step, dx - 1],
            recv_sem=kv_recv.at[block],
            device_id={"resp": yh * NX + lax.rem(x + dx, NX)},
            device_id_type=MESH,
        )

    def wait_block(block):
        pltpu.make_async_remote_copy(
            src_ref=kall.at[block],
            dst_ref=kall.at[block],
            send_sem=kvy_send.at[0],
            recv_sem=kv_recv.at[block],
            device_id={"resp": lax.rem(resp + 1, NX * NY)},
            device_id_type=MESH,
        ).wait_recv()

    for dy in (1, 3, 2):
        y_copy(dy).start()
    for dx in (1, 3, 2):
        x_copy(0, dx).start()

    for load in loads[6:]:
        load.wait()
    plen = plen_ref[0]
    rlen = rlen_ref[0, 0]

    gcol[...] = jnp.broadcast_to(qg_ref[...], (TILE, HD)).T
    loads[1].wait()
    loads[2].wait()
    for n in range(tiles):
        sl = pl.ds(n * TILE, TILE)
        xt = q_nat[sl, :].T.astype(F32)
        inv = lax.rsqrt(jnp.mean(xt * xt, axis=0, keepdims=True) + EPSILON)
        ut = xt * inv
        unit_qt[:, sl] = ut
        inv_q[:, sl] = jnp.broadcast_to(inv, (8, TILE))
        qt = (ut * gcol[...]).astype(BF)
        qnt[:, sl] = qt
        qn[sl, :] = qt.T

    loads[4].wait()
    loads[5].wait()
    for n in range(tiles):
        sl = pl.ds(n * TILE, TILE)
        lane = lax.broadcasted_iota(jnp.int32, (HD, TILE), 1) + n * TILE
        if n < tiles_r:
            keep = lane < rlen * 8
        else:
            keep = lane - rows_r < (plen - rows_p // 8 * resp) * 8
        dt[:, sl] = jnp.where(keep, d_nat[sl, :].T.astype(F32), 0.0)

    loads[3].wait()
    kf = kvr[0].astype(F32)
    inv_kr = lax.rsqrt(jnp.mean(kf * kf, axis=-1, keepdims=True) + EPSILON)
    ur = kf * inv_kr
    ukr[...] = ur
    kr = (ur * kg_ref[...]).astype(BF)
    knr[...] = kr
    knrt[...] = kr.T
    nkr = kr.shape[0]
    vt1[pl.ds(0, HD), pl.ds(0, nkr)] = kvr[1].T
    vt1[pl.ds(HD, 16), pl.ds(0, nkr)] = jnp.ones((16, nkr), BF)
    for n in range(tiles):
        sl = pl.ds(n * TILE, TILE)
        if n < tiles_r:
            s = dot(knr[...], qnt[:, sl])
            at = lax.broadcasted_iota(jnp.int32, s.shape, 0)
            lane = lax.broadcasted_iota(jnp.int32, s.shape, 1) + n * TILE
            e = jnp.where(at * 8 <= lane, jnp.exp2(s * exp_scale), 0.0).astype(BF)
            er_ref[:, sl] = e
            ol[:, sl] = dot(vt1[:, pl.ds(0, nkr)], e)
        else:
            ol[:, sl] = jnp.zeros((HD + 16, TILE), F32)

    def pass1(step, carry):
        chunk = lax.rem(yh + order(step), NY)

        @pl.when(step < NY - 1)
        def _():
            wait_block(lax.rem(yh + order(step + 1), NY) * NX + x)
            for dx in (1, 3, 2):
                x_copy(step + 1, dx).start()

        for dx in (1, 3, 2):
            wait_block(chunk * NX + lax.rem(x + dx, NX))

        n_keys = NX * kall.shape[2]
        at = lax.broadcasted_iota(jnp.int32, (n_keys, HD), 0) + chunk * n_keys
        k_raw = kall[pl.ds(chunk * NX, NX), 0].reshape(n_keys, HD).astype(F32)
        inv = lax.rsqrt(jnp.mean(k_raw * k_raw, axis=-1, keepdims=True) + EPSILON)
        unit = k_raw * inv
        uk_ref[step] = unit
        kf = unit * kg_ref[...]
        kn = kf.astype(BF)
        kn_ref[step] = kn
        knt_ref[step] = jnp.where(at < plen, kf, 0.0).astype(BF).T
        v = kall[pl.ds(chunk * NX, NX), 1].reshape(n_keys, HD).astype(F32)
        vt1[pl.ds(0, HD), :] = jnp.where(at < plen, v, 0.0).astype(BF).T
        lane = lax.broadcasted_iota(jnp.int32, (16, n_keys), 1) + chunk * n_keys
        vt1[pl.ds(HD, 16), :] = jnp.where(lane < plen, 1.0, 0.0).astype(BF)
        ahead_s = dot(kn, qnt[:, pl.ds(0, TILE)])
        for n in range(tiles):
            sl = pl.ds(n * TILE, TILE)
            s = ahead_s
            if n + 1 < tiles:
                ahead_s = dot(kn, qnt[:, pl.ds((n + 1) * TILE, TILE)])
            e = jnp.exp2(s * exp_scale)
            if n >= tiles_r:
                key = lax.broadcasted_iota(jnp.int32, s.shape, 0)
                lane = lax.broadcasted_iota(jnp.int32, s.shape, 1) + (n * TILE - rows_r)
                ahead = resp * (rows_p // 8) - chunk * n_keys
                e = jnp.where((key - ahead) * 8 <= lane, e, 0.0)
            e = e.astype(BF)
            e_ref[step, :, sl] = e
            ol[:, sl] += dot(vt1[...], e)
        return carry

    lax.fori_loop(0, NY, pass1, 0)

    for n in range(tiles):
        sl = pl.ds(n * TILE, TILE)
        rl = 1.0 / ol[pl.ds(HD, 1), sl]
        ds = (dt[:, sl] * rl).astype(BF)
        dst[:, sl] = ds
        delta = rl * jnp.sum(ds.astype(F32) * ol[pl.ds(0, HD), sl], axis=0, keepdims=True)
        delta_ref[:, sl] = jnp.broadcast_to(delta, (8, TILE))
        gqt[:, sl] = jnp.zeros((HD, TILE), F32)
    kterm[...] = jnp.zeros((8, HD), F32)

    def x_sum(step, dx):
        return pltpu.make_async_remote_copy(
            src_ref=part.at[step, lax.rem(x + dx, NX)],
            dst_ref=rx.at[step, dx - 1],
            send_sem=rx_send.at[step, dx - 1],
            recv_sem=rx_recv.at[step, dx - 1],
            device_id={"resp": yh * NX + lax.rem(x + dx, NX)},
            device_id_type=MESH,
        )

    def y_sum(step):
        dy = order(step)
        return pltpu.make_async_remote_copy(
            src_ref=ys.at[step],
            dst_ref=ry.at[dy - 1],
            send_sem=ry_send.at[step],
            recv_sem=ry_recv.at[dy - 1],
            device_id={"resp": lax.rem(yh + dy, NY) * NX + x},
            device_id_type=MESH,
        )

    def summed(step, which):
        total = own[step, which]
        for k in range(NX - 1):
            total = total + rx[step, k, which].astype(F32)
        return total

    span = kall.shape[2]

    def pass2(back, carry):
        step = NY - 1 - back
        chunk = lax.rem(yh + order(step), NY)
        n_keys = NX * span
        v = kall[pl.ds(chunk * NX, NX), 1].reshape(n_keys, HD)
        gk = jnp.zeros((n_keys, HD), F32)
        gv = jnp.zeros((n_keys, HD), F32)
        ahead_dp = dot(v, dst[:, pl.ds(0, TILE)])
        for n in range(tiles):
            sl = pl.ds(n * TILE, TILE)
            e = e_ref[step, :, sl]
            dp = ahead_dp
            if n + 1 < tiles:
                ahead_dp = dot(v, dst[:, pl.ds((n + 1) * TILE, TILE)])
            gv += dot(e, dst[:, sl], NT)
            gs = (e.astype(F32) * (dp - delta_ref[pl.ds(0, 1), sl])).astype(BF)
            gk += dot(gs, qn[sl, :])
            gqt[:, sl] += dot(knt_ref[step], gs)
        at = lax.broadcasted_iota(jnp.int32, (n_keys, HD), 0) + chunk * n_keys
        gk = jnp.where(at < plen, gk * scale, 0.0)
        gv = jnp.where(at < plen, gv, 0.0)
        kterm[...] += jnp.sum((gk * uk_ref[step]).reshape(n_keys // 8, 8, HD), axis=0)
        sums[0] = gk
        sums[1] = gv
        for which in range(2):
            for k in range(NX):
                part[step, k, which] = sums[which, pl.ds(k * span, span)].astype(BF)
            own[step, which] = sums[which, pl.ds(x * span, span)]
        for dx in (2, 1, 3):
            x_sum(step, dx).start()

        @pl.when(back == 0)
        def _():
            gkr = jnp.zeros((nkr, HD), F32)
            gvr = jnp.zeros((nkr, HD), F32)
            for n in range(tiles_r):
                sl = pl.ds(n * TILE, TILE)
                e = er_ref[:, sl]
                dp = dot(kvr[1], dst[:, sl])
                gs = (e.astype(F32) * (dp - delta_ref[pl.ds(0, 1), sl])).astype(BF)
                gkr += dot(gs, qn[sl, :])
                gvr += dot(e, dst[:, sl], NT)
                gqt[:, sl] += dot(knrt[...], gs)
            gkr = gkr * scale
            ur = ukr[...]
            kterm[...] += jnp.sum((gkr * ur).reshape(nkr // 8, 8, HD), axis=0)
            kf = kvr[0].astype(F32)
            inv = lax.rsqrt(jnp.mean(kf * kf, axis=-1, keepdims=True) + EPSILON)
            gu = gkr * kg_ref[...]
            dk = inv * (gu - ur * jnp.mean(gu * ur, axis=-1, keepdims=True))
            dkvr_v[0] = dk.astype(BF)
            dkvr_v[1] = gvr.astype(BF)

        @pl.when(back > 0)
        def _():
            before = step + 1
            for dx in (2, 1, 3):
                x_sum(before, dx).wait_recv()
            for which in range(2):
                ys[before, which] = summed(before, which).astype(BF)
            y_sum(before).start()

        return carry

    lax.fori_loop(0, NY, pass2, 0)

    stores = [
        pltpu.make_async_copy(dkvr_v, dkvr_out, out_sem.at[0]),
        pltpu.make_async_copy(dq_v.at[pl.ds(0, rows_r)], dqr_out, out_sem.at[1]),
        pltpu.make_async_copy(dq_v.at[pl.ds(rows_r, rows_p)], dqp_out, out_sem.at[2]),
        pltpu.make_async_copy(dkvp_v, dkvp_out, out_sem.at[3]),
        pltpu.make_async_copy(gsend.at[3, pl.ds(0, 2)], gains_out, out_sem.at[4]),
    ]
    stores[0].start()

    prod = jnp.zeros((HD, HD), F32)
    for n in range(rows // HD):
        sl = pl.ds(n * HD, HD)
        prod += gqt[:, sl] * unit_qt[:, sl]
    qterm = jnp.sum(prod.T, axis=0, keepdims=True) * scale
    key_sum = jnp.sum(kterm[...], axis=0, keepdims=True)
    which_row = lax.broadcasted_iota(jnp.int32, (8, HD), 0)
    gsend[0] = jnp.where(
        which_row == 0,
        jnp.broadcast_to(qterm, (8, HD)),
        jnp.where(which_row == 1, jnp.broadcast_to(key_sum, (8, HD)), 0.0),
    )

    def g_copy(stage, k):
        return pltpu.make_async_remote_copy(
            src_ref=gsend.at[stage],
            dst_ref=grecv.at[stage, stage_at[stage]],
            send_sem=g_send.at[stage, k - 1],
            recv_sem=g_recv.at[stage, k - 1],
            device_id=partner(stage, k),
            device_id_type=MESH,
        )

    def g_start(stage):
        for k in range(1, 8):
            g_copy(stage, k).start()
        grecv[stage, stage_at[stage]] = gsend[stage]

    def g_finish(stage):
        for k in range(1, 8):
            g_copy(stage, k).wait_recv()
        total = grecv[stage, 0]
        for k in range(1, 8):
            total = total + grecv[stage, k]
        gsend[stage + 1] = total

    g_start(0)

    for n in range(tiles):
        sl = pl.ds(n * TILE, TILE)
        ut = unit_qt[:, sl]
        gu = gqt[:, sl] * scale * gcol[...]
        back = inv_q[pl.ds(0, 1), sl] * (gu - ut * jnp.mean(gu * ut, axis=0, keepdims=True))
        dq_v[sl, :] = back.astype(BF).T
    stores[1].start()
    stores[2].start()
    for dy in (1, 3, 2):
        y_copy(dy).wait_send()
    for step in range(NY):
        for dx in (1, 3, 2):
            x_copy(step, dx).wait_send()

    g_finish(0)
    g_start(1)

    for dx in (2, 1, 3):
        x_sum(0, dx).wait_recv()

    g_finish(1)
    g_start(2)

    for step in range(NY):
        for dx in (1, 3, 2):
            x_sum(step, dx).wait_send()
    for step in range(1, NY):
        y_sum(step).wait_send()
        y_sum(step).wait_recv()
    totals = []
    for which in range(2):
        total = summed(0, which)
        for k in range(NY - 1):
            total = total + ry[k, which].astype(F32)
        totals.append(total)
    unit = uk_ref[0, pl.ds(x * span, span), :]
    kf = kall[resp, 0].astype(F32)
    inv = lax.rsqrt(jnp.mean(kf * kf, axis=-1, keepdims=True) + EPSILON)
    gu = totals[0] * kg_ref[...]
    dk = inv * (gu - unit * jnp.mean(gu * unit, axis=-1, keepdims=True))
    dkvp_v[0] = dk.astype(BF)
    dkvp_v[1] = totals[1].astype(BF)
    stores[3].start()

    g_finish(2)
    stores[4].start()

    for stage in range(3):
        for k in range(1, 8):
            g_copy(stage, k).wait_send()
    for store in stores:
        store.wait()


def hand_out(*refs):
    count = len(refs) // 2
    sem = refs[-1]
    copies = [
        pltpu.make_async_copy(refs[n], refs[count + n], sem.at[n]) for n in range(count)
    ]
    for copy in copies:
        copy.start()
    for copy in copies:
        copy.wait()


def shards(
    q_prompt,
    q_resp,
    kv_prompt,
    kv_resp,
    dout_prompt,
    dout_resp,
    q_gain,
    k_gain,
    resp_len,
    prompt_len,
):
    span = q_prompt.shape[1]
    length = q_resp.shape[2]
    rows_r = length * 8
    rows_p = span * 8
    rows = rows_r + rows_p
    n_keys = NX * span
    any_spec = pl.BlockSpec(memory_space=pl.ANY)
    hbm = pl.BlockSpec(memory_space=pltpu.HBM)
    dma = pltpu.SemaphoreType.DMA
    out = pl.pallas_call(
        kernel,
        out_shape=(
            jax.ShapeDtypeStruct((rows_r, HD), BF),
            jax.ShapeDtypeStruct((rows_p, HD), BF),
            jax.ShapeDtypeStruct((2, span, HD), BF),
            jax.ShapeDtypeStruct((2, length, HD), BF),
            jax.ShapeDtypeStruct((2, HD), F32),
        ),
        in_specs=[hbm] * 10,
        out_specs=[any_spec] * 5,
        scratch_shapes=[
            pltpu.VMEM((1, HD), F32),
            pltpu.VMEM((1, HD), F32),
            pltpu.SMEM((1, 1), jnp.int32),
            pltpu.SMEM((1,), jnp.int32),
            pltpu.VMEM((rows, HD), BF),
            pltpu.VMEM((rows, HD), BF),
            pltpu.VMEM((2, length, HD), BF),
            pltpu.VMEM((NX * NY, 2, span, HD), BF),
            pltpu.VMEM((HD, rows), F32),
            pltpu.VMEM((8, rows), F32),
            pltpu.VMEM((HD, rows), BF),
            pltpu.VMEM((rows, HD), BF),
            pltpu.VMEM((HD, rows), F32),
            pltpu.VMEM((HD, rows), BF),
            pltpu.VMEM((8, rows), F32),
            pltpu.VMEM((HD, TILE), F32),
            pltpu.VMEM((NY, n_keys, HD), BF),
            pltpu.VMEM((NY, HD, n_keys), BF),
            pltpu.VMEM((NY, n_keys, HD), F32),
            pltpu.VMEM((HD + 16, n_keys), BF),
            pltpu.VMEM((length, HD), BF),
            pltpu.VMEM((HD, length), BF),
            pltpu.VMEM((length, HD), F32),
            pltpu.VMEM((NY, n_keys, rows), BF),
            pltpu.VMEM((length, rows_r), BF),
            pltpu.VMEM((HD + 16, rows), F32),
            pltpu.VMEM((HD, rows), F32),
            pltpu.VMEM((2, n_keys, HD), F32),
            pltpu.VMEM((NY, NX, 2, span, HD), BF),
            pltpu.VMEM((NY, NX - 1, 2, span, HD), BF),
            pltpu.VMEM((NY, 2, span, HD), F32),
            pltpu.VMEM((NY, 2, span, HD), BF),
            pltpu.VMEM((NY - 1, 2, span, HD), BF),
            pltpu.VMEM((8, HD), F32),
            pltpu.VMEM((4, 8, HD), F32),
            pltpu.VMEM((3, 8, 8, HD), F32),
            pltpu.VMEM((rows, HD), BF),
            pltpu.VMEM((2, span, HD), BF),
            pltpu.VMEM((2, length, HD), BF),
            dma((10,)),
            dma((5,)),
            dma((NX * NY,)),
            dma((NY - 1,)),
            dma((NY, NX - 1)),
            dma((NY, NX - 1)),
            dma((NY, NX - 1)),
            dma((NY - 1,)),
            dma((NY,)),
            dma((3, 7)),
            dma((3, 7)),
        ],
        compiler_params=pltpu.CompilerParams(
            collective_id=0, has_side_effects=True
        ),
        name="attention_grads",
    )(
        q_resp.reshape(rows_r, HD),
        q_prompt.reshape(rows_p, HD),
        kv_prompt.reshape(2, span, HD),
        kv_resp.reshape(2, length, HD),
        dout_resp.reshape(rows_r, HD),
        dout_prompt.reshape(rows_p, HD),
        q_gain.reshape(1, HD),
        k_gain.reshape(1, HD),
        resp_len,
        prompt_len,
    )
    out = pl.pallas_call(
        hand_out,
        out_shape=tuple(jax.ShapeDtypeStruct(a.shape, a.dtype) for a in out),
        in_specs=[any_spec] * 5,
        out_specs=[any_spec] * 5,
        scratch_shapes=[dma((5,))],
        name="hand_out",
    )(*out)
    return (
        out[1].reshape(q_prompt.shape),
        out[0].reshape(q_resp.shape),
        out[2].reshape(kv_prompt.shape),
        out[3].reshape(kv_resp.shape),
        out[4],
    )


def solution(mesh):
    return jax.shard_map(
        shards,
        mesh=mesh,
        in_specs=(
            P("grp", "resp", "head", None),
            P("grp", "resp", None, "head", None),
            P("grp", None, "resp", "head", None),
            P("grp", "resp", None, None, "head", None),
            P("grp", "resp", "head", None),
            P("grp", "resp", None, "head", None),
            P(),
            P(),
            P("grp", "resp"),
            P("grp"),
        ),
        out_specs=(
            P("grp", "resp", "head", None),
            P("grp", "resp", None, "head", None),
            P("grp", None, "resp", "head", None),
            P("grp", "resp", None, None, "head", None),
            P(),
        ),
        check_vma=False,
    )
```

```python
import functools
import math

import jax
import jax.numpy as jnp
from jax import lax
from jax.experimental import pallas as pl
from jax.experimental.pallas import tpu as pltpu
from jax.sharding import PartitionSpec as P

EPSILON = 1e-06
MESH = pl.DeviceIdType.MESH
HD = 128
BF = jnp.bfloat16
F32 = jnp.float32
NX = 4
NY = 4
TILE = 512
NT = (((1,), (1,)), ((), ()))
NN = (((1,), (0,)), ((), ()))


def dot(lhs, rhs, dims=NN):
    return lax.dot_general(lhs, rhs, dims, preferred_element_type=F32)


def barrier_with(partners):
    barrier = pltpu.get_barrier_semaphore()
    for to in partners:
        pl.semaphore_signal(barrier, inc=1, device_id=to, device_id_type=MESH)
    pl.semaphore_wait(barrier, len(partners))


def gather_kernel(kvp_in, kall, in_sem, kv_recv, kvy_send, kvx_send):
    resp = lax.axis_index("resp")
    yh = resp // NX
    x = lax.rem(resp, NX)
    load = pltpu.make_async_copy(kvp_in, kall.at[resp], in_sem)
    load.start()

    def x_peer(dx):
        return {"resp": yh * NX + lax.rem(x + dx, NX)}

    def y_peer(dy):
        return {"resp": lax.rem(yh + dy, NY) * NX + x}

    barrier_with([x_peer(d) for d in (1, 2, 3)] + [y_peer(d) for d in (1, 2, 3)])
    load.wait()

    def y_copy(dy):
        return pltpu.make_async_remote_copy(
            src_ref=kall.at[resp],
            dst_ref=kall.at[resp],
            send_sem=kvy_send.at[dy - 1],
            recv_sem=kv_recv.at[resp],
            device_id=y_peer(dy),
            device_id_type=MESH,
        )

    def x_copy(step, dx):
        block = lax.rem(yh + step, NY) * NX + x
        return pltpu.make_async_remote_copy(
            src_ref=kall.at[block],
            dst_ref=kall.at[block],
            send_sem=kvx_send.at[step, dx - 1],
            recv_sem=kv_recv.at[block],
            device_id=x_peer(dx),
            device_id_type=MESH,
        )

    def wait_block(block):
        pltpu.make_async_remote_copy(
            src_ref=kall.at[block],
            dst_ref=kall.at[block],
            send_sem=kvy_send.at[0],
            recv_sem=kv_recv.at[block],
            device_id=x_peer(1),
            device_id_type=MESH,
        ).wait_recv()

    for dy in (1, 3, 2):
        y_copy(dy).start()
    for dx in (1, 3, 2):
        x_copy(0, dx).start()
    for step in (1, 3, 2):
        wait_block(lax.rem(yh + step, NY) * NX + x)
        for dx in (1, 3, 2):
            x_copy(step, dx).start()
    for step in (0, 1, 3, 2):
        for dx in (1, 3, 2):
            wait_block(lax.rem(yh + step, NY) * NX + lax.rem(x + dx, NX))
    for dy in (1, 3, 2):
        y_copy(dy).wait_send()
    for step in range(NY):
        for dx in (1, 3, 2):
            x_copy(step, dx).wait_send()


def attention_kernel(
    qr_in,
    qp_in,
    kall,
    kvr,
    dr_in,
    dp_in,
    qg_ref,
    kg_ref,
    rlen_ref,
    plen_ref,
    dqr_out,
    dqp_out,
    dkvr_v,
    part,
    own,
    gains_out,
    unit_qt,
    inv_q,
    qnt,
    qn,
    dt,
    dst,
    delta_ref,
    gcol,
    kn_ref,
    knt_ref,
    uk_ref,
    vt1,
    knr,
    knrt,
    ukr,
    e_ref,
    er_ref,
    ol,
    gqt,
    sums,
    kterm,
):
    resp = lax.axis_index("resp")
    x = lax.rem(resp, NX)
    rows_r = qr_in.shape[0]
    rows_p = qp_in.shape[0]
    rows = rows_r + rows_p
    tiles = rows // TILE
    tiles_r = rows_r // TILE
    scale = HD**-0.5
    exp_scale = scale * math.log2(math.e)

    plen = plen_ref[0]
    rlen = rlen_ref[0, 0]

    gcol[...] = jnp.broadcast_to(qg_ref[...], (TILE, HD)).T
    for n in range(tiles):
        sl = pl.ds(n * TILE, TILE)
        xt = (qr_in[sl, :] if n < tiles_r else qp_in[pl.ds(n * TILE - rows_r, TILE), :]).T.astype(F32)
        inv = lax.rsqrt(jnp.mean(xt * xt, axis=0, keepdims=True) + EPSILON)
        ut = xt * inv
        unit_qt[:, sl] = ut
        inv_q[:, sl] = jnp.broadcast_to(inv, (8, TILE))
        qt = (ut * gcol[...]).astype(BF)
        qnt[:, sl] = qt
        qn[sl, :] = qt.T

    for n in range(tiles):
        sl = pl.ds(n * TILE, TILE)
        lane = lax.broadcasted_iota(jnp.int32, (HD, TILE), 1) + n * TILE
        if n < tiles_r:
            keep = lane < rlen * 8
        else:
            keep = lane - rows_r < (plen - rows_p // 8 * resp) * 8
        dt[:, sl] = jnp.where(keep, (dr_in[sl, :] if n < tiles_r else dp_in[pl.ds(n * TILE - rows_r, TILE), :]).T.astype(F32), 0.0)

    kf = kvr[0].astype(F32)
    inv_kr = lax.rsqrt(jnp.mean(kf * kf, axis=-1, keepdims=True) + EPSILON)
    ur = kf * inv_kr
    ukr[...] = ur
    kr = (ur * kg_ref[...]).astype(BF)
    knr[...] = kr
    knrt[...] = kr.T
    nkr = kr.shape[0]
    vt1[pl.ds(0, HD), pl.ds(0, nkr)] = kvr[1].T
    vt1[pl.ds(HD, 16), pl.ds(0, nkr)] = jnp.ones((16, nkr), BF)
    for n in range(tiles):
        sl = pl.ds(n * TILE, TILE)
        if n < tiles_r:
            s = dot(knr[...], qnt[:, sl])
            at = lax.broadcasted_iota(jnp.int32, s.shape, 0)
            lane = lax.broadcasted_iota(jnp.int32, s.shape, 1) + n * TILE
            e = jnp.where(at * 8 <= lane, jnp.exp2(s * exp_scale), 0.0).astype(BF)
            er_ref[:, sl] = e
            ol[:, sl] = dot(vt1[:, pl.ds(0, nkr)], e)
        else:
            ol[:, sl] = jnp.zeros((HD + 16, TILE), F32)

    def pass1(step, carry):
        chunk = step

        n_keys = NX * kall.shape[2]
        at = lax.broadcasted_iota(jnp.int32, (n_keys, HD), 0) + chunk * n_keys
        k_raw = kall[pl.ds(chunk * NX, NX), 0].reshape(n_keys, HD).astype(F32)
        inv = lax.rsqrt(jnp.mean(k_raw * k_raw, axis=-1, keepdims=True) + EPSILON)
        unit = k_raw * inv
        uk_ref[step] = unit
        kf = unit * kg_ref[...]
        kn = kf.astype(BF)
        kn_ref[step] = kn
        knt_ref[step] = jnp.where(at < plen, kf, 0.0).astype(BF).T
        v = kall[pl.ds(chunk * NX, NX), 1].reshape(n_keys, HD).astype(F32)
        vt1[pl.ds(0, HD), :] = jnp.where(at < plen, v, 0.0).astype(BF).T
        lane = lax.broadcasted_iota(jnp.int32, (16, n_keys), 1) + chunk * n_keys
        vt1[pl.ds(HD, 16), :] = jnp.where(lane < plen, 1.0, 0.0).astype(BF)
        ahead_s = dot(kn, qnt[:, pl.ds(0, TILE)])
        for n in range(tiles):
            sl = pl.ds(n * TILE, TILE)
            s = ahead_s
            if n + 1 < tiles:
                ahead_s = dot(kn, qnt[:, pl.ds((n + 1) * TILE, TILE)])
            e = jnp.exp2(s * exp_scale)
            if n >= tiles_r:
                key = lax.broadcasted_iota(jnp.int32, s.shape, 0)
                lane = lax.broadcasted_iota(jnp.int32, s.shape, 1) + (n * TILE - rows_r)
                ahead = resp * (rows_p // 8) - chunk * n_keys
                e = jnp.where((key - ahead) * 8 <= lane, e, 0.0)
            e = e.astype(BF)
            e_ref[step, :, sl] = e
            ol[:, sl] += dot(vt1[...], e)
        return carry

    lax.fori_loop(0, NY, pass1, 0)

    for n in range(tiles):
        sl = pl.ds(n * TILE, TILE)
        rl = 1.0 / ol[pl.ds(HD, 1), sl]
        ds = (dt[:, sl] * rl).astype(BF)
        dst[:, sl] = ds
        delta = rl * jnp.sum(ds.astype(F32) * ol[pl.ds(0, HD), sl], axis=0, keepdims=True)
        delta_ref[:, sl] = jnp.broadcast_to(delta, (8, TILE))
        gqt[:, sl] = jnp.zeros((HD, TILE), F32)
    kterm[...] = jnp.zeros((8, HD), F32)

    span = kall.shape[2]

    def pass2(back, carry):
        step = NY - 1 - back
        chunk = step
        n_keys = NX * span
        v = kall[pl.ds(chunk * NX, NX), 1].reshape(n_keys, HD)
        gk = jnp.zeros((n_keys, HD), F32)
        gv = jnp.zeros((n_keys, HD), F32)
        ahead_dp = dot(v, dst[:, pl.ds(0, TILE)])
        for n in range(tiles):
            sl = pl.ds(n * TILE, TILE)
            e = e_ref[step, :, sl]
            dp = ahead_dp
            if n + 1 < tiles:
                ahead_dp = dot(v, dst[:, pl.ds((n + 1) * TILE, TILE)])
            gv += dot(e, dst[:, sl], NT)
            gs = (e.astype(F32) * (dp - delta_ref[pl.ds(0, 1), sl])).astype(BF)
            gk += dot(gs, qn[sl, :])
            gqt[:, sl] += dot(knt_ref[step], gs)
        at = lax.broadcasted_iota(jnp.int32, (n_keys, HD), 0) + chunk * n_keys
        gk = jnp.where(at < plen, gk * scale, 0.0)
        gv = jnp.where(at < plen, gv, 0.0)
        kterm[...] += jnp.sum((gk * uk_ref[step]).reshape(n_keys // 8, 8, HD), axis=0)
        sums[0] = gk
        sums[1] = gv
        for which in range(2):
            for k in range(NX):
                part[step, k, which] = sums[which, pl.ds(k * span, span)].astype(BF)
            own[step, which] = sums[which, pl.ds(x * span, span)]
        @pl.when(back == 0)
        def _():
            gkr = jnp.zeros((nkr, HD), F32)
            gvr = jnp.zeros((nkr, HD), F32)
            for n in range(tiles_r):
                sl = pl.ds(n * TILE, TILE)
                e = er_ref[:, sl]
                dp = dot(kvr[1], dst[:, sl])
                gs = (e.astype(F32) * (dp - delta_ref[pl.ds(0, 1), sl])).astype(BF)
                gkr += dot(gs, qn[sl, :])
                gvr += dot(e, dst[:, sl], NT)
                gqt[:, sl] += dot(knrt[...], gs)
            gkr = gkr * scale
            ur = ukr[...]
            kterm[...] += jnp.sum((gkr * ur).reshape(nkr // 8, 8, HD), axis=0)
            kf = kvr[0].astype(F32)
            inv = lax.rsqrt(jnp.mean(kf * kf, axis=-1, keepdims=True) + EPSILON)
            gu = gkr * kg_ref[...]
            dk = inv * (gu - ur * jnp.mean(gu * ur, axis=-1, keepdims=True))
            dkvr_v[0] = dk.astype(BF)
            dkvr_v[1] = gvr.astype(BF)

        return carry

    lax.fori_loop(0, NY, pass2, 0)

    prod = jnp.zeros((HD, HD), F32)
    for n in range(rows // HD):
        sl = pl.ds(n * HD, HD)
        prod += gqt[:, sl] * unit_qt[:, sl]
    qterm = jnp.sum(prod.T, axis=0, keepdims=True) * scale
    key_sum = jnp.sum(kterm[...], axis=0, keepdims=True)
    which_row = lax.broadcasted_iota(jnp.int32, (8, HD), 0)
    gains_out[...] = jnp.where(
        which_row == 0,
        jnp.broadcast_to(qterm, (8, HD)),
        jnp.where(which_row == 1, jnp.broadcast_to(key_sum, (8, HD)), 0.0),
    )

    for n in range(tiles):
        sl = pl.ds(n * TILE, TILE)
        ut = unit_qt[:, sl]
        gu = gqt[:, sl] * scale * gcol[...]
        back = inv_q[pl.ds(0, 1), sl] * (gu - ut * jnp.mean(gu * ut, axis=0, keepdims=True))
        if n < tiles_r:
            dqr_out[sl, :] = back.astype(BF).T
        else:
            dqp_out[pl.ds(n * TILE - rows_r, TILE), :] = back.astype(BF).T

def sums_kernel(
    part,
    own,
    gains_in,
    kv_in,
    kg_ref,
    dkvp_out,
    gains_out,
    rx,
    ys,
    ry,
    gsend,
    grecv,
    rx_recv,
    rx_send,
    ry_recv,
    ry_send,
    g_recv,
    g_send,
):
    resp = lax.axis_index("resp")
    head = lax.axis_index("head")
    grp = lax.axis_index("grp")
    yh = resp // NX
    x = lax.rem(resp, NX)
    yl = head // 2
    core = lax.rem(head, 2)
    ngrp = 8
    y8 = 2 * yh + yl

    def partner(stage, k):
        if stage == 0:
            return {"grp": lax.rem(grp + k, ngrp)}
        if stage == 1:
            to = lax.rem(y8 + k, 8)
            return {"resp": (to // 2) * NX + x, "head": lax.rem(to, 2) * 2 + core}
        to = lax.rem(2 * x + core + k, 8)
        return {"resp": yh * NX + to // 2, "head": yl * 2 + lax.rem(to, 2)}

    stage_at = (grp, y8, 2 * x + core)
    barrier_with([partner(stage, k) for stage in range(3) for k in range(1, 8)])

    def chunk_at(step):
        return lax.rem(yh + step, NY)

    def x_sum(step, dx):
        return pltpu.make_async_remote_copy(
            src_ref=part.at[chunk_at(step), lax.rem(x + dx, NX)],
            dst_ref=rx.at[step, dx - 1],
            send_sem=rx_send.at[step, dx - 1],
            recv_sem=rx_recv.at[step, dx - 1],
            device_id={"resp": yh * NX + lax.rem(x + dx, NX)},
            device_id_type=MESH,
        )

    def y_sum(step):
        return pltpu.make_async_remote_copy(
            src_ref=ys.at[step],
            dst_ref=ry.at[step - 1],
            send_sem=ry_send.at[step],
            recv_sem=ry_recv.at[step - 1],
            device_id={"resp": chunk_at(step) * NX + x},
            device_id_type=MESH,
        )

    def summed(step, which):
        total = own[chunk_at(step), which]
        for k in range(NX - 1):
            total = total + rx[step, k, which].astype(F32)
        return total

    def g_copy(stage, k):
        return pltpu.make_async_remote_copy(
            src_ref=gsend.at[stage],
            dst_ref=grecv.at[stage, stage_at[stage]],
            send_sem=g_send.at[stage, k - 1],
            recv_sem=g_recv.at[stage, k - 1],
            device_id=partner(stage, k),
            device_id_type=MESH,
        )

    def g_start(stage):
        for k in range(1, 8):
            g_copy(stage, k).start()
        grecv[stage, stage_at[stage]] = gsend[stage]

    def g_finish(stage):
        for k in range(1, 8):
            g_copy(stage, k).wait_recv()
        total = grecv[stage, 0]
        for k in range(1, 8):
            total = total + grecv[stage, k]
        gsend[stage + 1] = total

    gsend[0] = gains_in[...]
    g_start(0)
    for step in (2, 3, 1, 0):
        for dx in (2, 1, 3):
            x_sum(step, dx).start()
    g_finish(0)
    g_start(1)
    for step in (2, 3, 1):
        for dx in (2, 1, 3):
            x_sum(step, dx).wait_recv()
        for which in range(2):
            ys[step, which] = summed(step, which).astype(BF)
        y_sum(step).start()
    g_finish(1)
    g_start(2)
    for dx in (2, 1, 3):
        x_sum(0, dx).wait_recv()
    for step in (2, 3, 1):
        y_sum(step).wait_recv()
    totals = []
    for which in range(2):
        total = summed(0, which)
        for k in range(NY - 1):
            total = total + ry[k, which].astype(F32)
        totals.append(total)
    kf = kv_in[0].astype(F32)
    inv = lax.rsqrt(jnp.mean(kf * kf, axis=-1, keepdims=True) + EPSILON)
    unit = kf * inv
    gu = totals[0] * kg_ref[...]
    dk = inv * (gu - unit * jnp.mean(gu * unit, axis=-1, keepdims=True))
    dkvp_out[0] = dk.astype(BF)
    dkvp_out[1] = totals[1].astype(BF)
    for step in range(NY):
        for dx in (1, 3, 2):
            x_sum(step, dx).wait_send()
    for step in range(1, NY):
        y_sum(step).wait_send()
    g_finish(2)
    gains_out[...] = gsend[3, pl.ds(0, 2), :]
    for stage in range(3):
        for k in range(1, 8):
            g_copy(stage, k).wait_send()


def shards(
    q_prompt,
    q_resp,
    kv_prompt,
    kv_resp,
    dout_prompt,
    dout_resp,
    q_gain,
    k_gain,
    resp_len,
    prompt_len,
):
    span = q_prompt.shape[1]
    length = q_resp.shape[2]
    rows_r = length * 8
    rows_p = span * 8
    rows = rows_r + rows_p
    n_keys = NX * span
    any_spec = pl.BlockSpec(memory_space=pl.ANY)
    vmem = pl.BlockSpec(memory_space=pltpu.VMEM)
    smem = pl.BlockSpec(memory_space=pltpu.SMEM)
    dma = pltpu.SemaphoreType.DMA
    limit = 32 * 2**20
    own_kv = kv_prompt.reshape(2, span, HD)
    gathered = pl.pallas_call(
        gather_kernel,
        out_shape=jax.ShapeDtypeStruct((NX * NY, 2, span, HD), BF),
        in_specs=[any_spec],
        out_specs=any_spec,
        scratch_shapes=[
            dma,
            dma((NX * NY,)),
            dma((NY - 1,)),
            dma((NY, NX - 1)),
        ],
        compiler_params=pltpu.CompilerParams(
            collective_id=0, has_side_effects=True, vmem_limit_bytes=limit
        ),
        name="gather_keys",
    )(own_kv)
    dq_r, dq_p, dkv_r, part, own, gains = pl.pallas_call(
        attention_kernel,
        out_shape=(
            jax.ShapeDtypeStruct((rows_r, HD), BF),
            jax.ShapeDtypeStruct((rows_p, HD), BF),
            jax.ShapeDtypeStruct((2, length, HD), BF),
            jax.ShapeDtypeStruct((NY, NX, 2, span, HD), BF),
            jax.ShapeDtypeStruct((NY, 2, span, HD), F32),
            jax.ShapeDtypeStruct((8, HD), F32),
        ),
        in_specs=[vmem] * 8 + [smem] * 2,
        out_specs=[vmem] * 6,
        scratch_shapes=[
            pltpu.VMEM((HD, rows), F32),
            pltpu.VMEM((8, rows), F32),
            pltpu.VMEM((HD, rows), BF),
            pltpu.VMEM((rows, HD), BF),
            pltpu.VMEM((HD, rows), F32),
            pltpu.VMEM((HD, rows), BF),
            pltpu.VMEM((8, rows), F32),
            pltpu.VMEM((HD, TILE), F32),
            pltpu.VMEM((NY, n_keys, HD), BF),
            pltpu.VMEM((NY, HD, n_keys), BF),
            pltpu.VMEM((NY, n_keys, HD), F32),
            pltpu.VMEM((HD + 16, n_keys), BF),
            pltpu.VMEM((length, HD), BF),
            pltpu.VMEM((HD, length), BF),
            pltpu.VMEM((length, HD), F32),
            pltpu.VMEM((NY, n_keys, rows), BF),
            pltpu.VMEM((length, rows_r), BF),
            pltpu.VMEM((HD + 16, rows), F32),
            pltpu.VMEM((HD, rows), F32),
            pltpu.VMEM((2, n_keys, HD), F32),
            pltpu.VMEM((8, HD), F32),
        ],
        compiler_params=pltpu.CompilerParams(vmem_limit_bytes=limit),
        name="attention_grads",
    )(
        q_resp.reshape(rows_r, HD),
        q_prompt.reshape(rows_p, HD),
        gathered,
        kv_resp.reshape(2, length, HD),
        dout_resp.reshape(rows_r, HD),
        dout_prompt.reshape(rows_p, HD),
        q_gain.reshape(1, HD),
        k_gain.reshape(1, HD),
        resp_len,
        prompt_len,
    )
    dkv_p, gain_grads = pl.pallas_call(
        sums_kernel,
        out_shape=(
            jax.ShapeDtypeStruct((2, span, HD), BF),
            jax.ShapeDtypeStruct((2, HD), F32),
        ),
        in_specs=[vmem] * 5,
        out_specs=[vmem] * 2,
        scratch_shapes=[
            pltpu.VMEM((NY, NX - 1, 2, span, HD), BF),
            pltpu.VMEM((NY, 2, span, HD), BF),
            pltpu.VMEM((NY - 1, 2, span, HD), BF),
            pltpu.VMEM((4, 8, HD), F32),
            pltpu.VMEM((3, 8, 8, HD), F32),
            dma((NY, NX - 1)),
            dma((NY, NX - 1)),
            dma((NY - 1,)),
            dma((NY,)),
            dma((3, 7)),
            dma((3, 7)),
        ],
        compiler_params=pltpu.CompilerParams(
            collective_id=1, has_side_effects=True, vmem_limit_bytes=limit
        ),
        name="sum_gradients",
    )(part, own, gains, own_kv, k_gain.reshape(1, HD))
    return (
        dq_p.reshape(q_prompt.shape),
        dq_r.reshape(q_resp.shape),
        dkv_p.reshape(kv_prompt.shape),
        dkv_r.reshape(kv_resp.shape),
        gain_grads,
    )


def solution(mesh):
    return jax.shard_map(
        shards,
        mesh=mesh,
        in_specs=(
            P("grp", "resp", "head", None),
            P("grp", "resp", None, "head", None),
            P("grp", None, "resp", "head", None),
            P("grp", "resp", None, None, "head", None),
            P("grp", "resp", "head", None),
            P("grp", "resp", None, "head", None),
            P(),
            P(),
            P("grp", "resp"),
            P("grp"),
        ),
        out_specs=(
            P("grp", "resp", "head", None),
            P("grp", "resp", None, "head", None),
            P("grp", None, "resp", "head", None),
            P("grp", "resp", None, None, "head", None),
            P(),
        ),
        check_vma=False,
    )
```

```python
import functools
import math

import jax
import jax.numpy as jnp
from jax import lax
from jax.experimental import pallas as pl
from jax.experimental.pallas import tpu as pltpu
from jax.sharding import PartitionSpec as P

EPSILON = 1e-06
MESH = pl.DeviceIdType.MESH
HD = 128
BF = jnp.bfloat16
F32 = jnp.float32
NX = 4
NY = 4
TILE = 512
NT = (((1,), (1,)), ((), ()))
NN = (((1,), (0,)), ((), ()))


def dot(lhs, rhs, dims=NN):
    return lax.dot_general(lhs, rhs, dims, preferred_element_type=F32)


def order(step):
    return step + step // 2 - 2 * (step // 3)


def kernel(
    qr_in,
    qp_in,
    kvp_in,
    kvr_in,
    dr_in,
    dp_in,
    qg_in,
    kg_in,
    rlen_in,
    plen_in,
    dqr_out,
    dqp_out,
    dkvp_out,
    dkvr_out,
    gains_out,
    qg_ref,
    kg_ref,
    rlen_ref,
    plen_ref,
    q_nat,
    d_nat,
    kvr,
    kall,
    unit_qt,
    inv_q,
    qnt,
    qn,
    dt,
    dst,
    delta_ref,
    gcol,
    knt_ref,
    uk_ref,
    vt1,
    knr,
    knrt,
    ukr,
    e_ref,
    er_ref,
    ol,
    gqt,
    sums,
    x1_send,
    x1_recv,
    x2_send,
    x2_recv,
    y1_send,
    y1_recv,
    y2_send,
    y2_recv,
    kterm,
    gsend,
    grecv,
    dq_v,
    dkvp_v,
    dkvr_v,
    in_sem,
    out_sem,
    kv_got,
    half_got,
    kv_sent,
    half_sent,
    x_got,
    x_sent,
    y_got,
    y_sent,
    g_recv,
    g_send,
):
    resp = lax.axis_index("resp")
    head = lax.axis_index("head")
    grp = lax.axis_index("grp")
    yh = resp // NX
    x = lax.rem(resp, NX)
    yl = head // 2
    core = lax.rem(head, 2)
    ngrp = 8
    y8 = 2 * yh + yl
    rows_r = qr_in.shape[0]
    rows_p = qp_in.shape[0]
    rows = rows_r + rows_p
    tiles = rows // TILE
    tiles_r = rows_r // TILE
    scale = HD**-0.5
    exp_scale = scale * math.log2(math.e)

    def partner(stage, k):
        if stage == 0:
            return {"grp": lax.rem(grp + k, ngrp)}
        if stage == 1:
            to = lax.rem(y8 + k, 8)
            return {"resp": (to // 2) * NX + x, "head": lax.rem(to, 2) * 2 + core}
        to = lax.rem(2 * x + core + k, 8)
        return {"resp": yh * NX + to // 2, "head": yl * 2 + lax.rem(to, 2)}

    stage_at = (grp, y8, 2 * x + core)

    barrier = pltpu.get_barrier_semaphore()
    for stage in range(3):
        for k in range(1, 8):
            pl.semaphore_signal(
                barrier, inc=1, device_id=partner(stage, k), device_id_type=MESH
            )

    loads = [
        pltpu.make_async_copy(kvp_in, kall.at[resp], in_sem.at[0]),
        pltpu.make_async_copy(qr_in, q_nat.at[pl.ds(0, rows_r)], in_sem.at[1]),
        pltpu.make_async_copy(qp_in, q_nat.at[pl.ds(rows_r, rows_p)], in_sem.at[2]),
        pltpu.make_async_copy(kvr_in, kvr, in_sem.at[3]),
        pltpu.make_async_copy(dr_in, d_nat.at[pl.ds(0, rows_r)], in_sem.at[4]),
        pltpu.make_async_copy(dp_in, d_nat.at[pl.ds(rows_r, rows_p)], in_sem.at[5]),
        pltpu.make_async_copy(qg_in, qg_ref, in_sem.at[6]),
        pltpu.make_async_copy(kg_in, kg_ref, in_sem.at[7]),
        pltpu.make_async_copy(rlen_in, rlen_ref, in_sem.at[8]),
        pltpu.make_async_copy(plen_in, plen_ref, in_sem.at[9]),
    ]
    for load in loads:
        load.start()

    loads[0].wait()
    pl.semaphore_wait(barrier, 21)

    def towards(way):
        if way < 2:
            return {"resp": yh * NX + lax.rem(x + 1 + 2 * way, NX)}
        return {"resp": lax.rem(yh + 1 + 2 * (way - 2), NY) * NX + x}

    def send(src, dst, sent, got, way):
        return pltpu.make_async_remote_copy(
            src_ref=src,
            dst_ref=dst,
            send_sem=sent,
            recv_sem=got,
            device_id=towards(way),
            device_id_type=MESH,
        )

    def chunk_at(slot):
        return lax.rem(yh + order(slot), NY)

    def block_at(slot, dx):
        return chunk_at(slot) * NX + lax.rem(x + dx, NX)

    def near(block, slot, way):
        return send(
            kall.at[block],
            kall.at[block],
            kv_sent.at[slot, way],
            kv_got.at[block],
            way,
        )

    def far(block, slot, way):
        half = way % 2
        return send(
            kall.at[block, half],
            kall.at[block, half],
            half_sent.at[slot, way],
            half_got.at[block, half],
            way,
        )

    def x_far(slot, run):
        for way, dx in ((0, 3), (1, 1)):
            block = block_at(slot, dx)
            if run:
                near(block, 0, 0).wait_recv()
                far(block, slot, way).start()
            else:
                far(block, slot, way).wait_send()

    up_block = block_at(1, 0)
    down_block = block_at(2, 0)
    far_block = block_at(3, 0)
    for way in (2, 3, 0, 1):
        near(resp, 0, way).start()

    for load in loads[6:]:
        load.wait()
    plen = plen_ref[0]
    rlen = rlen_ref[0, 0]

    gcol[...] = jnp.broadcast_to(qg_ref[...], (TILE, HD)).T
    loads[1].wait()
    loads[2].wait()
    for n in range(tiles):
        sl = pl.ds(n * TILE, TILE)
        xt = q_nat[sl, :].T.astype(F32)
        inv = lax.rsqrt(jnp.mean(xt * xt, axis=0, keepdims=True) + EPSILON)
        ut = xt * inv
        unit_qt[:, sl] = ut
        inv_q[:, sl] = jnp.broadcast_to(inv, (8, TILE))
        qt = (ut * gcol[...]).astype(BF)
        qnt[:, sl] = qt
        qn[sl, :] = qt.T

    near(down_block, 0, 0).wait_recv()
    far(down_block, 0, 2).start()
    near(up_block, 0, 0).wait_recv()
    far(up_block, 0, 3).start()
    for way in (0, 1):
        near(up_block, 1, way).start()
    for way in (0, 1):
        near(down_block, 2, way).start()
    x_far(0, True)

    loads[4].wait()
    loads[5].wait()
    for n in range(tiles):
        sl = pl.ds(n * TILE, TILE)
        lane = lax.broadcasted_iota(jnp.int32, (HD, TILE), 1) + n * TILE
        if n < tiles_r:
            keep = lane < rlen * 8
        else:
            keep = lane - rows_r < (plen - rows_p // 8 * resp) * 8
        dt[:, sl] = jnp.where(keep, d_nat[sl, :].T.astype(F32), 0.0)

    loads[3].wait()
    kf = kvr[0].astype(F32)
    inv_kr = lax.rsqrt(jnp.mean(kf * kf, axis=-1, keepdims=True) + EPSILON)
    ur = kf * inv_kr
    ukr[...] = ur
    kr = (ur * kg_ref[...]).astype(BF)
    knr[...] = kr
    knrt[...] = kr.T
    nkr = kr.shape[0]
    vt1[pl.ds(0, HD), pl.ds(0, nkr)] = kvr[1].T
    vt1[pl.ds(HD, 16), pl.ds(0, nkr)] = jnp.ones((16, nkr), BF)
    for n in range(tiles):
        sl = pl.ds(n * TILE, TILE)
        if n < tiles_r:
            s = dot(knr[...], qnt[:, sl])
            at = lax.broadcasted_iota(jnp.int32, s.shape, 0)
            lane = lax.broadcasted_iota(jnp.int32, s.shape, 1) + n * TILE
            e = jnp.where(at * 8 <= lane, jnp.exp2(s * exp_scale), 0.0).astype(BF)
            er_ref[:, sl] = e
            ol[:, sl] = dot(vt1[:, pl.ds(0, nkr)], e)
        else:
            ol[:, sl] = jnp.zeros((HD + 16, TILE), F32)

    for half in range(2):
        far(far_block, 0, half).wait_recv()
    for way in (0, 1):
        near(far_block, 3, way).start()
    x_far(1, True)
    x_far(2, True)

    def pass1(step, carry):
        chunk = chunk_at(step)

        @pl.when(step == 1)
        def _():
            x_far(3, True)

        for half in range(2):
            far(block_at(step, 2), 0, half).wait_recv()

        n_keys = NX * kall.shape[2]
        at = lax.broadcasted_iota(jnp.int32, (n_keys, HD), 0) + chunk * n_keys
        k_raw = kall[pl.ds(chunk * NX, NX), 0].reshape(n_keys, HD).astype(F32)
        inv = lax.rsqrt(jnp.mean(k_raw * k_raw, axis=-1, keepdims=True) + EPSILON)
        unit = k_raw * inv
        uk_ref[step] = unit
        kf = unit * kg_ref[...]
        kn = kf.astype(BF)
        knt_ref[step] = jnp.where(at < plen, kf, 0.0).astype(BF).T
        v = kall[pl.ds(chunk * NX, NX), 1].reshape(n_keys, HD).astype(F32)
        vt1[pl.ds(0, HD), :] = jnp.where(at < plen, v, 0.0).astype(BF).T
        lane = lax.broadcasted_iota(jnp.int32, (16, n_keys), 1) + chunk * n_keys
        vt1[pl.ds(HD, 16), :] = jnp.where(lane < plen, 1.0, 0.0).astype(BF)
        ahead_s = dot(kn, qnt[:, pl.ds(0, TILE)])
        for n in range(tiles):
            sl = pl.ds(n * TILE, TILE)
            s = ahead_s
            if n + 1 < tiles:
                ahead_s = dot(kn, qnt[:, pl.ds((n + 1) * TILE, TILE)])
            e = jnp.exp2(s * exp_scale)
            if n >= tiles_r:
                key = lax.broadcasted_iota(jnp.int32, s.shape, 0)
                lane = lax.broadcasted_iota(jnp.int32, s.shape, 1) + (n * TILE - rows_r)
                ahead = resp * (rows_p // 8) - chunk * n_keys
                e = jnp.where((key - ahead) * 8 <= lane, e, 0.0)
            e = e.astype(BF)
            e_ref[step, :, sl] = e
            ol[:, sl] += dot(vt1[...], e)
        return carry

    lax.fori_loop(0, NY, pass1, 0)

    for n in range(tiles):
        sl = pl.ds(n * TILE, TILE)
        rl = 1.0 / ol[pl.ds(HD, 1), sl]
        ds = (dt[:, sl] * rl).astype(BF)
        dst[:, sl] = ds
        delta = rl * jnp.sum(ds.astype(F32) * ol[pl.ds(0, HD), sl], axis=0, keepdims=True)
        delta_ref[:, sl] = jnp.broadcast_to(delta, (8, TILE))
        gqt[:, sl] = jnp.zeros((HD, TILE), F32)
    kterm[...] = jnp.zeros((8, HD), F32)

    def x_first(slot, way):
        return send(
            x1_send.at[slot, way],
            x1_recv.at[slot, way],
            x_sent.at[slot, way],
            x_got.at[slot, way],
            way,
        )

    def x_second(slot, way):
        return send(
            x2_send.at[slot, way],
            x2_recv.at[slot, way],
            x_sent.at[slot, 2 + way],
            x_got.at[slot, 2 + way],
            way,
        )

    def y_first(way):
        return send(
            y1_send.at[way], y1_recv.at[way], y_sent.at[way], y_got.at[way], 2 + way
        )

    def y_second(way):
        return send(
            y2_send.at[way], y2_recv.at[way], y_sent.at[2 + way], y_got.at[2 + way], 2 + way
        )

    def piece(slot, which, dx):
        return sums[slot, which, pl.ds(lax.rem(x + dx, NX) * span, span), :]

    def x_start(slot):
        x1_send[slot, 0, 0] = piece(slot, 0, 2).astype(BF)
        x1_send[slot, 0, 1] = piece(slot, 1, 1).astype(BF)
        x1_send[slot, 1, 0] = piece(slot, 0, 3).astype(BF)
        x1_send[slot, 1, 1] = piece(slot, 1, 2).astype(BF)
        for way in range(2):
            x_first(slot, way).start()

    def x_pass_on(slot):
        for way, dx in ((0, 1), (1, 3)):
            x_first(slot, way).wait_recv()
            got = x1_recv[slot, way, way].astype(F32)
            x2_send[slot, way] = (piece(slot, way, dx) + got).astype(BF)
            x_second(slot, way).start()

    def x_total(slot):
        totals = []
        for which in range(2):
            x_second(slot, which).wait_recv()
            first = x1_recv[slot, 1 - which, which].astype(F32)
            second = x2_recv[slot, which].astype(F32)
            totals.append(piece(slot, which, 0) + first + second)
        return totals

    def y_far():
        for which, total in enumerate(x_total(3)):
            y1_send[which] = total.astype(BF)
            y_first(which).start()

    def y_near(way):
        totals = x_total(1 + way)
        y_first(way).wait_recv()
        totals[way] = totals[way] + y1_recv[way].astype(F32)
        for which in range(2):
            y2_send[way, which] = totals[which].astype(BF)
        y_second(way).start()

    span = kall.shape[2]

    def pass2(back, carry):
        step = NY - 1 - back
        chunk = chunk_at(step)
        n_keys = NX * span
        v = kall[pl.ds(chunk * NX, NX), 1].reshape(n_keys, HD)
        gk = jnp.zeros((n_keys, HD), F32)
        gv = jnp.zeros((n_keys, HD), F32)
        ahead_dp = dot(v, dst[:, pl.ds(0, TILE)])
        for n in range(tiles):
            sl = pl.ds(n * TILE, TILE)
            e = e_ref[step, :, sl]
            dp = ahead_dp
            if n + 1 < tiles:
                ahead_dp = dot(v, dst[:, pl.ds((n + 1) * TILE, TILE)])
            gv += dot(e, dst[:, sl], NT)
            gs = (e.astype(F32) * (dp - delta_ref[pl.ds(0, 1), sl])).astype(BF)
            gk += dot(gs, qn[sl, :])
            gqt[:, sl] += dot(knt_ref[step], gs)
        at = lax.broadcasted_iota(jnp.int32, (n_keys, HD), 0) + chunk * n_keys
        gk = jnp.where(at < plen, gk * scale, 0.0)
        gv = jnp.where(at < plen, gv, 0.0)
        kterm[...] += jnp.sum((gk * uk_ref[step]).reshape(n_keys // 8, 8, HD), axis=0)
        sums[step, 0] = gk
        sums[step, 1] = gv
        x_start(step)

        @pl.when(back == 0)
        def _():
            gkr = jnp.zeros((nkr, HD), F32)
            gvr = jnp.zeros((nkr, HD), F32)
            for n in range(tiles_r):
                sl = pl.ds(n * TILE, TILE)
                e = er_ref[:, sl]
                dp = dot(kvr[1], dst[:, sl])
                gs = (e.astype(F32) * (dp - delta_ref[pl.ds(0, 1), sl])).astype(BF)
                gkr += dot(gs, qn[sl, :])
                gvr += dot(e, dst[:, sl], NT)
                gqt[:, sl] += dot(knrt[...], gs)
            gkr = gkr * scale
            ur = ukr[...]
            kterm[...] += jnp.sum((gkr * ur).reshape(nkr // 8, 8, HD), axis=0)
            kf = kvr[0].astype(F32)
            inv = lax.rsqrt(jnp.mean(kf * kf, axis=-1, keepdims=True) + EPSILON)
            gu = gkr * kg_ref[...]
            dk = inv * (gu - ur * jnp.mean(gu * ur, axis=-1, keepdims=True))
            dkvr_v[0] = dk.astype(BF)
            dkvr_v[1] = gvr.astype(BF)

        @pl.when(back >= 2)
        def _():
            x_pass_on(step + 2)

        @pl.when(back == NY - 1)
        def _():
            y_far()

        return carry

    lax.fori_loop(0, NY, pass2, 0)

    stores = [
        pltpu.make_async_copy(dkvr_v, dkvr_out, out_sem.at[0]),
        pltpu.make_async_copy(dq_v.at[pl.ds(0, rows_r)], dqr_out, out_sem.at[1]),
        pltpu.make_async_copy(dq_v.at[pl.ds(rows_r, rows_p)], dqp_out, out_sem.at[2]),
        pltpu.make_async_copy(dkvp_v, dkvp_out, out_sem.at[3]),
        pltpu.make_async_copy(gsend.at[3, pl.ds(0, 2)], gains_out, out_sem.at[4]),
    ]
    stores[0].start()

    prod = jnp.zeros((HD, HD), F32)
    for n in range(rows // HD):
        sl = pl.ds(n * HD, HD)
        prod += gqt[:, sl] * unit_qt[:, sl]
    qterm = jnp.sum(prod.T, axis=0, keepdims=True) * scale
    key_sum = jnp.sum(kterm[...], axis=0, keepdims=True)
    which_row = lax.broadcasted_iota(jnp.int32, (8, HD), 0)
    gsend[0] = jnp.where(
        which_row == 0,
        jnp.broadcast_to(qterm, (8, HD)),
        jnp.where(which_row == 1, jnp.broadcast_to(key_sum, (8, HD)), 0.0),
    )

    def g_copy(stage, k):
        return pltpu.make_async_remote_copy(
            src_ref=gsend.at[stage],
            dst_ref=grecv.at[stage, stage_at[stage]],
            send_sem=g_send.at[stage, k - 1],
            recv_sem=g_recv.at[stage, k - 1],
            device_id=partner(stage, k),
            device_id_type=MESH,
        )

    def g_start(stage):
        for k in range(1, 8):
            g_copy(stage, k).start()
        grecv[stage, stage_at[stage]] = gsend[stage]

    def g_finish(stage):
        for k in range(1, 8):
            g_copy(stage, k).wait_recv()
        total = grecv[stage, 0]
        for k in range(1, 8):
            total = total + grecv[stage, k]
        gsend[stage + 1] = total

    g_start(0)
    x_pass_on(1)
    y_near(1)
    x_pass_on(0)

    for n in range(tiles):
        sl = pl.ds(n * TILE, TILE)
        ut = unit_qt[:, sl]
        gu = gqt[:, sl] * scale * gcol[...]
        back = inv_q[pl.ds(0, 1), sl] * (gu - ut * jnp.mean(gu * ut, axis=0, keepdims=True))
        dq_v[sl, :] = back.astype(BF).T
    stores[1].start()
    stores[2].start()

    g_finish(0)
    g_start(1)
    y_near(0)
    totals = x_total(0)

    for way in range(4):
        near(resp, 0, way).wait_send()
    far(down_block, 0, 2).wait_send()
    far(up_block, 0, 3).wait_send()
    for slot in range(NY):
        if slot > 0:
            for way in range(2):
                near(block_at(slot, 0), slot, way).wait_send()
        x_far(slot, False)
        for way in range(2):
            x_first(slot, way).wait_send()
            x_second(slot, way).wait_send()

    g_finish(1)
    g_start(2)

    for way in range(2):
        y_second(way).wait_recv()
        y_first(way).wait_send()
        y_second(way).wait_send()
    for which in range(2):
        for way in range(2):
            totals[which] = totals[which] + y2_recv[way, which].astype(F32)
    unit = uk_ref[0, pl.ds(x * span, span), :]
    kf = kall[resp, 0].astype(F32)
    inv = lax.rsqrt(jnp.mean(kf * kf, axis=-1, keepdims=True) + EPSILON)
    gu = totals[0] * kg_ref[...]
    dk = inv * (gu - unit * jnp.mean(gu * unit, axis=-1, keepdims=True))
    dkvp_v[0] = dk.astype(BF)
    dkvp_v[1] = totals[1].astype(BF)
    stores[3].start()

    g_finish(2)
    stores[4].start()

    for stage in range(3):
        for k in range(1, 8):
            g_copy(stage, k).wait_send()
    for store in stores:
        store.wait()


def hand_out(*refs):
    ins, outs, held = refs[:5], refs[5:10], refs[10:15]
    in_sem, out_sem = refs[15:]
    loads = [pltpu.make_async_copy(ins[n], held[n], in_sem.at[n]) for n in range(5)]
    stores = [pltpu.make_async_copy(held[n], outs[n], out_sem.at[n]) for n in range(5)]
    for load in loads:
        load.start()
    for load, store in zip(loads, stores):
        load.wait()
        store.start()
    for store in stores:
        store.wait()


def shards(
    q_prompt,
    q_resp,
    kv_prompt,
    kv_resp,
    dout_prompt,
    dout_resp,
    q_gain,
    k_gain,
    resp_len,
    prompt_len,
):
    span = q_prompt.shape[1]
    length = q_resp.shape[2]
    rows_r = length * 8
    rows_p = span * 8
    rows = rows_r + rows_p
    n_keys = NX * span
    any_spec = pl.BlockSpec(memory_space=pl.ANY)
    hbm = pl.BlockSpec(memory_space=pltpu.HBM)
    dma = pltpu.SemaphoreType.DMA
    out = pl.pallas_call(
        kernel,
        out_shape=(
            jax.ShapeDtypeStruct((rows_r, HD), BF),
            jax.ShapeDtypeStruct((rows_p, HD), BF),
            jax.ShapeDtypeStruct((2, span, HD), BF),
            jax.ShapeDtypeStruct((2, length, HD), BF),
            jax.ShapeDtypeStruct((2, HD), F32),
        ),
        in_specs=[hbm] * 10,
        out_specs=[any_spec] * 5,
        scratch_shapes=[
            pltpu.VMEM((1, HD), F32),
            pltpu.VMEM((1, HD), F32),
            pltpu.SMEM((1, 1), jnp.int32),
            pltpu.SMEM((1,), jnp.int32),
            pltpu.VMEM((rows, HD), BF),
            pltpu.VMEM((rows, HD), BF),
            pltpu.VMEM((2, length, HD), BF),
            pltpu.VMEM((NX * NY, 2, span, HD), BF),
            pltpu.VMEM((HD, rows), F32),
            pltpu.VMEM((8, rows), F32),
            pltpu.VMEM((HD, rows), BF),
            pltpu.VMEM((rows, HD), BF),
            pltpu.VMEM((HD, rows), F32),
            pltpu.VMEM((HD, rows), BF),
            pltpu.VMEM((8, rows), F32),
            pltpu.VMEM((HD, TILE), F32),
            pltpu.VMEM((NY, HD, n_keys), BF),
            pltpu.VMEM((NY, n_keys, HD), F32),
            pltpu.VMEM((HD + 16, n_keys), BF),
            pltpu.VMEM((length, HD), BF),
            pltpu.VMEM((HD, length), BF),
            pltpu.VMEM((length, HD), F32),
            pltpu.VMEM((NY, n_keys, rows), BF),
            pltpu.VMEM((length, rows_r), BF),
            pltpu.VMEM((HD + 16, rows), F32),
            pltpu.VMEM((HD, rows), F32),
            pltpu.VMEM((NY, 2, n_keys, HD), F32),
            pltpu.VMEM((NY, 2, 2, span, HD), BF),
            pltpu.VMEM((NY, 2, 2, span, HD), BF),
            pltpu.VMEM((NY, 2, span, HD), BF),
            pltpu.VMEM((NY, 2, span, HD), BF),
            pltpu.VMEM((2, span, HD), BF),
            pltpu.VMEM((2, span, HD), BF),
            pltpu.VMEM((2, 2, span, HD), BF),
            pltpu.VMEM((2, 2, span, HD), BF),
            pltpu.VMEM((8, HD), F32),
            pltpu.VMEM((4, 8, HD), F32),
            pltpu.VMEM((3, 8, 8, HD), F32),
            pltpu.VMEM((rows, HD), BF),
            pltpu.VMEM((2, span, HD), BF),
            pltpu.VMEM((2, length, HD), BF),
            dma((10,)),
            dma((5,)),
            dma((NX * NY,)),
            dma((NX * NY, 2)),
            dma((NY, 4)),
            dma((NY, 4)),
            dma((NY, 4)),
            dma((NY, 4)),
            dma((4,)),
            dma((4,)),
            dma((3, 7)),
            dma((3, 7)),
        ],
        compiler_params=pltpu.CompilerParams(
            collective_id=0, has_side_effects=True
        ),
        name="attention_grads",
    )(
        q_resp.reshape(rows_r, HD),
        q_prompt.reshape(rows_p, HD),
        kv_prompt.reshape(2, span, HD),
        kv_resp.reshape(2, length, HD),
        dout_resp.reshape(rows_r, HD),
        dout_prompt.reshape(rows_p, HD),
        q_gain.reshape(1, HD),
        k_gain.reshape(1, HD),
        resp_len,
        prompt_len,
    )
    out = pl.pallas_call(
        hand_out,
        out_shape=tuple(jax.ShapeDtypeStruct(a.shape, a.dtype) for a in out),
        in_specs=[any_spec] * 5,
        out_specs=[any_spec] * 5,
        scratch_shapes=[pltpu.VMEM(a.shape, a.dtype) for a in out] + [dma((5,))] * 2,
        name="hand_out",
    )(*out)
    return (
        out[1].reshape(q_prompt.shape),
        out[0].reshape(q_resp.shape),
        out[2].reshape(kv_prompt.shape),
        out[3].reshape(kv_resp.shape),
        out[4],
    )


def solution(mesh):
    return jax.shard_map(
        shards,
        mesh=mesh,
        in_specs=(
            P("grp", "resp", "head", None),
            P("grp", "resp", None, "head", None),
            P("grp", None, "resp", "head", None),
            P("grp", "resp", None, None, "head", None),
            P("grp", "resp", "head", None),
            P("grp", "resp", None, "head", None),
            P(),
            P(),
            P("grp", "resp"),
            P("grp"),
        ),
        out_specs=(
            P("grp", "resp", "head", None),
            P("grp", "resp", None, "head", None),
            P("grp", None, "resp", "head", None),
            P("grp", "resp", None, None, "head", None),
            P(),
        ),
        check_vma=False,
    )
```

```python
import functools
import math

import jax
import jax.numpy as jnp
from jax import lax
from jax.experimental import pallas as pl
from jax.experimental.pallas import tpu as pltpu
from jax.sharding import PartitionSpec as P

EPSILON = 1e-06
MESH = pl.DeviceIdType.MESH
HD = 128
BF = jnp.bfloat16
F32 = jnp.float32
NX = 4
NY = 4
TILE = 512
NT = (((1,), (1,)), ((), ()))
NN = (((1,), (0,)), ((), ()))


def dot(lhs, rhs, dims=NN):
    return lax.dot_general(lhs, rhs, dims, preferred_element_type=F32)


def order(step):
    return step + step // 2 - 2 * (step // 3)


def kernel(
    qr_in,
    qp_in,
    kvp_in,
    kvr_in,
    dr_in,
    dp_in,
    qg_in,
    kg_in,
    rlen_in,
    plen_in,
    dqr_out,
    dqp_out,
    dkvp_out,
    dkvr_out,
    gains_out,
    qg_ref,
    kg_ref,
    rlen_ref,
    plen_ref,
    q_nat,
    d_nat,
    kvr,
    kall,
    unit_qt,
    inv_q,
    qnt,
    qn,
    dt,
    dst,
    delta_ref,
    gcol,
    kn_ref,
    knt_ref,
    vt1,
    knr,
    knrt,
    ukr,
    e_ref,
    er_ref,
    ol,
    sums,
    part,
    rx,
    own,
    ys,
    ry,
    kterm,
    gsend,
    grecv,
    dq_v,
    dkvp_v,
    dkvr_v,
    in_sem,
    out_sem,
    kvx_got,
    kvy_got,
    kv_sent,
    rx_got,
    rx_sent,
    ry_got,
    ry_sent,
    g_got,
    g_sent,
):
    resp = lax.axis_index("resp")
    head = lax.axis_index("head")
    grp = lax.axis_index("grp")
    yh = resp // NX
    x = lax.rem(resp, NX)
    yl = head // 2
    core = lax.rem(head, 2)
    ngrp = 8
    y8 = 2 * yh + yl
    rows_r = qr_in.shape[0]
    rows_p = qp_in.shape[0]
    rows = rows_r + rows_p
    tiles = rows // TILE
    tiles_r = rows_r // TILE
    scale = HD**-0.5
    exp_scale = scale * math.log2(math.e)

    def partner(stage, k):
        if stage == 0:
            return {"grp": lax.rem(grp + k, ngrp)}
        if stage == 1:
            to = lax.rem(y8 + k, 8)
            return {"resp": (to // 2) * NX + x, "head": lax.rem(to, 2) * 2 + core}
        to = lax.rem(2 * x + core + k, 8)
        return {"resp": yh * NX + to // 2, "head": yl * 2 + lax.rem(to, 2)}

    stage_at = (grp, y8, 2 * x + core)

    loads = [
        pltpu.make_async_copy(kvp_in, kall.at[resp], in_sem.at[0]),
        pltpu.make_async_copy(qr_in, q_nat.at[pl.ds(0, rows_r)], in_sem.at[1]),
        pltpu.make_async_copy(qp_in, q_nat.at[pl.ds(rows_r, rows_p)], in_sem.at[2]),
        pltpu.make_async_copy(kvr_in, kvr, in_sem.at[3]),
        pltpu.make_async_copy(dr_in, d_nat.at[pl.ds(0, rows_r)], in_sem.at[4]),
        pltpu.make_async_copy(dp_in, d_nat.at[pl.ds(rows_r, rows_p)], in_sem.at[5]),
        pltpu.make_async_copy(qg_in, qg_ref, in_sem.at[6]),
        pltpu.make_async_copy(kg_in, kg_ref, in_sem.at[7]),
        pltpu.make_async_copy(rlen_in, rlen_ref, in_sem.at[8]),
        pltpu.make_async_copy(plen_in, plen_ref, in_sem.at[9]),
    ]
    loads[0].start()
    barrier = pltpu.get_barrier_semaphore()
    for stage in range(3):
        for k in range(1, 8):
            pl.semaphore_signal(
                barrier, inc=1, device_id=partner(stage, k), device_id_type=MESH
            )

    loads[0].wait()
    pl.semaphore_wait(barrier, 21)

    def remote(src, dst, sent, got, to):
        return pltpu.make_async_remote_copy(
            src_ref=src,
            dst_ref=dst,
            send_sem=sent,
            recv_sem=got,
            device_id={"resp": to},
            device_id_type=MESH,
        )

    def wait_for(ref, sem):
        pltpu.make_async_copy(ref, ref, sem).wait()

    def x_peer(dx):
        return yh * NX + lax.rem(x + dx, NX)

    def y_peer(dy):
        return lax.rem(yh + dy, NY) * NX + x

    def chunk_at(slot):
        return lax.rem(yh + order(slot), NY)

    def along_x(slot):
        block = kall.at[chunk_at(slot) * NX + x]
        for dx in (2, 1, 3):
            remote(block, block, kv_sent, kvx_got.at[slot], x_peer(dx)).start()

    for dy in (2, 1, 3):
        remote(
            kall.at[resp], kall.at[resp], kv_sent, kvy_got.at[dy - 1], y_peer(dy)
        ).start()
    along_x(0)
    for load in loads[1:]:
        load.start()

    def forward(slot):
        dy = (0, 1, 3, 2)[slot]
        wait_for(kall.at[y_peer(dy)], kvy_got.at[(4 - dy) - 1])
        along_x(slot)

    for load in loads[6:]:
        load.wait()
    plen = plen_ref[0]
    rlen = rlen_ref[0, 0]

    gcol[...] = jnp.broadcast_to(qg_ref[...], (TILE, HD)).T
    loads[1].wait()
    loads[2].wait()
    for n in range(tiles):
        sl = pl.ds(n * TILE, TILE)
        xt = q_nat[sl, :].T.astype(F32)
        inv = lax.rsqrt(jnp.mean(xt * xt, axis=0, keepdims=True) + EPSILON)
        ut = xt * inv
        unit_qt[:, sl] = ut
        inv_q[:, sl] = jnp.broadcast_to(inv, (8, TILE))
        qt = (ut * gcol[...]).astype(BF)
        qnt[:, sl] = qt
        qn[sl, :] = qt.T

    forward(1)
    forward(2)

    loads[4].wait()
    loads[5].wait()
    for n in range(tiles):
        sl = pl.ds(n * TILE, TILE)
        lane = lax.broadcasted_iota(jnp.int32, (HD, TILE), 1) + n * TILE
        if n < tiles_r:
            keep = lane < rlen * 8
        else:
            keep = lane - rows_r < (plen - rows_p // 8 * resp) * 8
        dt[:, sl] = jnp.where(keep, d_nat[sl, :].T.astype(F32), 0.0)

    loads[3].wait()
    kf = kvr[0].astype(F32)
    inv_kr = lax.rsqrt(jnp.mean(kf * kf, axis=-1, keepdims=True) + EPSILON)
    ur = kf * inv_kr
    ukr[...] = ur
    kr = (ur * kg_ref[...]).astype(BF)
    knr[...] = kr
    knrt[...] = kr.T
    nkr = kr.shape[0]
    vt1[pl.ds(0, HD), pl.ds(0, nkr)] = kvr[1].T
    vt1[pl.ds(HD, 16), pl.ds(0, nkr)] = jnp.ones((16, nkr), BF)
    for n in range(tiles):
        sl = pl.ds(n * TILE, TILE)
        if n < tiles_r:
            s = dot(knr[...], qnt[:, sl])
            at = lax.broadcasted_iota(jnp.int32, s.shape, 0)
            lane = lax.broadcasted_iota(jnp.int32, s.shape, 1) + n * TILE
            e = jnp.where(at * 8 <= lane, jnp.exp2(s * exp_scale), 0.0).astype(BF)
            er_ref[:, sl] = e
            ol[:, sl] = dot(vt1[:, pl.ds(0, nkr)], e)
        else:
            ol[:, sl] = jnp.zeros((HD + 16, TILE), F32)

    forward(3)

    def pass1(step, carry):
        chunk = chunk_at(step)
        wait_for(kall.at[pl.ds(0, NX - 1)], kvx_got.at[step])
        n_keys = NX * kall.shape[2]
        at = lax.broadcasted_iota(jnp.int32, (n_keys, HD), 0) + chunk * n_keys
        k_raw = kall[pl.ds(chunk * NX, NX), 0].reshape(n_keys, HD).astype(F32)
        inv = lax.rsqrt(jnp.mean(k_raw * k_raw, axis=-1, keepdims=True) + EPSILON)
        unit = k_raw * inv
        kf = unit * kg_ref[...]
        kn = kf.astype(BF)
        kn_ref[step] = kn
        knt_ref[step] = jnp.where(at < plen, kf, 0.0).astype(BF).T
        v = kall[pl.ds(chunk * NX, NX), 1].reshape(n_keys, HD).astype(F32)
        vt1[pl.ds(0, HD), :] = jnp.where(at < plen, v, 0.0).astype(BF).T
        lane = lax.broadcasted_iota(jnp.int32, (16, n_keys), 1) + chunk * n_keys
        vt1[pl.ds(HD, 16), :] = jnp.where(lane < plen, 1.0, 0.0).astype(BF)
        ahead_s = dot(kn, qnt[:, pl.ds(0, TILE)])
        for n in range(tiles):
            sl = pl.ds(n * TILE, TILE)
            s = ahead_s
            if n + 1 < tiles:
                ahead_s = dot(kn, qnt[:, pl.ds((n + 1) * TILE, TILE)])
            e = jnp.exp2(s * exp_scale)
            if n >= tiles_r:
                key = lax.broadcasted_iota(jnp.int32, s.shape, 0)
                lane = lax.broadcasted_iota(jnp.int32, s.shape, 1) + (n * TILE - rows_r)
                ahead = resp * (rows_p // 8) - chunk * n_keys
                e = jnp.where((key - ahead) * 8 <= lane, e, 0.0)
            e = e.astype(BF)
            e_ref[step, :, sl] = e
            ol[:, sl] += dot(vt1[...], e)
        return carry

    lax.fori_loop(0, NY, pass1, 0)

    for n in range(tiles):
        sl = pl.ds(n * TILE, TILE)
        rl = 1.0 / ol[pl.ds(HD, 1), sl]
        ds = (dt[:, sl] * rl).astype(BF)
        dst[:, sl] = ds
        delta = rl * jnp.sum(ds.astype(F32) * ol[pl.ds(0, HD), sl], axis=0, keepdims=True)
        delta_ref[:, sl] = jnp.broadcast_to(delta, (8, TILE))
    kterm[...] = jnp.zeros((8, HD), F32)

    def summed(slot, which):
        total = own[slot, which]
        for k in range(NX - 1):
            total = total + rx[slot, k, which].astype(F32)
        return total

    def along_y(slot):
        dy = (0, 1, 3, 2)[slot]
        wait_for(rx.at[slot], rx_got.at[slot])
        for which in range(2):
            ys[slot, which] = summed(slot, which).astype(BF)
        remote(ys.at[slot], ry.at[dy - 1], ry_sent, ry_got, y_peer(dy)).start()

    span = kall.shape[2]

    def pass2(back, carry):
        step = NY - 1 - back
        chunk = chunk_at(step)
        n_keys = NX * span
        v = kall[pl.ds(chunk * NX, NX), 1].reshape(n_keys, HD)
        gk = jnp.zeros((n_keys, HD), F32)
        gv = jnp.zeros((n_keys, HD), F32)
        ahead_dp = dot(v, dst[:, pl.ds(0, TILE)])
        for n in range(tiles):
            sl = pl.ds(n * TILE, TILE)
            e = e_ref[step, :, sl]
            dp = ahead_dp
            if n + 1 < tiles:
                ahead_dp = dot(v, dst[:, pl.ds((n + 1) * TILE, TILE)])
            gv += dot(e, dst[:, sl], NT)
            gs = (e.astype(F32) * (dp - delta_ref[pl.ds(0, 1), sl])).astype(BF)
            gk += dot(gs, qn[sl, :])
            e_ref[step, :, sl] = gs
        at = lax.broadcasted_iota(jnp.int32, (n_keys, HD), 0) + chunk * n_keys
        gk = jnp.where(at < plen, gk * scale, 0.0)
        gv = jnp.where(at < plen, gv, 0.0)
        kn = kn_ref[step].astype(F32)
        kterm[...] += jnp.sum((gk * kn).reshape(n_keys // 8, 8, HD), axis=0)
        sums[0] = gk
        sums[1] = gv
        for which in range(2):
            for k in range(NX):
                part[step, k, which] = sums[which, pl.ds(k * span, span)].astype(BF)
            own[step, which] = sums[which, pl.ds(x * span, span)]
        for dx in (2, 1, 3):
            remote(
                part.at[step, lax.rem(x + dx, NX)],
                rx.at[step, dx - 1],
                rx_sent,
                rx_got.at[step],
                x_peer(dx),
            ).start()

        @pl.when(back == 0)
        def _():
            gkr = jnp.zeros((nkr, HD), F32)
            gvr = jnp.zeros((nkr, HD), F32)
            for n in range(tiles_r):
                sl = pl.ds(n * TILE, TILE)
                e = er_ref[:, sl]
                dp = dot(kvr[1], dst[:, sl])
                gs = (e.astype(F32) * (dp - delta_ref[pl.ds(0, 1), sl])).astype(BF)
                gkr += dot(gs, qn[sl, :])
                gvr += dot(e, dst[:, sl], NT)
                er_ref[:, sl] = gs
            gkr = gkr * scale
            ur = ukr[...]
            kn = knr[...].astype(F32)
            kterm[...] += jnp.sum((gkr * kn).reshape(nkr // 8, 8, HD), axis=0)
            kf = kvr[0].astype(F32)
            inv = lax.rsqrt(jnp.mean(kf * kf, axis=-1, keepdims=True) + EPSILON)
            gu = gkr * kg_ref[...]
            dk = inv * (gu - ur * jnp.mean(gu * ur, axis=-1, keepdims=True))
            dkvr_v[0] = dk.astype(BF)
            dkvr_v[1] = gvr.astype(BF)

        return carry

    lax.fori_loop(0, NY, pass2, 0)

    stores = [
        pltpu.make_async_copy(dkvr_v, dkvr_out, out_sem.at[0]),
        pltpu.make_async_copy(dq_v.at[pl.ds(0, rows_r)], dqr_out, out_sem.at[1]),
        pltpu.make_async_copy(dq_v.at[pl.ds(rows_r, rows_p)], dqp_out, out_sem.at[2]),
        pltpu.make_async_copy(dkvp_v, dkvp_out, out_sem.at[3]),
        pltpu.make_async_copy(gsend.at[3, pl.ds(0, 2)], gains_out, out_sem.at[4]),
    ]
    stores[0].start()

    term = jnp.sum(kterm[...], axis=0, keepdims=True)
    qterm = term / qg_ref[...]
    key_sum = term / kg_ref[...]
    which_row = lax.broadcasted_iota(jnp.int32, (8, HD), 0)
    gsend[0] = jnp.where(
        which_row == 0,
        jnp.broadcast_to(qterm, (8, HD)),
        jnp.where(which_row == 1, jnp.broadcast_to(key_sum, (8, HD)), 0.0),
    )

    def g_start(stage):
        for k in range(1, 8):
            pltpu.make_async_remote_copy(
                src_ref=gsend.at[stage],
                dst_ref=grecv.at[stage, stage_at[stage]],
                send_sem=g_sent,
                recv_sem=g_got.at[stage],
                device_id=partner(stage, k),
                device_id_type=MESH,
            ).start()
        grecv[stage, stage_at[stage]] = gsend[stage]

    def g_finish(stage):
        wait_for(grecv.at[stage, pl.ds(0, 7)], g_got.at[stage])
        total = grecv[stage, 0]
        for k in range(1, 8):
            total = total + grecv[stage, k]
        gsend[stage + 1] = total

    g_start(0)

    for n in range(tiles):
        sl = pl.ds(n * TILE, TILE)
        gq = dot(knt_ref[0], e_ref[0, :, sl])
        for slot in range(1, NY):
            gq += dot(knt_ref[slot], e_ref[slot, :, sl])
        if n < tiles_r:
            gq += dot(knrt[...], er_ref[:, sl])
        ut = unit_qt[:, sl]
        gu = gq * scale * gcol[...]
        back = inv_q[pl.ds(0, 1), sl] * (gu - ut * jnp.mean(gu * ut, axis=0, keepdims=True))
        dq_v[sl, :] = back.astype(BF).T
    stores[1].start()
    stores[2].start()

    along_y(3)
    g_finish(0)
    g_start(1)
    along_y(2)
    along_y(1)
    wait_for(rx.at[0], rx_got.at[0])
    totals = [summed(0, which) for which in range(2)]
    kf = kall[resp, 0].astype(F32)
    inv = lax.rsqrt(jnp.mean(kf * kf, axis=-1, keepdims=True) + EPSILON)
    unit = kf * inv
    wait_for(kall.at[pl.ds(0, 15)], kv_sent)
    wait_for(rx, rx_sent)

    g_finish(1)
    g_start(2)

    wait_for(ry, ry_got)
    for which in range(2):
        for k in range(NY - 1):
            totals[which] = totals[which] + ry[k, which].astype(F32)
    gu = totals[0] * kg_ref[...]
    dk = inv * (gu - unit * jnp.mean(gu * unit, axis=-1, keepdims=True))
    dkvp_v[0] = dk.astype(BF)
    dkvp_v[1] = totals[1].astype(BF)
    stores[3].start()
    wait_for(ry, ry_sent)

    g_finish(2)
    stores[4].start()
    wait_for(grecv.at[:, pl.ds(0, 7)], g_sent)
    for store in stores:
        store.wait()


def hand_out(*refs):
    ins, outs, held = refs[:5], refs[5:10], refs[10:15]
    in_sem, out_sem = refs[15:]
    loads = [pltpu.make_async_copy(ins[n], held[n], in_sem.at[n]) for n in range(5)]
    stores = [pltpu.make_async_copy(held[n], outs[n], out_sem.at[n]) for n in range(5)]
    for load in loads:
        load.start()
    for load, store in zip(loads, stores):
        load.wait()
        store.start()
    for store in stores:
        store.wait()


def shards(
    q_prompt,
    q_resp,
    kv_prompt,
    kv_resp,
    dout_prompt,
    dout_resp,
    q_gain,
    k_gain,
    resp_len,
    prompt_len,
):
    span = q_prompt.shape[1]
    length = q_resp.shape[2]
    rows_r = length * 8
    rows_p = span * 8
    rows = rows_r + rows_p
    n_keys = NX * span
    any_spec = pl.BlockSpec(memory_space=pl.ANY)
    hbm = pl.BlockSpec(memory_space=pltpu.HBM)
    dma = pltpu.SemaphoreType.DMA
    out = pl.pallas_call(
        kernel,
        out_shape=(
            jax.ShapeDtypeStruct((rows_r, HD), BF),
            jax.ShapeDtypeStruct((rows_p, HD), BF),
            jax.ShapeDtypeStruct((2, span, HD), BF),
            jax.ShapeDtypeStruct((2, length, HD), BF),
            jax.ShapeDtypeStruct((2, HD), F32),
        ),
        in_specs=[hbm] * 10,
        out_specs=[any_spec] * 5,
        scratch_shapes=[
            pltpu.VMEM((1, HD), F32),
            pltpu.VMEM((1, HD), F32),
            pltpu.SMEM((1, 1), jnp.int32),
            pltpu.SMEM((1,), jnp.int32),
            pltpu.VMEM((rows, HD), BF),
            pltpu.VMEM((rows, HD), BF),
            pltpu.VMEM((2, length, HD), BF),
            pltpu.VMEM((NX * NY, 2, span, HD), BF),
            pltpu.VMEM((HD, rows), F32),
            pltpu.VMEM((8, rows), F32),
            pltpu.VMEM((HD, rows), BF),
            pltpu.VMEM((rows, HD), BF),
            pltpu.VMEM((HD, rows), F32),
            pltpu.VMEM((HD, rows), BF),
            pltpu.VMEM((8, rows), F32),
            pltpu.VMEM((HD, TILE), F32),
            pltpu.VMEM((NY, n_keys, HD), BF),
            pltpu.VMEM((NY, HD, n_keys), BF),
            pltpu.VMEM((HD + 16, n_keys), BF),
            pltpu.VMEM((length, HD), BF),
            pltpu.VMEM((HD, length), BF),
            pltpu.VMEM((length, HD), F32),
            pltpu.VMEM((NY, n_keys, rows), BF),
            pltpu.VMEM((length, rows_r), BF),
            pltpu.VMEM((HD + 16, rows), F32),
            pltpu.VMEM((2, n_keys, HD), F32),
            pltpu.VMEM((NY, NX, 2, span, HD), BF),
            pltpu.VMEM((NY, NX - 1, 2, span, HD), BF),
            pltpu.VMEM((NY, 2, span, HD), F32),
            pltpu.VMEM((NY, 2, span, HD), BF),
            pltpu.VMEM((NY - 1, 2, span, HD), BF),
            pltpu.VMEM((8, HD), F32),
            pltpu.VMEM((4, 8, HD), F32),
            pltpu.VMEM((3, 8, 8, HD), F32),
            pltpu.VMEM((rows, HD), BF),
            pltpu.VMEM((2, span, HD), BF),
            pltpu.VMEM((2, length, HD), BF),
            dma((10,)),
            dma((5,)),
            dma((NY,)),
            dma((NY - 1,)),
            dma,
            dma((NY,)),
            dma,
            dma,
            dma,
            dma((3,)),
            dma,
        ],
        compiler_params=pltpu.CompilerParams(
            collective_id=0, has_side_effects=True
        ),
        name="attention_grads",
    )(
        q_resp.reshape(rows_r, HD),
        q_prompt.reshape(rows_p, HD),
        kv_prompt.reshape(2, span, HD),
        kv_resp.reshape(2, length, HD),
        dout_resp.reshape(rows_r, HD),
        dout_prompt.reshape(rows_p, HD),
        q_gain.reshape(1, HD),
        k_gain.reshape(1, HD),
        resp_len,
        prompt_len,
    )
    out = pl.pallas_call(
        hand_out,
        out_shape=tuple(jax.ShapeDtypeStruct(a.shape, a.dtype) for a in out),
        in_specs=[any_spec] * 5,
        out_specs=[any_spec] * 5,
        scratch_shapes=[pltpu.VMEM(a.shape, a.dtype) for a in out] + [dma((5,))] * 2,
        name="hand_out",
    )(*out)
    return (
        out[1].reshape(q_prompt.shape),
        out[0].reshape(q_resp.shape),
        out[2].reshape(kv_prompt.shape),
        out[3].reshape(kv_resp.shape),
        out[4],
    )


def solution(mesh):
    return jax.shard_map(
        shards,
        mesh=mesh,
        in_specs=(
            P("grp", "resp", "head", None),
            P("grp", "resp", None, "head", None),
            P("grp", None, "resp", "head", None),
            P("grp", "resp", None, None, "head", None),
            P("grp", "resp", "head", None),
            P("grp", "resp", None, "head", None),
            P(),
            P(),
            P("grp", "resp"),
            P("grp"),
        ),
        out_specs=(
            P("grp", "resp", "head", None),
            P("grp", "resp", None, "head", None),
            P("grp", None, "resp", "head", None),
            P("grp", "resp", None, None, "head", None),
            P(),
        ),
        check_vma=False,
    )
```

```python
import functools
import math

import jax
import jax.numpy as jnp
from jax import lax
from jax.experimental import pallas as pl
from jax.experimental.pallas import tpu as pltpu
from jax.sharding import PartitionSpec as P

EPSILON = 1e-06
MESH = pl.DeviceIdType.MESH
HD = 128
BF = jnp.bfloat16
F32 = jnp.float32
NX = 4
NY = 4
TILE = 512
FARTHEST_FIRST = (4, 3, 5, 2, 6, 1, 7)
NT = (((1,), (1,)), ((), ()))
NN = (((1,), (0,)), ((), ()))


def dot(lhs, rhs, dims=NN):
    return lax.dot_general(lhs, rhs, dims, preferred_element_type=F32)


def order(step):
    return step + step // 2 - 2 * (step // 3)


def kernel(
    qr_in,
    qp_in,
    kvp_in,
    kvr_in,
    dr_in,
    dp_in,
    qg_in,
    kg_in,
    rlen_in,
    plen_in,
    dqr_out,
    dqp_out,
    dkvp_out,
    dkvr_out,
    gains_out,
    qg_ref,
    kg_ref,
    rlen_ref,
    plen_ref,
    q_nat,
    d_nat,
    kvr,
    kall,
    unit_qt,
    inv_q,
    qnt,
    qn,
    dt,
    dst,
    delta_ref,
    gcol,
    kn_ref,
    knt_ref,
    vt1,
    knr,
    knrt,
    ukr,
    e_ref,
    er_ref,
    gs_ref,
    gsr_ref,
    ol,
    sums,
    vsum,
    part,
    rx,
    own,
    ys,
    ry,
    kterm,
    gsend,
    grecv,
    dq_v,
    dkvp_v,
    dkvr_v,
    in_sem,
    out_sem,
    kvx_got,
    kvy_got,
    kv_sent,
    rx_got,
    rx_sent,
    ry_got,
    ry_sent,
    g_got,
    g_sent,
):
    resp = lax.axis_index("resp")
    head = lax.axis_index("head")
    grp = lax.axis_index("grp")
    yh = resp // NX
    x = lax.rem(resp, NX)
    yl = head // 2
    core = lax.rem(head, 2)
    ngrp = 8
    y8 = 2 * yh + yl
    rows_r = qr_in.shape[0]
    rows_p = qp_in.shape[0]
    rows = rows_r + rows_p
    tiles = rows // TILE
    tiles_r = rows_r // TILE
    scale = HD**-0.5
    exp_scale = scale * math.log2(math.e)

    def partner(stage, k):
        if stage == 0:
            return {"grp": lax.rem(grp + k, ngrp)}
        if stage == 1:
            to = lax.rem(y8 + k, 8)
            return {"resp": (to // 2) * NX + x, "head": lax.rem(to, 2) * 2 + core}
        to = lax.rem(2 * x + core + k, 8)
        return {"resp": yh * NX + to // 2, "head": yl * 2 + lax.rem(to, 2)}

    stage_at = (grp, y8, 2 * x + core)

    loads = [
        pltpu.make_async_copy(kvp_in, kall.at[resp], in_sem.at[0]),
        pltpu.make_async_copy(qr_in, q_nat.at[pl.ds(0, rows_r)], in_sem.at[1]),
        pltpu.make_async_copy(qp_in, q_nat.at[pl.ds(rows_r, rows_p)], in_sem.at[2]),
        pltpu.make_async_copy(kvr_in, kvr, in_sem.at[3]),
        pltpu.make_async_copy(dr_in, d_nat.at[pl.ds(0, rows_r)], in_sem.at[4]),
        pltpu.make_async_copy(dp_in, d_nat.at[pl.ds(rows_r, rows_p)], in_sem.at[5]),
        pltpu.make_async_copy(qg_in, qg_ref, in_sem.at[6]),
        pltpu.make_async_copy(kg_in, kg_ref, in_sem.at[7]),
        pltpu.make_async_copy(rlen_in, rlen_ref, in_sem.at[8]),
        pltpu.make_async_copy(plen_in, plen_ref, in_sem.at[9]),
    ]
    loads[0].start()
    barrier = pltpu.get_barrier_semaphore()
    for k in FARTHEST_FIRST:
        for stage in range(3):
            pl.semaphore_signal(
                barrier, inc=1, device_id=partner(stage, k), device_id_type=MESH
            )

    loads[0].wait()
    pl.semaphore_wait(barrier, 21)

    def remote(src, dst, sent, got, to):
        return pltpu.make_async_remote_copy(
            src_ref=src,
            dst_ref=dst,
            send_sem=sent,
            recv_sem=got,
            device_id={"resp": to},
            device_id_type=MESH,
        )

    def wait_for(ref, sem):
        pltpu.make_async_copy(ref, ref, sem).wait()

    def x_peer(dx):
        return yh * NX + lax.rem(x + dx, NX)

    def y_peer(dy):
        return lax.rem(yh + dy, NY) * NX + x

    def chunk_at(slot):
        return lax.rem(yh + order(slot), NY)

    def along_x(slot):
        block = kall.at[chunk_at(slot) * NX + x]
        for dx in (2, 1, 3):
            remote(block, block, kv_sent, kvx_got.at[slot], x_peer(dx)).start()

    for dy in (2, 1, 3):
        remote(
            kall.at[resp], kall.at[resp], kv_sent, kvy_got.at[dy - 1], y_peer(dy)
        ).start()
    along_x(0)
    for load in loads[1:]:
        load.start()

    def forward(slot):
        dy = (0, 1, 3, 2)[slot]
        wait_for(kall.at[y_peer(dy)], kvy_got.at[(4 - dy) - 1])
        along_x(slot)

    for load in loads[6:]:
        load.wait()
    plen = plen_ref[0]
    rlen = rlen_ref[0, 0]

    gcol[...] = jnp.broadcast_to(qg_ref[...], (TILE, HD)).T
    loads[1].wait()
    loads[2].wait()
    for n in range(tiles):
        sl = pl.ds(n * TILE, TILE)
        xt = q_nat[sl, :].T.astype(F32)
        inv = lax.rsqrt(jnp.mean(xt * xt, axis=0, keepdims=True) + EPSILON)
        ut = xt * inv
        unit_qt[:, sl] = ut
        inv_q[:, sl] = jnp.broadcast_to(inv, (8, TILE))
        qt = (ut * gcol[...]).astype(BF)
        qnt[:, sl] = qt
        qn[sl, :] = qt.T

    forward(1)
    forward(2)

    loads[4].wait()
    loads[5].wait()
    for n in range(tiles):
        sl = pl.ds(n * TILE, TILE)
        lane = lax.broadcasted_iota(jnp.int32, (HD, TILE), 1) + n * TILE
        if n < tiles_r:
            keep = lane < rlen * 8
        else:
            keep = lane - rows_r < (plen - rows_p // 8 * resp) * 8
        dt[:, sl] = jnp.where(keep, d_nat[sl, :].T.astype(F32), 0.0)

    loads[3].wait()
    kf = kvr[0].astype(F32)
    inv_kr = lax.rsqrt(jnp.mean(kf * kf, axis=-1, keepdims=True) + EPSILON)
    ur = kf * inv_kr
    ukr[...] = ur
    kr = (ur * kg_ref[...]).astype(BF)
    knr[...] = kr
    knrt[...] = kr.T
    nkr = kr.shape[0]
    vt1[pl.ds(0, HD), pl.ds(0, nkr)] = kvr[1].T
    vt1[pl.ds(HD, 16), pl.ds(0, nkr)] = jnp.ones((16, nkr), BF)
    for n in range(tiles):
        sl = pl.ds(n * TILE, TILE)
        if n < tiles_r:
            s = dot(knr[...], qnt[:, sl])
            at = lax.broadcasted_iota(jnp.int32, s.shape, 0)
            lane = lax.broadcasted_iota(jnp.int32, s.shape, 1) + n * TILE
            e = jnp.where(at * 8 <= lane, jnp.exp2(s * exp_scale), 0.0).astype(BF)
            er_ref[:, sl] = e
            ol[:, sl] = dot(vt1[:, pl.ds(0, nkr)], e)
        else:
            ol[:, sl] = jnp.zeros((HD + 16, TILE), F32)

    forward(3)

    def pass1(step, carry):
        chunk = chunk_at(step)
        wait_for(kall.at[pl.ds(0, NX - 1)], kvx_got.at[step])
        n_keys = NX * kall.shape[2]
        at = lax.broadcasted_iota(jnp.int32, (n_keys, HD), 0) + chunk * n_keys
        k_raw = kall[pl.ds(chunk * NX, NX), 0].reshape(n_keys, HD).astype(F32)
        inv = lax.rsqrt(jnp.mean(k_raw * k_raw, axis=-1, keepdims=True) + EPSILON)
        unit = k_raw * inv
        kf = unit * kg_ref[...]
        kn = kf.astype(BF)
        kn_ref[step] = kn
        knt_ref[step] = jnp.where(at < plen, kf, 0.0).astype(BF).T
        v = kall[pl.ds(chunk * NX, NX), 1].reshape(n_keys, HD).astype(F32)
        vt1[pl.ds(0, HD), :] = jnp.where(at < plen, v, 0.0).astype(BF).T
        lane = lax.broadcasted_iota(jnp.int32, (16, n_keys), 1) + chunk * n_keys
        vt1[pl.ds(HD, 16), :] = jnp.where(lane < plen, 1.0, 0.0).astype(BF)
        ahead_s = dot(kn, qnt[:, pl.ds(0, TILE)])
        for n in range(tiles):
            sl = pl.ds(n * TILE, TILE)
            s = ahead_s
            if n + 1 < tiles:
                ahead_s = dot(kn, qnt[:, pl.ds((n + 1) * TILE, TILE)])
            e = jnp.exp2(s * exp_scale)
            if n >= tiles_r:
                key = lax.broadcasted_iota(jnp.int32, s.shape, 0)
                lane = lax.broadcasted_iota(jnp.int32, s.shape, 1) + (n * TILE - rows_r)
                ahead = resp * (rows_p // 8) - chunk * n_keys
                e = jnp.where((key - ahead) * 8 <= lane, e, 0.0)
            e = e.astype(BF)
            e_ref[step, :, sl] = e
            ol[:, sl] += dot(vt1[...], e)
        return carry

    lax.fori_loop(0, NY, pass1, 0)

    for n in range(tiles):
        sl = pl.ds(n * TILE, TILE)
        rl = 1.0 / ol[pl.ds(HD, 1), sl]
        ds = (dt[:, sl] * rl).astype(BF)
        dst[:, sl] = ds
        delta = rl * jnp.sum(ds.astype(F32) * ol[pl.ds(0, HD), sl], axis=0, keepdims=True)
        delta_ref[:, sl] = jnp.broadcast_to(delta, (8, TILE))
    kterm[...] = jnp.zeros((8, HD), F32)

    def summed(slot, which):
        total = own[slot, which]
        for k in range(NX - 1):
            total = total + rx[slot, k, which].astype(F32)
        return total

    def along_y(slot):
        dy = (0, 1, 3, 2)[slot]
        wait_for(rx.at[slot], rx_got.at[slot])
        for which in range(2):
            ys[slot, which] = summed(slot, which).astype(BF)
        remote(ys.at[slot], ry.at[dy - 1], ry_sent, ry_got, y_peer(dy)).start()

    span = kall.shape[2]

    def pass2(back, carry):
        step = NY - 1 - back
        chunk = chunk_at(step)
        n_keys = NX * span
        v = kall[pl.ds(chunk * NX, NX), 1].reshape(n_keys, HD)
        gk = jnp.zeros((n_keys, HD), F32)
        ahead_dp = dot(v, dst[:, pl.ds(0, TILE)])
        for n in range(tiles):
            sl = pl.ds(n * TILE, TILE)
            dp = ahead_dp
            if n + 1 < tiles:
                ahead_dp = dot(v, dst[:, pl.ds((n + 1) * TILE, TILE)])
            e = e_ref[step, :, sl].astype(F32)
            gs = (e * (dp - delta_ref[pl.ds(0, 1), sl])).astype(BF)
            gs_ref[step, :, sl] = gs
            gk += dot(gs, qn[sl, :])
        at = lax.broadcasted_iota(jnp.int32, (n_keys, HD), 0) + chunk * n_keys
        gk = jnp.where(at < plen, gk * scale, 0.0)
        kn = kn_ref[step].astype(F32)
        kterm[...] += jnp.sum((gk * kn).reshape(n_keys // 8, 8, HD), axis=0)
        sums[step] = gk
        return carry

    lax.fori_loop(0, NY, pass2, 0)

    gkr = jnp.zeros((nkr, HD), F32)
    for n in range(tiles_r):
        sl = pl.ds(n * TILE, TILE)
        dp = dot(kvr[1], dst[:, sl])
        e = er_ref[:, sl].astype(F32)
        gs = (e * (dp - delta_ref[pl.ds(0, 1), sl])).astype(BF)
        gsr_ref[:, sl] = gs
        gkr += dot(gs, qn[sl, :])
    gkr = gkr * scale
    kn = knr[...].astype(F32)
    kterm[...] += jnp.sum((gkr * kn).reshape(nkr // 8, 8, HD), axis=0)

    stores = [
        pltpu.make_async_copy(dkvr_v, dkvr_out, out_sem.at[0]),
        pltpu.make_async_copy(dq_v.at[pl.ds(0, rows_r)], dqr_out, out_sem.at[1]),
        pltpu.make_async_copy(dq_v.at[pl.ds(rows_r, rows_p)], dqp_out, out_sem.at[2]),
        pltpu.make_async_copy(dkvp_v, dkvp_out, out_sem.at[3]),
        pltpu.make_async_copy(gsend.at[3, pl.ds(0, 2)], gains_out, out_sem.at[4]),
    ]
    term = jnp.sum(kterm[...], axis=0, keepdims=True)
    qterm = term / qg_ref[...]
    key_sum = term / kg_ref[...]
    which_row = lax.broadcasted_iota(jnp.int32, (8, HD), 0)
    gsend[0] = jnp.where(
        which_row == 0,
        jnp.broadcast_to(qterm, (8, HD)),
        jnp.where(which_row == 1, jnp.broadcast_to(key_sum, (8, HD)), 0.0),
    )

    def g_start(stage):
        for k in FARTHEST_FIRST:
            pltpu.make_async_remote_copy(
                src_ref=gsend.at[stage],
                dst_ref=grecv.at[stage, stage_at[stage]],
                send_sem=g_sent,
                recv_sem=g_got.at[stage],
                device_id=partner(stage, k),
                device_id_type=MESH,
            ).start()
        grecv[stage, stage_at[stage]] = gsend[stage]

    def g_finish(stage):
        wait_for(grecv.at[stage, pl.ds(0, 7)], g_got.at[stage])
        total = grecv[stage, 0]
        for k in range(1, 8):
            total = total + grecv[stage, k]
        gsend[stage + 1] = total

    g_start(0)

    def pass3(back, carry):
        step = NY - 1 - back
        n_keys = NX * span
        at = lax.broadcasted_iota(jnp.int32, (n_keys, HD), 0) + chunk_at(step) * n_keys
        gv = dot(e_ref[step], dst[...], NT)
        vsum[...] = jnp.where(at < plen, gv, 0.0)
        for k in range(NX):
            part[step, k, 0] = sums[step, pl.ds(k * span, span), :].astype(BF)
            part[step, k, 1] = vsum[pl.ds(k * span, span), :].astype(BF)
        own[step, 0] = sums[step, pl.ds(x * span, span), :]
        own[step, 1] = vsum[pl.ds(x * span, span), :]
        for dx in (2, 1, 3):
            remote(
                part.at[step, lax.rem(x + dx, NX)],
                rx.at[step, dx - 1],
                rx_sent,
                rx_got.at[step],
                x_peer(dx),
            ).start()
        return carry

    lax.fori_loop(0, NY, pass3, 0)

    gvr = dot(er_ref[...], dst[:, pl.ds(0, rows_r)], NT)
    ur = ukr[...]
    kf = kvr[0].astype(F32)
    inv = lax.rsqrt(jnp.mean(kf * kf, axis=-1, keepdims=True) + EPSILON)
    gu = gkr * kg_ref[...]
    dk = inv * (gu - ur * jnp.mean(gu * ur, axis=-1, keepdims=True))
    dkvr_v[0] = dk.astype(BF)
    dkvr_v[1] = gvr.astype(BF)
    stores[0].start()


    for n in range(tiles):
        sl = pl.ds(n * TILE, TILE)
        gq = dot(knt_ref[0], gs_ref[0, :, sl])
        for slot in range(1, NY):
            gq += dot(knt_ref[slot], gs_ref[slot, :, sl])
        if n < tiles_r:
            gq += dot(knrt[...], gsr_ref[:, sl])
        ut = unit_qt[:, sl]
        gu = gq * scale * gcol[...]
        back = inv_q[pl.ds(0, 1), sl] * (gu - ut * jnp.mean(gu * ut, axis=0, keepdims=True))
        dq_v[sl, :] = back.astype(BF).T
    stores[1].start()
    stores[2].start()

    along_y(3)
    g_finish(0)
    g_start(1)
    along_y(2)
    along_y(1)
    wait_for(rx.at[0], rx_got.at[0])
    totals = [summed(0, which) for which in range(2)]
    kf = kall[resp, 0].astype(F32)
    inv = lax.rsqrt(jnp.mean(kf * kf, axis=-1, keepdims=True) + EPSILON)
    unit = kf * inv
    wait_for(kall.at[pl.ds(0, 15)], kv_sent)
    wait_for(rx, rx_sent)

    g_finish(1)
    g_start(2)

    wait_for(ry, ry_got)
    for which in range(2):
        for k in range(NY - 1):
            totals[which] = totals[which] + ry[k, which].astype(F32)
    gu = totals[0] * kg_ref[...]
    dk = inv * (gu - unit * jnp.mean(gu * unit, axis=-1, keepdims=True))
    dkvp_v[0] = dk.astype(BF)
    dkvp_v[1] = totals[1].astype(BF)
    stores[3].start()
    wait_for(ry, ry_sent)

    g_finish(2)
    stores[4].start()
    wait_for(grecv.at[:, pl.ds(0, 7)], g_sent)
    for store in stores:
        store.wait()


def hand_out(*refs):
    ins, outs, held = refs[:5], refs[5:10], refs[10:15]
    in_sem, out_sem = refs[15:]
    loads = [pltpu.make_async_copy(ins[n], held[n], in_sem.at[n]) for n in range(5)]
    stores = [pltpu.make_async_copy(held[n], outs[n], out_sem.at[n]) for n in range(5)]
    for load in loads:
        load.start()
    for load, store in zip(loads, stores):
        load.wait()
        store.start()
    for store in stores:
        store.wait()


def shards(
    q_prompt,
    q_resp,
    kv_prompt,
    kv_resp,
    dout_prompt,
    dout_resp,
    q_gain,
    k_gain,
    resp_len,
    prompt_len,
):
    span = q_prompt.shape[1]
    length = q_resp.shape[2]
    rows_r = length * 8
    rows_p = span * 8
    rows = rows_r + rows_p
    n_keys = NX * span
    any_spec = pl.BlockSpec(memory_space=pl.ANY)
    hbm = pl.BlockSpec(memory_space=pltpu.HBM)
    dma = pltpu.SemaphoreType.DMA
    out = pl.pallas_call(
        kernel,
        out_shape=(
            jax.ShapeDtypeStruct((rows_r, HD), BF),
            jax.ShapeDtypeStruct((rows_p, HD), BF),
            jax.ShapeDtypeStruct((2, span, HD), BF),
            jax.ShapeDtypeStruct((2, length, HD), BF),
            jax.ShapeDtypeStruct((2, HD), F32),
        ),
        in_specs=[hbm] * 10,
        out_specs=[any_spec] * 5,
        scratch_shapes=[
            pltpu.VMEM((1, HD), F32),
            pltpu.VMEM((1, HD), F32),
            pltpu.SMEM((1, 1), jnp.int32),
            pltpu.SMEM((1,), jnp.int32),
            pltpu.VMEM((rows, HD), BF),
            pltpu.VMEM((rows, HD), BF),
            pltpu.VMEM((2, length, HD), BF),
            pltpu.VMEM((NX * NY, 2, span, HD), BF),
            pltpu.VMEM((HD, rows), F32),
            pltpu.VMEM((8, rows), F32),
            pltpu.VMEM((HD, rows), BF),
            pltpu.VMEM((rows, HD), BF),
            pltpu.VMEM((HD, rows), F32),
            pltpu.VMEM((HD, rows), BF),
            pltpu.VMEM((8, rows), F32),
            pltpu.VMEM((HD, TILE), F32),
            pltpu.VMEM((NY, n_keys, HD), BF),
            pltpu.VMEM((NY, HD, n_keys), BF),
            pltpu.VMEM((HD + 16, n_keys), BF),
            pltpu.VMEM((length, HD), BF),
            pltpu.VMEM((HD, length), BF),
            pltpu.VMEM((length, HD), F32),
            pltpu.VMEM((NY, n_keys, rows), BF),
            pltpu.VMEM((length, rows_r), BF),
            pltpu.VMEM((NY, n_keys, rows), BF),
            pltpu.VMEM((length, rows_r), BF),
            pltpu.VMEM((HD + 16, rows), F32),
            pltpu.VMEM((NY, n_keys, HD), F32),
            pltpu.VMEM((n_keys, HD), F32),
            pltpu.VMEM((NY, NX, 2, span, HD), BF),
            pltpu.VMEM((NY, NX - 1, 2, span, HD), BF),
            pltpu.VMEM((NY, 2, span, HD), F32),
            pltpu.VMEM((NY, 2, span, HD), BF),
            pltpu.VMEM((NY - 1, 2, span, HD), BF),
            pltpu.VMEM((8, HD), F32),
            pltpu.VMEM((4, 8, HD), F32),
            pltpu.VMEM((3, 8, 8, HD), F32),
            pltpu.VMEM((rows, HD), BF),
            pltpu.VMEM((2, span, HD), BF),
            pltpu.VMEM((2, length, HD), BF),
            dma((10,)),
            dma((5,)),
            dma((NY,)),
            dma((NY - 1,)),
            dma,
            dma((NY,)),
            dma,
            dma,
            dma,
            dma((3,)),
            dma,
        ],
        compiler_params=pltpu.CompilerParams(
            collective_id=0, has_side_effects=True, vmem_limit_bytes=62 * 2**20
        ),
        name="attention_grads",
    )(
        q_resp.reshape(rows_r, HD),
        q_prompt.reshape(rows_p, HD),
        kv_prompt.reshape(2, span, HD),
        kv_resp.reshape(2, length, HD),
        dout_resp.reshape(rows_r, HD),
        dout_prompt.reshape(rows_p, HD),
        q_gain.reshape(1, HD),
        k_gain.reshape(1, HD),
        resp_len,
        prompt_len,
    )
    out = pl.pallas_call(
        hand_out,
        out_shape=tuple(jax.ShapeDtypeStruct(a.shape, a.dtype) for a in out),
        in_specs=[any_spec] * 5,
        out_specs=[any_spec] * 5,
        scratch_shapes=[pltpu.VMEM(a.shape, a.dtype) for a in out] + [dma((5,))] * 2,
        name="hand_out",
    )(*out)
    return (
        out[1].reshape(q_prompt.shape),
        out[0].reshape(q_resp.shape),
        out[2].reshape(kv_prompt.shape),
        out[3].reshape(kv_resp.shape),
        out[4],
    )


def solution(mesh):
    return jax.shard_map(
        shards,
        mesh=mesh,
        in_specs=(
            P("grp", "resp", "head", None),
            P("grp", "resp", None, "head", None),
            P("grp", None, "resp", "head", None),
            P("grp", "resp", None, None, "head", None),
            P("grp", "resp", "head", None),
            P("grp", "resp", None, "head", None),
            P(),
            P(),
            P("grp", "resp"),
            P("grp"),
        ),
        out_specs=(
            P("grp", "resp", "head", None),
            P("grp", "resp", None, "head", None),
            P("grp", None, "resp", "head", None),
            P("grp", "resp", None, None, "head", None),
            P(),
        ),
        check_vma=False,
    )
```

```python
import functools
import math

import jax
import jax.numpy as jnp
from jax import lax
from jax.experimental import pallas as pl
from jax.experimental.pallas import tpu as pltpu
from jax.sharding import PartitionSpec as P

EPSILON = 1e-06
MESH = pl.DeviceIdType.MESH
HD = 128
BF = jnp.bfloat16
F32 = jnp.float32
NX = 4
NY = 4
TILE = 512
FARTHEST_FIRST = (4, 3, 5, 2, 6, 1, 7)
NT = (((1,), (1,)), ((), ()))
NN = (((1,), (0,)), ((), ()))


def dot(lhs, rhs, dims=NN):
    return lax.dot_general(lhs, rhs, dims, preferred_element_type=F32)


def order(step):
    return step + step // 2 - 2 * (step // 3)


def kernel(
    qr_in,
    qp_in,
    kvp_in,
    kvr_in,
    dr_in,
    dp_in,
    qg_in,
    kg_in,
    rlen_in,
    plen_in,
    dqr_out,
    dqp_out,
    dkvp_out,
    dkvr_out,
    gains_out,
    qg_ref,
    kg_ref,
    rlen_ref,
    plen_ref,
    q_nat,
    d_nat,
    kvr,
    kall,
    unit_qt,
    inv_q,
    qnt,
    qn,
    dt,
    dst,
    delta_ref,
    gcol,
    kn_ref,
    knt_ref,
    vt1,
    knr,
    knrt,
    ukr,
    e_ref,
    er_ref,
    gs_ref,
    gsr_ref,
    ol,
    sums,
    vsum,
    part,
    rx,
    own,
    ys,
    ry,
    kterm,
    gsend,
    grecv,
    dq_v,
    dkvp_v,
    dkvr_v,
    in_sem,
    out_sem,
    near_got,
    far_got,
    kvy_got,
    kv_sent,
    rx_got,
    rx_sent,
    ry_got,
    ry_sent,
    g_got,
    g_sent,
):
    resp = lax.axis_index("resp")
    head = lax.axis_index("head")
    grp = lax.axis_index("grp")
    yh = resp // NX
    x = lax.rem(resp, NX)
    yl = head // 2
    core = lax.rem(head, 2)
    ngrp = 8
    y8 = 2 * yh + yl
    rows_r = qr_in.shape[0]
    rows_p = qp_in.shape[0]
    rows = rows_r + rows_p
    tiles = rows // TILE
    tiles_r = rows_r // TILE
    scale = HD**-0.5
    exp_scale = scale * math.log2(math.e)

    def partner(stage, k):
        if stage == 0:
            return {"grp": lax.rem(grp + k, ngrp)}
        if stage == 1:
            to = lax.rem(y8 + k, 8)
            return {"resp": (to // 2) * NX + x, "head": lax.rem(to, 2) * 2 + core}
        to = lax.rem(2 * x + core + k, 8)
        return {"resp": yh * NX + to // 2, "head": yl * 2 + lax.rem(to, 2)}

    stage_at = (grp, y8, 2 * x + core)

    loads = [
        pltpu.make_async_copy(kvp_in, kall.at[resp], in_sem.at[0]),
        pltpu.make_async_copy(qr_in, q_nat.at[pl.ds(0, rows_r)], in_sem.at[1]),
        pltpu.make_async_copy(qp_in, q_nat.at[pl.ds(rows_r, rows_p)], in_sem.at[2]),
        pltpu.make_async_copy(kvr_in, kvr, in_sem.at[3]),
        pltpu.make_async_copy(dr_in, d_nat.at[pl.ds(0, rows_r)], in_sem.at[4]),
        pltpu.make_async_copy(dp_in, d_nat.at[pl.ds(rows_r, rows_p)], in_sem.at[5]),
        pltpu.make_async_copy(qg_in, qg_ref, in_sem.at[6]),
        pltpu.make_async_copy(kg_in, kg_ref, in_sem.at[7]),
        pltpu.make_async_copy(rlen_in, rlen_ref, in_sem.at[8]),
        pltpu.make_async_copy(plen_in, plen_ref, in_sem.at[9]),
    ]
    loads[0].start()
    barrier = pltpu.get_barrier_semaphore()
    for k in FARTHEST_FIRST:
        for stage in range(3):
            pl.semaphore_signal(
                barrier, inc=1, device_id=partner(stage, k), device_id_type=MESH
            )

    loads[0].wait()
    pl.semaphore_wait(barrier, 21)

    def remote(src, dst, sent, got, to):
        return pltpu.make_async_remote_copy(
            src_ref=src,
            dst_ref=dst,
            send_sem=sent,
            recv_sem=got,
            device_id={"resp": to},
            device_id_type=MESH,
        )

    def wait_for(ref, sem):
        pltpu.make_async_copy(ref, ref, sem).wait()

    def x_peer(dx):
        return yh * NX + lax.rem(x + dx, NX)

    def y_peer(dy):
        return lax.rem(yh + dy, NY) * NX + x

    def chunk_at(slot):
        return lax.rem(yh + order(slot), NY)

    def near_x(slot):
        block = kall.at[chunk_at(slot) * NX + x]
        for way in range(2):
            remote(
                block, block, kv_sent, near_got.at[slot, way], x_peer(1 + 2 * way)
            ).start()

    def far_x(slot):
        for way in range(2):
            block = chunk_at(slot) * NX + lax.rem(x + 3 - 2 * way, NX)
            wait_for(kall.at[block], near_got.at[slot, way])
            half = kall.at[block, way]
            remote(half, half, kv_sent, far_got.at[slot], x_peer(1 + 2 * way)).start()

    for dy in (2, 1, 3):
        remote(
            kall.at[resp], kall.at[resp], kv_sent, kvy_got.at[dy - 1], y_peer(dy)
        ).start()
    near_x(0)
    for load in loads[1:]:
        load.start()

    def forward(slot):
        dy = (0, 1, 3, 2)[slot]
        wait_for(kall.at[y_peer(dy)], kvy_got.at[(4 - dy) - 1])
        near_x(slot)

    for load in loads[6:]:
        load.wait()
    plen = plen_ref[0]
    rlen = rlen_ref[0, 0]

    gcol[...] = jnp.broadcast_to(qg_ref[...], (TILE, HD)).T
    loads[1].wait()
    loads[2].wait()
    for n in range(tiles):
        sl = pl.ds(n * TILE, TILE)
        xt = q_nat[sl, :].T.astype(F32)
        inv = lax.rsqrt(jnp.mean(xt * xt, axis=0, keepdims=True) + EPSILON)
        ut = xt * inv
        unit_qt[:, sl] = ut
        inv_q[:, sl] = jnp.broadcast_to(inv, (8, TILE))
        qt = (ut * gcol[...]).astype(BF)
        qnt[:, sl] = qt
        qn[sl, :] = qt.T

    forward(1)
    forward(2)
    far_x(0)

    loads[4].wait()
    loads[5].wait()
    for n in range(tiles):
        sl = pl.ds(n * TILE, TILE)
        lane = lax.broadcasted_iota(jnp.int32, (HD, TILE), 1) + n * TILE
        if n < tiles_r:
            keep = lane < rlen * 8
        else:
            keep = lane - rows_r < (plen - rows_p // 8 * resp) * 8
        dt[:, sl] = jnp.where(keep, d_nat[sl, :].T.astype(F32), 0.0)

    loads[3].wait()
    kf = kvr[0].astype(F32)
    inv_kr = lax.rsqrt(jnp.mean(kf * kf, axis=-1, keepdims=True) + EPSILON)
    ur = kf * inv_kr
    ukr[...] = ur
    kr = (ur * kg_ref[...]).astype(BF)
    knr[...] = kr
    knrt[...] = kr.T
    nkr = kr.shape[0]
    vt1[pl.ds(0, HD), pl.ds(0, nkr)] = kvr[1].T
    vt1[pl.ds(HD, 16), pl.ds(0, nkr)] = jnp.ones((16, nkr), BF)
    for n in range(tiles):
        sl = pl.ds(n * TILE, TILE)
        if n < tiles_r:
            s = dot(knr[...], qnt[:, sl])
            at = lax.broadcasted_iota(jnp.int32, s.shape, 0)
            lane = lax.broadcasted_iota(jnp.int32, s.shape, 1) + n * TILE
            e = jnp.where(at * 8 <= lane, jnp.exp2(s * exp_scale), 0.0).astype(BF)
            er_ref[:, sl] = e
            ol[:, sl] = dot(vt1[:, pl.ds(0, nkr)], e)
        else:
            ol[:, sl] = jnp.zeros((HD + 16, TILE), F32)

    forward(3)
    far_x(1)
    far_x(2)

    def pass1(step, carry):
        chunk = chunk_at(step)

        @pl.when(step == 1)
        def _():
            far_x(3)

        wait_for(kall.at[0], far_got.at[step])
        n_keys = NX * kall.shape[2]
        at = lax.broadcasted_iota(jnp.int32, (n_keys, HD), 0) + chunk * n_keys
        k_raw = kall[pl.ds(chunk * NX, NX), 0].reshape(n_keys, HD).astype(F32)
        inv = lax.rsqrt(jnp.mean(k_raw * k_raw, axis=-1, keepdims=True) + EPSILON)
        unit = k_raw * inv
        kf = unit * kg_ref[...]
        kn = kf.astype(BF)
        kn_ref[step] = kn
        knt_ref[step] = jnp.where(at < plen, kf, 0.0).astype(BF).T
        v = kall[pl.ds(chunk * NX, NX), 1].reshape(n_keys, HD).astype(F32)
        vt1[pl.ds(0, HD), :] = jnp.where(at < plen, v, 0.0).astype(BF).T
        lane = lax.broadcasted_iota(jnp.int32, (16, n_keys), 1) + chunk * n_keys
        vt1[pl.ds(HD, 16), :] = jnp.where(lane < plen, 1.0, 0.0).astype(BF)
        ahead_s = dot(kn, qnt[:, pl.ds(0, TILE)])
        for n in range(tiles):
            sl = pl.ds(n * TILE, TILE)
            s = ahead_s
            if n + 1 < tiles:
                ahead_s = dot(kn, qnt[:, pl.ds((n + 1) * TILE, TILE)])
            e = jnp.exp2(s * exp_scale)
            if n >= tiles_r:
                key = lax.broadcasted_iota(jnp.int32, s.shape, 0)
                lane = lax.broadcasted_iota(jnp.int32, s.shape, 1) + (n * TILE - rows_r)
                ahead = resp * (rows_p // 8) - chunk * n_keys
                e = jnp.where((key - ahead) * 8 <= lane, e, 0.0)
            e = e.astype(BF)
            e_ref[step, :, sl] = e
            ol[:, sl] += dot(vt1[...], e)
        return carry

    lax.fori_loop(0, NY, pass1, 0)

    for n in range(tiles):
        sl = pl.ds(n * TILE, TILE)
        rl = 1.0 / ol[pl.ds(HD, 1), sl]
        ds = (dt[:, sl] * rl).astype(BF)
        dst[:, sl] = ds
        delta = rl * jnp.sum(ds.astype(F32) * ol[pl.ds(0, HD), sl], axis=0, keepdims=True)
        delta_ref[:, sl] = jnp.broadcast_to(delta, (8, TILE))
    kterm[...] = jnp.zeros((8, HD), F32)

    def summed(slot, which):
        total = own[slot, which]
        for k in range(NX - 1):
            total = total + rx[slot, k, which].astype(F32)
        return total

    def along_y(slot):
        dy = (0, 1, 3, 2)[slot]
        wait_for(rx.at[slot], rx_got.at[slot])
        for which in range(2):
            ys[slot, which] = summed(slot, which).astype(BF)
        remote(ys.at[slot], ry.at[dy - 1], ry_sent, ry_got, y_peer(dy)).start()

    span = kall.shape[2]

    def value_sums(step):
        n_keys = NX * span
        at = lax.broadcasted_iota(jnp.int32, (n_keys, HD), 0) + chunk_at(step) * n_keys
        gv = dot(e_ref[step], dst[...], NT)
        vsum[...] = jnp.where(at < plen, gv, 0.0)
        for k in range(NX):
            part[step, k, 0] = sums[step, pl.ds(k * span, span), :].astype(BF)
            part[step, k, 1] = vsum[pl.ds(k * span, span), :].astype(BF)
        own[step, 0] = sums[step, pl.ds(x * span, span), :]
        own[step, 1] = vsum[pl.ds(x * span, span), :]
        for dx in (2, 1, 3):
            remote(
                part.at[step, lax.rem(x + dx, NX)],
                rx.at[step, dx - 1],
                rx_sent,
                rx_got.at[step],
                x_peer(dx),
            ).start()

    def pass2(back, carry):
        step = NY - 1 - back
        chunk = chunk_at(step)
        n_keys = NX * span
        v = kall[pl.ds(chunk * NX, NX), 1].reshape(n_keys, HD)
        gk = jnp.zeros((n_keys, HD), F32)
        ahead_dp = dot(v, dst[:, pl.ds(0, TILE)])
        for n in range(tiles):
            sl = pl.ds(n * TILE, TILE)
            dp = ahead_dp
            if n + 1 < tiles:
                ahead_dp = dot(v, dst[:, pl.ds((n + 1) * TILE, TILE)])
            e = e_ref[step, :, sl].astype(F32)
            gs = (e * (dp - delta_ref[pl.ds(0, 1), sl])).astype(BF)
            gs_ref[step, :, sl] = gs
            gk += dot(gs, qn[sl, :])
        at = lax.broadcasted_iota(jnp.int32, (n_keys, HD), 0) + chunk * n_keys
        gk = jnp.where(at < plen, gk * scale, 0.0)
        kn = kn_ref[step].astype(F32)
        kterm[...] += jnp.sum((gk * kn).reshape(n_keys // 8, 8, HD), axis=0)
        sums[step] = gk

        @pl.when(back == 0)
        def _():
            value_sums(step)

        return carry

    lax.fori_loop(0, NY, pass2, 0)

    gkr = jnp.zeros((nkr, HD), F32)
    for n in range(tiles_r):
        sl = pl.ds(n * TILE, TILE)
        dp = dot(kvr[1], dst[:, sl])
        e = er_ref[:, sl].astype(F32)
        gs = (e * (dp - delta_ref[pl.ds(0, 1), sl])).astype(BF)
        gsr_ref[:, sl] = gs
        gkr += dot(gs, qn[sl, :])
    gkr = gkr * scale
    kn = knr[...].astype(F32)
    kterm[...] += jnp.sum((gkr * kn).reshape(nkr // 8, 8, HD), axis=0)

    stores = [
        pltpu.make_async_copy(dkvr_v, dkvr_out, out_sem.at[0]),
        pltpu.make_async_copy(dq_v.at[pl.ds(0, rows_r)], dqr_out, out_sem.at[1]),
        pltpu.make_async_copy(dq_v.at[pl.ds(rows_r, rows_p)], dqp_out, out_sem.at[2]),
        pltpu.make_async_copy(dkvp_v, dkvp_out, out_sem.at[3]),
        pltpu.make_async_copy(gsend.at[3, pl.ds(0, 2)], gains_out, out_sem.at[4]),
    ]
    term = jnp.sum(kterm[...], axis=0, keepdims=True)
    qterm = term / qg_ref[...]
    key_sum = term / kg_ref[...]
    which_row = lax.broadcasted_iota(jnp.int32, (8, HD), 0)
    gsend[0] = jnp.where(
        which_row == 0,
        jnp.broadcast_to(qterm, (8, HD)),
        jnp.where(which_row == 1, jnp.broadcast_to(key_sum, (8, HD)), 0.0),
    )

    def g_start(stage):
        for k in FARTHEST_FIRST:
            pltpu.make_async_remote_copy(
                src_ref=gsend.at[stage],
                dst_ref=grecv.at[stage, stage_at[stage]],
                send_sem=g_sent,
                recv_sem=g_got.at[stage],
                device_id=partner(stage, k),
                device_id_type=MESH,
            ).start()
        grecv[stage, stage_at[stage]] = gsend[stage]

    def g_finish(stage):
        wait_for(grecv.at[stage, pl.ds(0, 7)], g_got.at[stage])
        total = grecv[stage, 0]
        for k in range(1, 8):
            total = total + grecv[stage, k]
        gsend[stage + 1] = total

    g_start(0)

    def pass3(back, carry):
        value_sums(NY - 1 - back)
        return carry

    lax.fori_loop(1, NY, pass3, 0)
    along_y(3)

    gvr = dot(er_ref[...], dst[:, pl.ds(0, rows_r)], NT)
    ur = ukr[...]
    kf = kvr[0].astype(F32)
    inv = lax.rsqrt(jnp.mean(kf * kf, axis=-1, keepdims=True) + EPSILON)
    gu = gkr * kg_ref[...]
    dk = inv * (gu - ur * jnp.mean(gu * ur, axis=-1, keepdims=True))
    dkvr_v[0] = dk.astype(BF)
    dkvr_v[1] = gvr.astype(BF)
    stores[0].start()


    for n in range(tiles):
        sl = pl.ds(n * TILE, TILE)
        gq = dot(knt_ref[0], gs_ref[0, :, sl])
        for slot in range(1, NY):
            gq += dot(knt_ref[slot], gs_ref[slot, :, sl])
        if n < tiles_r:
            gq += dot(knrt[...], gsr_ref[:, sl])
        ut = unit_qt[:, sl]
        gu = gq * scale * gcol[...]
        back = inv_q[pl.ds(0, 1), sl] * (gu - ut * jnp.mean(gu * ut, axis=0, keepdims=True))
        dq_v[sl, :] = back.astype(BF).T
    stores[1].start()
    stores[2].start()

    along_y(2)
    g_finish(0)
    g_start(1)
    along_y(1)
    wait_for(rx.at[0], rx_got.at[0])
    totals = [summed(0, which) for which in range(2)]
    kf = kall[resp, 0].astype(F32)
    inv = lax.rsqrt(jnp.mean(kf * kf, axis=-1, keepdims=True) + EPSILON)
    unit = kf * inv
    wait_for(kall.at[pl.ds(0, 15)], kv_sent)
    wait_for(rx, rx_sent)

    g_finish(1)
    g_start(2)

    wait_for(ry, ry_got)
    for which in range(2):
        for k in range(NY - 1):
            totals[which] = totals[which] + ry[k, which].astype(F32)
    gu = totals[0] * kg_ref[...]
    dk = inv * (gu - unit * jnp.mean(gu * unit, axis=-1, keepdims=True))
    dkvp_v[0] = dk.astype(BF)
    dkvp_v[1] = totals[1].astype(BF)
    stores[3].start()
    wait_for(ry, ry_sent)

    g_finish(2)
    stores[4].start()
    wait_for(grecv.at[:, pl.ds(0, 7)], g_sent)
    for store in stores:
        store.wait()


def hand_out(*refs):
    ins, outs, held = refs[:5], refs[5:10], refs[10:15]
    in_sem, out_sem = refs[15:]
    loads = [pltpu.make_async_copy(ins[n], held[n], in_sem.at[n]) for n in range(5)]
    stores = [pltpu.make_async_copy(held[n], outs[n], out_sem.at[n]) for n in range(5)]
    for load in loads:
        load.start()
    for load, store in zip(loads, stores):
        load.wait()
        store.start()
    for store in stores:
        store.wait()


def shards(
    q_prompt,
    q_resp,
    kv_prompt,
    kv_resp,
    dout_prompt,
    dout_resp,
    q_gain,
    k_gain,
    resp_len,
    prompt_len,
):
    span = q_prompt.shape[1]
    length = q_resp.shape[2]
    rows_r = length * 8
    rows_p = span * 8
    rows = rows_r + rows_p
    n_keys = NX * span
    any_spec = pl.BlockSpec(memory_space=pl.ANY)
    hbm = pl.BlockSpec(memory_space=pltpu.HBM)
    dma = pltpu.SemaphoreType.DMA
    out = pl.pallas_call(
        kernel,
        out_shape=(
            jax.ShapeDtypeStruct((rows_r, HD), BF),
            jax.ShapeDtypeStruct((rows_p, HD), BF),
            jax.ShapeDtypeStruct((2, span, HD), BF),
            jax.ShapeDtypeStruct((2, length, HD), BF),
            jax.ShapeDtypeStruct((2, HD), F32),
        ),
        in_specs=[hbm] * 10,
        out_specs=[any_spec] * 5,
        scratch_shapes=[
            pltpu.VMEM((1, HD), F32),
            pltpu.VMEM((1, HD), F32),
            pltpu.SMEM((1, 1), jnp.int32),
            pltpu.SMEM((1,), jnp.int32),
            pltpu.VMEM((rows, HD), BF),
            pltpu.VMEM((rows, HD), BF),
            pltpu.VMEM((2, length, HD), BF),
            pltpu.VMEM((NX * NY, 2, span, HD), BF),
            pltpu.VMEM((HD, rows), F32),
            pltpu.VMEM((8, rows), F32),
            pltpu.VMEM((HD, rows), BF),
            pltpu.VMEM((rows, HD), BF),
            pltpu.VMEM((HD, rows), F32),
            pltpu.VMEM((HD, rows), BF),
            pltpu.VMEM((8, rows), F32),
            pltpu.VMEM((HD, TILE), F32),
            pltpu.VMEM((NY, n_keys, HD), BF),
            pltpu.VMEM((NY, HD, n_keys), BF),
            pltpu.VMEM((HD + 16, n_keys), BF),
            pltpu.VMEM((length, HD), BF),
            pltpu.VMEM((HD, length), BF),
            pltpu.VMEM((length, HD), F32),
            pltpu.VMEM((NY, n_keys, rows), BF),
            pltpu.VMEM((length, rows_r), BF),
            pltpu.VMEM((NY, n_keys, rows), BF),
            pltpu.VMEM((length, rows_r), BF),
            pltpu.VMEM((HD + 16, rows), F32),
            pltpu.VMEM((NY, n_keys, HD), F32),
            pltpu.VMEM((n_keys, HD), F32),
            pltpu.VMEM((NY, NX, 2, span, HD), BF),
            pltpu.VMEM((NY, NX - 1, 2, span, HD), BF),
            pltpu.VMEM((NY, 2, span, HD), F32),
            pltpu.VMEM((NY, 2, span, HD), BF),
            pltpu.VMEM((NY - 1, 2, span, HD), BF),
            pltpu.VMEM((8, HD), F32),
            pltpu.VMEM((4, 8, HD), F32),
            pltpu.VMEM((3, 8, 8, HD), F32),
            pltpu.VMEM((rows, HD), BF),
            pltpu.VMEM((2, span, HD), BF),
            pltpu.VMEM((2, length, HD), BF),
            dma((10,)),
            dma((5,)),
            dma((NY, 2)),
            dma((NY,)),
            dma((NY - 1,)),
            dma,
            dma((NY,)),
            dma,
            dma,
            dma,
            dma((3,)),
            dma,
        ],
        compiler_params=pltpu.CompilerParams(
            collective_id=0, has_side_effects=True, vmem_limit_bytes=62 * 2**20
        ),
        name="attention_grads",
    )(
        q_resp.reshape(rows_r, HD),
        q_prompt.reshape(rows_p, HD),
        kv_prompt.reshape(2, span, HD),
        kv_resp.reshape(2, length, HD),
        dout_resp.reshape(rows_r, HD),
        dout_prompt.reshape(rows_p, HD),
        q_gain.reshape(1, HD),
        k_gain.reshape(1, HD),
        resp_len,
        prompt_len,
    )
    out = pl.pallas_call(
        hand_out,
        out_shape=tuple(jax.ShapeDtypeStruct(a.shape, a.dtype) for a in out),
        in_specs=[any_spec] * 5,
        out_specs=[any_spec] * 5,
        scratch_shapes=[pltpu.VMEM(a.shape, a.dtype) for a in out] + [dma((5,))] * 2,
        name="hand_out",
    )(*out)
    return (
        out[1].reshape(q_prompt.shape),
        out[0].reshape(q_resp.shape),
        out[2].reshape(kv_prompt.shape),
        out[3].reshape(kv_resp.shape),
        out[4],
    )


def solution(mesh):
    return jax.shard_map(
        shards,
        mesh=mesh,
        in_specs=(
            P("grp", "resp", "head", None),
            P("grp", "resp", None, "head", None),
            P("grp", None, "resp", "head", None),
            P("grp", "resp", None, None, "head", None),
            P("grp", "resp", "head", None),
            P("grp", "resp", None, "head", None),
            P(),
            P(),
            P("grp", "resp"),
            P("grp"),
        ),
        out_specs=(
            P("grp", "resp", "head", None),
            P("grp", "resp", None, "head", None),
            P("grp", None, "resp", "head", None),
            P("grp", "resp", None, None, "head", None),
            P(),
        ),
        check_vma=False,
    )
```

```python
import functools
import math

import jax
import jax.numpy as jnp
from jax import lax
from jax.experimental import pallas as pl
from jax.experimental.pallas import tpu as pltpu
from jax.sharding import PartitionSpec as P

EPSILON = 1e-06
MESH = pl.DeviceIdType.MESH
HD = 128
BF = jnp.bfloat16
F32 = jnp.float32
NX = 4
NY = 4
TILE = 512
FARTHEST_FIRST = (4, 3, 5, 2, 6, 1, 7)
NT = (((1,), (1,)), ((), ()))
NN = (((1,), (0,)), ((), ()))


def dot(lhs, rhs, dims=NN):
    return lax.dot_general(lhs, rhs, dims, preferred_element_type=F32)


def order(step):
    return step + step // 2 - 2 * (step // 3)


def kernel(
    qr_in,
    qp_in,
    kvp_in,
    kvr_in,
    dr_in,
    dp_in,
    qg_in,
    kg_in,
    rlen_in,
    plen_in,
    dqr_out,
    dqp_out,
    dkvp_out,
    dkvr_out,
    gains_out,
    qg_ref,
    kg_ref,
    rlen_ref,
    plen_ref,
    q_nat,
    d_nat,
    kvr,
    kall,
    unit_qt,
    inv_q,
    qnt,
    qn,
    dt,
    dst,
    delta_ref,
    rl_ref,
    dp_ref,
    dpr_ref,
    gcol,
    kn_ref,
    knt_ref,
    vt1,
    knr,
    knrt,
    ukr,
    e_ref,
    er_ref,
    gs_ref,
    gsr_ref,
    ol,
    sums,
    vsum,
    part,
    rx,
    own,
    ys,
    ry,
    kterm,
    gsend,
    grecv,
    dq_v,
    dkvp_v,
    dkvr_v,
    in_sem,
    out_sem,
    kvx_got,
    kvy_got,
    kv_sent,
    rx_got,
    rx_sent,
    ry_got,
    ry_sent,
    g_got,
    g_sent,
):
    resp = lax.axis_index("resp")
    head = lax.axis_index("head")
    grp = lax.axis_index("grp")
    yh = resp // NX
    x = lax.rem(resp, NX)
    yl = head // 2
    core = lax.rem(head, 2)
    ngrp = 8
    y8 = 2 * yh + yl
    rows_r = qr_in.shape[0]
    rows_p = qp_in.shape[0]
    rows = rows_r + rows_p
    tiles = rows // TILE
    tiles_r = rows_r // TILE
    scale = HD**-0.5
    exp_scale = scale * math.log2(math.e)

    def partner(stage, k):
        if stage == 0:
            return {"grp": lax.rem(grp + k, ngrp)}
        if stage == 1:
            to = lax.rem(y8 + k, 8)
            return {"resp": (to // 2) * NX + x, "head": lax.rem(to, 2) * 2 + core}
        to = lax.rem(2 * x + core + k, 8)
        return {"resp": yh * NX + to // 2, "head": yl * 2 + lax.rem(to, 2)}

    stage_at = (grp, y8, 2 * x + core)

    loads = [
        pltpu.make_async_copy(kvp_in, kall.at[resp], in_sem.at[0]),
        pltpu.make_async_copy(qr_in, q_nat.at[pl.ds(0, rows_r)], in_sem.at[1]),
        pltpu.make_async_copy(qp_in, q_nat.at[pl.ds(rows_r, rows_p)], in_sem.at[2]),
        pltpu.make_async_copy(kvr_in, kvr, in_sem.at[3]),
        pltpu.make_async_copy(dr_in, d_nat.at[pl.ds(0, rows_r)], in_sem.at[4]),
        pltpu.make_async_copy(dp_in, d_nat.at[pl.ds(rows_r, rows_p)], in_sem.at[5]),
        pltpu.make_async_copy(qg_in, qg_ref, in_sem.at[6]),
        pltpu.make_async_copy(kg_in, kg_ref, in_sem.at[7]),
        pltpu.make_async_copy(rlen_in, rlen_ref, in_sem.at[8]),
        pltpu.make_async_copy(plen_in, plen_ref, in_sem.at[9]),
    ]
    loads[0].start()
    barrier = pltpu.get_barrier_semaphore()
    for k in FARTHEST_FIRST:
        for stage in range(3):
            pl.semaphore_signal(
                barrier, inc=1, device_id=partner(stage, k), device_id_type=MESH
            )

    loads[1].start()
    loads[2].start()
    loads[0].wait()
    pl.semaphore_wait(barrier, 21)

    def remote(src, dst, sent, got, to):
        return pltpu.make_async_remote_copy(
            src_ref=src,
            dst_ref=dst,
            send_sem=sent,
            recv_sem=got,
            device_id={"resp": to},
            device_id_type=MESH,
        )

    def wait_for(ref, sem):
        pltpu.make_async_copy(ref, ref, sem).wait()

    def x_peer(dx):
        return yh * NX + lax.rem(x + dx, NX)

    def y_peer(dy):
        return lax.rem(yh + dy, NY) * NX + x

    def chunk_at(slot):
        return lax.rem(yh + order(slot), NY)

    def along_x(slot):
        block = kall.at[chunk_at(slot) * NX + x]
        for dx in (2, 1, 3):
            remote(block, block, kv_sent, kvx_got.at[slot], x_peer(dx)).start()

    for dy in (2, 1, 3):
        remote(
            kall.at[resp], kall.at[resp], kv_sent, kvy_got.at[dy - 1], y_peer(dy)
        ).start()
    along_x(0)
    for load in loads[3:]:
        load.start()

    def forward(slot):
        dy = (0, 1, 3, 2)[slot]
        wait_for(kall.at[y_peer(dy)], kvy_got.at[(4 - dy) - 1])
        along_x(slot)

    for load in loads[6:]:
        load.wait()
    plen = plen_ref[0]
    rlen = rlen_ref[0, 0]

    gcol[...] = jnp.broadcast_to(qg_ref[...], (TILE, HD)).T
    loads[1].wait()
    loads[2].wait()
    for n in range(tiles):
        sl = pl.ds(n * TILE, TILE)
        xt = q_nat[sl, :].T.astype(F32)
        inv = lax.rsqrt(jnp.mean(xt * xt, axis=0, keepdims=True) + EPSILON)
        ut = xt * inv
        unit_qt[:, sl] = ut
        inv_q[:, sl] = jnp.broadcast_to(inv, (8, TILE))
        qt = (ut * gcol[...]).astype(BF)
        qnt[:, sl] = qt
        qn[sl, :] = qt.T

    forward(1)
    forward(2)

    loads[4].wait()
    loads[5].wait()
    for n in range(tiles):
        sl = pl.ds(n * TILE, TILE)
        lane = lax.broadcasted_iota(jnp.int32, (HD, TILE), 1) + n * TILE
        if n < tiles_r:
            keep = lane < rlen * 8
        else:
            keep = lane - rows_r < (plen - rows_p // 8 * resp) * 8
        dt[:, sl] = jnp.where(keep, d_nat[sl, :].T.astype(F32), 0.0).astype(BF)

    forward(3)

    loads[3].wait()
    kf = kvr[0].astype(F32)
    inv_kr = lax.rsqrt(jnp.mean(kf * kf, axis=-1, keepdims=True) + EPSILON)
    ur = kf * inv_kr
    ukr[...] = ur
    kr = (ur * kg_ref[...]).astype(BF)
    knr[...] = kr
    knrt[...] = kr.T
    nkr = kr.shape[0]
    vt1[pl.ds(0, HD), pl.ds(0, nkr)] = kvr[1].T
    vt1[pl.ds(HD, 16), pl.ds(0, nkr)] = jnp.ones((16, nkr), BF)
    for n in range(tiles):
        sl = pl.ds(n * TILE, TILE)
        if n < tiles_r:
            s = dot(knr[...], qnt[:, sl])
            at = lax.broadcasted_iota(jnp.int32, s.shape, 0)
            lane = lax.broadcasted_iota(jnp.int32, s.shape, 1) + n * TILE
            e = jnp.where(at * 8 <= lane, jnp.exp2(s * exp_scale), 0.0).astype(BF)
            er_ref[:, sl] = e
            dpr_ref[:, sl] = dot(kvr[1], dt[:, sl])
            ol[:, sl] = dot(vt1[:, pl.ds(0, nkr)], e)
        else:
            ol[:, sl] = jnp.zeros((HD + 16, TILE), F32)

    def pass1(step, carry):
        chunk = chunk_at(step)
        wait_for(kall.at[pl.ds(0, NX - 1)], kvx_got.at[step])
        n_keys = NX * kall.shape[2]
        at = lax.broadcasted_iota(jnp.int32, (n_keys, HD), 0) + chunk * n_keys
        k_raw = kall[pl.ds(chunk * NX, NX), 0].reshape(n_keys, HD).astype(F32)
        inv = lax.rsqrt(jnp.mean(k_raw * k_raw, axis=-1, keepdims=True) + EPSILON)
        unit = k_raw * inv
        kf = unit * kg_ref[...]
        kn = kf.astype(BF)
        kn_ref[step] = kn
        knt_ref[step] = jnp.where(at < plen, kf, 0.0).astype(BF).T
        v = kall[pl.ds(chunk * NX, NX), 1].reshape(n_keys, HD)
        vt1[pl.ds(0, HD), :] = jnp.where(at < plen, v.astype(F32), 0.0).astype(BF).T
        lane = lax.broadcasted_iota(jnp.int32, (16, n_keys), 1) + chunk * n_keys
        vt1[pl.ds(HD, 16), :] = jnp.where(lane < plen, 1.0, 0.0).astype(BF)
        ahead_s = dot(kn, qnt[:, pl.ds(0, TILE)])
        for n in range(tiles):
            sl = pl.ds(n * TILE, TILE)
            s = ahead_s
            if n + 1 < tiles:
                ahead_s = dot(kn, qnt[:, pl.ds((n + 1) * TILE, TILE)])
            e = jnp.exp2(s * exp_scale)
            if n >= tiles_r:
                key = lax.broadcasted_iota(jnp.int32, s.shape, 0)
                lane = lax.broadcasted_iota(jnp.int32, s.shape, 1) + (n * TILE - rows_r)
                ahead = resp * (rows_p // 8) - chunk * n_keys
                e = jnp.where((key - ahead) * 8 <= lane, e, 0.0)
            e = e.astype(BF)
            e_ref[step, :, sl] = e
            dp_ref[step, :, sl] = dot(v, dt[:, sl])
            ol[:, sl] += dot(vt1[...], e)
        return carry

    lax.fori_loop(0, NY, pass1, 0)

    for n in range(tiles):
        sl = pl.ds(n * TILE, TILE)
        rl = 1.0 / ol[pl.ds(HD, 1), sl]
        d = dt[:, sl].astype(F32)
        dst[:, sl] = (d * rl).astype(BF)
        delta = rl * jnp.sum(d * ol[pl.ds(0, HD), sl], axis=0, keepdims=True)
        delta_ref[:, sl] = jnp.broadcast_to(delta, (8, TILE))
        rl_ref[:, sl] = jnp.broadcast_to(rl, (8, TILE))
    kterm[...] = jnp.zeros((8, HD), F32)

    def summed(slot, which):
        total = own[slot, which]
        for k in range(NX - 1):
            total = total + rx[slot, k, which].astype(F32)
        return total

    def along_y(slot):
        dy = (0, 1, 3, 2)[slot]
        wait_for(rx.at[slot], rx_got.at[slot])
        for which in range(2):
            ys[slot, which] = summed(slot, which).astype(BF)
        remote(ys.at[slot], ry.at[dy - 1], ry_sent, ry_got, y_peer(dy)).start()

    span = kall.shape[2]

    def pass2(back, carry):
        step = NY - 1 - back
        chunk = chunk_at(step)
        n_keys = NX * span
        gk = jnp.zeros((n_keys, HD), F32)
        for n in range(tiles):
            sl = pl.ds(n * TILE, TILE)
            weights = e_ref[step, :, sl].astype(F32) * rl_ref[pl.ds(0, 1), sl]
            dp = dp_ref[step, :, sl]
            gs = (weights * (dp - delta_ref[pl.ds(0, 1), sl])).astype(BF)
            gs_ref[step, :, sl] = gs
            gk += dot(gs, qn[sl, :])
        at = lax.broadcasted_iota(jnp.int32, (n_keys, HD), 0) + chunk * n_keys
        gk = jnp.where(at < plen, gk * scale, 0.0)
        kn = kn_ref[step].astype(F32)
        kterm[...] += jnp.sum((gk * kn).reshape(n_keys // 8, 8, HD), axis=0)
        sums[step] = gk
        return carry

    lax.fori_loop(0, NY, pass2, 0)

    gkr = jnp.zeros((nkr, HD), F32)
    for n in range(tiles_r):
        sl = pl.ds(n * TILE, TILE)
        weights = er_ref[:, sl].astype(F32) * rl_ref[pl.ds(0, 1), sl]
        gs = (weights * (dpr_ref[:, sl] - delta_ref[pl.ds(0, 1), sl])).astype(BF)
        gsr_ref[:, sl] = gs
        gkr += dot(gs, qn[sl, :])
    gkr = gkr * scale
    kn = knr[...].astype(F32)
    kterm[...] += jnp.sum((gkr * kn).reshape(nkr // 8, 8, HD), axis=0)

    stores = [
        pltpu.make_async_copy(dkvr_v, dkvr_out, out_sem.at[0]),
        pltpu.make_async_copy(dq_v.at[pl.ds(0, rows_r)], dqr_out, out_sem.at[1]),
        pltpu.make_async_copy(dq_v.at[pl.ds(rows_r, rows_p)], dqp_out, out_sem.at[2]),
        pltpu.make_async_copy(dkvp_v, dkvp_out, out_sem.at[3]),
        pltpu.make_async_copy(gsend.at[3, pl.ds(0, 2)], gains_out, out_sem.at[4]),
    ]
    term = jnp.sum(kterm[...], axis=0, keepdims=True)
    qterm = term / qg_ref[...]
    key_sum = term / kg_ref[...]
    which_row = lax.broadcasted_iota(jnp.int32, (8, HD), 0)
    gsend[0] = jnp.where(
        which_row == 0,
        jnp.broadcast_to(qterm, (8, HD)),
        jnp.where(which_row == 1, jnp.broadcast_to(key_sum, (8, HD)), 0.0),
    )

    def g_start(stage):
        for k in FARTHEST_FIRST:
            pltpu.make_async_remote_copy(
                src_ref=gsend.at[stage],
                dst_ref=grecv.at[stage, stage_at[stage]],
                send_sem=g_sent,
                recv_sem=g_got.at[stage],
                device_id=partner(stage, k),
                device_id_type=MESH,
            ).start()
        grecv[stage, stage_at[stage]] = gsend[stage]

    def g_finish(stage):
        wait_for(grecv.at[stage, pl.ds(0, 7)], g_got.at[stage])
        total = grecv[stage, 0]
        for k in range(1, 8):
            total = total + grecv[stage, k]
        gsend[stage + 1] = total

    g_start(0)

    def pass3(back, carry):
        step = NY - 1 - back
        n_keys = NX * span
        at = lax.broadcasted_iota(jnp.int32, (n_keys, HD), 0) + chunk_at(step) * n_keys
        gv = dot(e_ref[step], dst[...], NT)
        vsum[...] = jnp.where(at < plen, gv, 0.0)
        for k in range(NX):
            part[step, k, 0] = sums[step, pl.ds(k * span, span), :].astype(BF)
            part[step, k, 1] = vsum[pl.ds(k * span, span), :].astype(BF)
        own[step, 0] = sums[step, pl.ds(x * span, span), :]
        own[step, 1] = vsum[pl.ds(x * span, span), :]
        for dx in (2, 1, 3):
            remote(
                part.at[step, lax.rem(x + dx, NX)],
                rx.at[step, dx - 1],
                rx_sent,
                rx_got.at[step],
                x_peer(dx),
            ).start()
        return carry

    lax.fori_loop(0, NY, pass3, 0)

    gvr = dot(er_ref[...], dst[:, pl.ds(0, rows_r)], NT)
    ur = ukr[...]
    kf = kvr[0].astype(F32)
    inv = lax.rsqrt(jnp.mean(kf * kf, axis=-1, keepdims=True) + EPSILON)
    gu = gkr * kg_ref[...]
    dk = inv * (gu - ur * jnp.mean(gu * ur, axis=-1, keepdims=True))
    dkvr_v[0] = dk.astype(BF)
    dkvr_v[1] = gvr.astype(BF)
    stores[0].start()


    for n in range(tiles):
        sl = pl.ds(n * TILE, TILE)
        gq = dot(knt_ref[0], gs_ref[0, :, sl])
        for slot in range(1, NY):
            gq += dot(knt_ref[slot], gs_ref[slot, :, sl])
        if n < tiles_r:
            gq += dot(knrt[...], gsr_ref[:, sl])
        ut = unit_qt[:, sl]
        gu = gq * scale * gcol[...]
        back = inv_q[pl.ds(0, 1), sl] * (gu - ut * jnp.mean(gu * ut, axis=0, keepdims=True))
        dq_v[sl, :] = back.astype(BF).T
        if n < 2:
            along_y(3 - n)
    stores[1].start()
    stores[2].start()

    g_finish(0)
    g_start(1)
    along_y(1)
    wait_for(rx.at[0], rx_got.at[0])
    totals = [summed(0, which) for which in range(2)]
    kf = kall[resp, 0].astype(F32)
    inv = lax.rsqrt(jnp.mean(kf * kf, axis=-1, keepdims=True) + EPSILON)
    unit = kf * inv
    wait_for(kall.at[pl.ds(0, 15)], kv_sent)
    wait_for(rx, rx_sent)

    g_finish(1)
    g_start(2)

    wait_for(ry, ry_got)
    for which in range(2):
        for k in range(NY - 1):
            totals[which] = totals[which] + ry[k, which].astype(F32)
    gu = totals[0] * kg_ref[...]
    dk = inv * (gu - unit * jnp.mean(gu * unit, axis=-1, keepdims=True))
    dkvp_v[0] = dk.astype(BF)
    dkvp_v[1] = totals[1].astype(BF)
    stores[3].start()
    wait_for(ry, ry_sent)

    g_finish(2)
    stores[4].start()
    wait_for(grecv.at[:, pl.ds(0, 7)], g_sent)
    for store in stores:
        store.wait()


def hand_out(*refs):
    ins, outs, held = refs[:5], refs[5:10], refs[10:15]
    in_sem, out_sem = refs[15:]
    loads = [pltpu.make_async_copy(ins[n], held[n], in_sem.at[n]) for n in range(5)]
    stores = [pltpu.make_async_copy(held[n], outs[n], out_sem.at[n]) for n in range(5)]
    for load in loads:
        load.start()
    for load, store in zip(loads, stores):
        load.wait()
        store.start()
    for store in stores:
        store.wait()


def shards(
    q_prompt,
    q_resp,
    kv_prompt,
    kv_resp,
    dout_prompt,
    dout_resp,
    q_gain,
    k_gain,
    resp_len,
    prompt_len,
):
    span = q_prompt.shape[1]
    length = q_resp.shape[2]
    rows_r = length * 8
    rows_p = span * 8
    rows = rows_r + rows_p
    n_keys = NX * span
    any_spec = pl.BlockSpec(memory_space=pl.ANY)
    hbm = pl.BlockSpec(memory_space=pltpu.HBM)
    dma = pltpu.SemaphoreType.DMA
    out = pl.pallas_call(
        kernel,
        out_shape=(
            jax.ShapeDtypeStruct((rows_r, HD), BF),
            jax.ShapeDtypeStruct((rows_p, HD), BF),
            jax.ShapeDtypeStruct((2, span, HD), BF),
            jax.ShapeDtypeStruct((2, length, HD), BF),
            jax.ShapeDtypeStruct((2, HD), F32),
        ),
        in_specs=[hbm] * 10,
        out_specs=[any_spec] * 5,
        scratch_shapes=[
            pltpu.VMEM((1, HD), F32),
            pltpu.VMEM((1, HD), F32),
            pltpu.SMEM((1, 1), jnp.int32),
            pltpu.SMEM((1,), jnp.int32),
            pltpu.VMEM((rows, HD), BF),
            pltpu.VMEM((rows, HD), BF),
            pltpu.VMEM((2, length, HD), BF),
            pltpu.VMEM((NX * NY, 2, span, HD), BF),
            pltpu.VMEM((HD, rows), F32),
            pltpu.VMEM((8, rows), F32),
            pltpu.VMEM((HD, rows), BF),
            pltpu.VMEM((rows, HD), BF),
            pltpu.VMEM((HD, rows), BF),
            pltpu.VMEM((HD, rows), BF),
            pltpu.VMEM((8, rows), F32),
            pltpu.VMEM((8, rows), F32),
            pltpu.VMEM((NY, n_keys, rows), F32),
            pltpu.VMEM((length, rows_r), F32),
            pltpu.VMEM((HD, TILE), F32),
            pltpu.VMEM((NY, n_keys, HD), BF),
            pltpu.VMEM((NY, HD, n_keys), BF),
            pltpu.VMEM((HD + 16, n_keys), BF),
            pltpu.VMEM((length, HD), BF),
            pltpu.VMEM((HD, length), BF),
            pltpu.VMEM((length, HD), F32),
            pltpu.VMEM((NY, n_keys, rows), BF),
            pltpu.VMEM((length, rows_r), BF),
            pltpu.VMEM((NY, n_keys, rows), BF),
            pltpu.VMEM((length, rows_r), BF),
            pltpu.VMEM((HD + 16, rows), F32),
            pltpu.VMEM((NY, n_keys, HD), F32),
            pltpu.VMEM((n_keys, HD), F32),
            pltpu.VMEM((NY, NX, 2, span, HD), BF),
            pltpu.VMEM((NY, NX - 1, 2, span, HD), BF),
            pltpu.VMEM((NY, 2, span, HD), F32),
            pltpu.VMEM((NY, 2, span, HD), BF),
            pltpu.VMEM((NY - 1, 2, span, HD), BF),
            pltpu.VMEM((8, HD), F32),
            pltpu.VMEM((4, 8, HD), F32),
            pltpu.VMEM((3, 8, 8, HD), F32),
            pltpu.VMEM((rows, HD), BF),
            pltpu.VMEM((2, span, HD), BF),
            pltpu.VMEM((2, length, HD), BF),
            dma((10,)),
            dma((5,)),
            dma((NY,)),
            dma((NY - 1,)),
            dma,
            dma((NY,)),
            dma,
            dma,
            dma,
            dma((3,)),
            dma,
        ],
        compiler_params=pltpu.CompilerParams(
            collective_id=0, has_side_effects=True, vmem_limit_bytes=62 * 2**20
        ),
        name="attention_grads",
    )(
        q_resp.reshape(rows_r, HD),
        q_prompt.reshape(rows_p, HD),
        kv_prompt.reshape(2, span, HD),
        kv_resp.reshape(2, length, HD),
        dout_resp.reshape(rows_r, HD),
        dout_prompt.reshape(rows_p, HD),
        q_gain.reshape(1, HD),
        k_gain.reshape(1, HD),
        resp_len,
        prompt_len,
    )
    out = pl.pallas_call(
        hand_out,
        out_shape=tuple(jax.ShapeDtypeStruct(a.shape, a.dtype) for a in out),
        in_specs=[any_spec] * 5,
        out_specs=[any_spec] * 5,
        scratch_shapes=[pltpu.VMEM(a.shape, a.dtype) for a in out] + [dma((5,))] * 2,
        name="hand_out",
    )(*out)
    return (
        out[1].reshape(q_prompt.shape),
        out[0].reshape(q_resp.shape),
        out[2].reshape(kv_prompt.shape),
        out[3].reshape(kv_resp.shape),
        out[4],
    )


def solution(mesh):
    return jax.shard_map(
        shards,
        mesh=mesh,
        in_specs=(
            P("grp", "resp", "head", None),
            P("grp", "resp", None, "head", None),
            P("grp", None, "resp", "head", None),
            P("grp", "resp", None, None, "head", None),
            P("grp", "resp", "head", None),
            P("grp", "resp", None, "head", None),
            P(),
            P(),
            P("grp", "resp"),
            P("grp"),
        ),
        out_specs=(
            P("grp", "resp", "head", None),
            P("grp", "resp", None, "head", None),
            P("grp", None, "resp", "head", None),
            P("grp", "resp", None, None, "head", None),
            P(),
        ),
        check_vma=False,
    )
```

```python
import functools
import math

import jax
import jax.numpy as jnp
from jax import lax
from jax.experimental import pallas as pl
from jax.experimental.pallas import tpu as pltpu
from jax.sharding import PartitionSpec as P

EPSILON = 1e-06
MESH = pl.DeviceIdType.MESH
HD = 128
BF = jnp.bfloat16
F32 = jnp.float32
NX = 4
NY = 4
TILE = 512
FARTHEST_FIRST = (4, 3, 5, 2, 6, 1, 7)
NT = (((1,), (1,)), ((), ()))
NN = (((1,), (0,)), ((), ()))


def dot(lhs, rhs, dims=NN):
    return lax.dot_general(lhs, rhs, dims, preferred_element_type=F32)


def order(step):
    return step + step // 2 - 2 * (step // 3)


def kernel(
    qr_in,
    qp_in,
    kvp_in,
    kvr_in,
    dr_in,
    dp_in,
    qg_in,
    kg_in,
    rlen_in,
    plen_in,
    dqr_out,
    dqp_out,
    dkvp_out,
    dkvr_out,
    gains_out,
    qg_ref,
    kg_ref,
    rlen_ref,
    plen_ref,
    q_nat,
    d_nat,
    kvr,
    kall,
    unit_qt,
    inv_q,
    qnt,
    qn,
    dt,
    dst,
    delta_ref,
    gcol,
    kn_ref,
    knt_ref,
    vt1,
    knr,
    knrt,
    ukr,
    e_ref,
    er_ref,
    gs_ref,
    gsr_ref,
    ol,
    sums,
    vsum,
    part,
    rx,
    own,
    ys,
    ry,
    kterm,
    gsend,
    grecv,
    dq_v,
    dkvp_v,
    dkvr_v,
    in_sem,
    out_sem,
    kvx_got,
    kvy_got,
    kv_sent,
    rx_got,
    rx_sent,
    ry_got,
    ry_sent,
    g_got,
    g_sent,
    z_ready,
):
    resp = lax.axis_index("resp")
    head = lax.axis_index("head")
    grp = lax.axis_index("grp")
    yh = resp // NX
    x = lax.rem(resp, NX)
    yl = head // 2
    core = lax.rem(head, 2)
    ngrp = 8
    y8 = 2 * yh + yl
    rows_r = qr_in.shape[0]
    rows_p = qp_in.shape[0]
    rows = rows_r + rows_p
    tiles = rows // TILE
    tiles_r = rows_r // TILE
    scale = HD**-0.5
    exp_scale = scale * math.log2(math.e)

    def partner(stage, k):
        if stage == 0:
            return {"grp": lax.rem(grp + k, ngrp)}
        if stage == 1:
            to = lax.rem(y8 + k, 8)
            return {"resp": (to // 2) * NX + x, "head": lax.rem(to, 2) * 2 + core}
        to = lax.rem(2 * x + core + k, 8)
        return {"resp": yh * NX + to // 2, "head": yl * 2 + lax.rem(to, 2)}

    stage_at = (grp, y8, 2 * x + core)

    loads = [
        pltpu.make_async_copy(kvp_in, kall.at[resp], in_sem.at[0]),
        pltpu.make_async_copy(qr_in, q_nat.at[pl.ds(0, rows_r)], in_sem.at[1]),
        pltpu.make_async_copy(qp_in, q_nat.at[pl.ds(rows_r, rows_p)], in_sem.at[2]),
        pltpu.make_async_copy(kvr_in, kvr, in_sem.at[3]),
        pltpu.make_async_copy(dr_in, d_nat.at[pl.ds(0, rows_r)], in_sem.at[4]),
        pltpu.make_async_copy(dp_in, d_nat.at[pl.ds(rows_r, rows_p)], in_sem.at[5]),
        pltpu.make_async_copy(qg_in, qg_ref, in_sem.at[6]),
        pltpu.make_async_copy(kg_in, kg_ref, in_sem.at[7]),
        pltpu.make_async_copy(rlen_in, rlen_ref, in_sem.at[8]),
        pltpu.make_async_copy(plen_in, plen_ref, in_sem.at[9]),
    ]
    loads[0].start()
    barrier = pltpu.get_barrier_semaphore()
    for k in FARTHEST_FIRST:
        for stage in (1, 2):
            pl.semaphore_signal(
                barrier, inc=1, device_id=partner(stage, k), device_id_type=MESH
            )
    for k in range(7, 0, -1):

        @pl.when(grp + k < ngrp)
        def _(k=k):
            pl.semaphore_signal(
                barrier, inc=1, device_id={"grp": grp + k}, device_id_type=MESH
            )

    loads[0].wait()
    pl.semaphore_wait(barrier, 14 + grp)

    def remote(src, dst, sent, got, to):
        return pltpu.make_async_remote_copy(
            src_ref=src,
            dst_ref=dst,
            send_sem=sent,
            recv_sem=got,
            device_id={"resp": to},
            device_id_type=MESH,
        )

    def wait_for(ref, sem):
        pltpu.make_async_copy(ref, ref, sem).wait()

    def x_peer(dx):
        return yh * NX + lax.rem(x + dx, NX)

    def y_peer(dy):
        return lax.rem(yh + dy, NY) * NX + x

    def chunk_at(slot):
        return lax.rem(yh + order(slot), NY)

    def along_x(slot):
        block = kall.at[chunk_at(slot) * NX + x]
        for dx in (2, 1, 3):
            remote(block, block, kv_sent, kvx_got.at[slot], x_peer(dx)).start()

    for dy in (2, 1, 3):
        remote(
            kall.at[resp], kall.at[resp], kv_sent, kvy_got.at[dy - 1], y_peer(dy)
        ).start()
    along_x(0)
    for load in loads[1:]:
        load.start()

    def forward(slot):
        dy = (0, 1, 3, 2)[slot]
        wait_for(kall.at[y_peer(dy)], kvy_got.at[(4 - dy) - 1])
        along_x(slot)

    for load in loads[6:]:
        load.wait()
    plen = plen_ref[0]
    rlen = rlen_ref[0, 0]

    gcol[...] = jnp.broadcast_to(qg_ref[...], (TILE, HD)).T
    loads[1].wait()
    loads[2].wait()
    for n in range(tiles):
        sl = pl.ds(n * TILE, TILE)
        xt = q_nat[sl, :].T.astype(F32)
        inv = lax.rsqrt(jnp.mean(xt * xt, axis=0, keepdims=True) + EPSILON)
        ut = xt * inv
        unit_qt[:, sl] = ut
        inv_q[:, sl] = jnp.broadcast_to(inv, (8, TILE))
        qt = (ut * gcol[...]).astype(BF)
        qnt[:, sl] = qt
        qn[sl, :] = qt.T

    forward(1)
    forward(2)
    for k in range(7, 0, -1):

        @pl.when(grp >= k)
        def _(k=k):
            pl.semaphore_signal(
                z_ready, inc=1, device_id={"grp": grp - k}, device_id_type=MESH
            )


    loads[4].wait()
    loads[5].wait()
    for n in range(tiles):
        sl = pl.ds(n * TILE, TILE)
        lane = lax.broadcasted_iota(jnp.int32, (HD, TILE), 1) + n * TILE
        if n < tiles_r:
            keep = lane < rlen * 8
        else:
            keep = lane - rows_r < (plen - rows_p // 8 * resp) * 8
        dt[:, sl] = jnp.where(keep, d_nat[sl, :].T.astype(F32), 0.0)

    loads[3].wait()
    kf = kvr[0].astype(F32)
    inv_kr = lax.rsqrt(jnp.mean(kf * kf, axis=-1, keepdims=True) + EPSILON)
    ur = kf * inv_kr
    ukr[...] = ur
    kr = (ur * kg_ref[...]).astype(BF)
    knr[...] = kr
    knrt[...] = kr.T
    nkr = kr.shape[0]
    vt1[pl.ds(0, HD), pl.ds(0, nkr)] = kvr[1].T
    vt1[pl.ds(HD, 16), pl.ds(0, nkr)] = jnp.ones((16, nkr), BF)
    for n in range(tiles):
        sl = pl.ds(n * TILE, TILE)
        if n < tiles_r:
            s = dot(knr[...], qnt[:, sl])
            at = lax.broadcasted_iota(jnp.int32, s.shape, 0)
            lane = lax.broadcasted_iota(jnp.int32, s.shape, 1) + n * TILE
            e = jnp.where(at * 8 <= lane, jnp.exp2(s * exp_scale), 0.0).astype(BF)
            er_ref[:, sl] = e
            ol[:, sl] = dot(vt1[:, pl.ds(0, nkr)], e)
        else:
            ol[:, sl] = jnp.zeros((HD + 16, TILE), F32)

    forward(3)

    def pass1(step, carry):
        chunk = chunk_at(step)
        wait_for(kall.at[pl.ds(0, NX - 1)], kvx_got.at[step])
        n_keys = NX * kall.shape[2]
        at = lax.broadcasted_iota(jnp.int32, (n_keys, HD), 0) + chunk * n_keys
        k_raw = kall[pl.ds(chunk * NX, NX), 0].reshape(n_keys, HD).astype(F32)
        inv = lax.rsqrt(jnp.mean(k_raw * k_raw, axis=-1, keepdims=True) + EPSILON)
        unit = k_raw * inv
        kf = unit * kg_ref[...]
        kn = kf.astype(BF)
        kn_ref[step] = kn
        knt_ref[step] = jnp.where(at < plen, kf, 0.0).astype(BF).T
        v = kall[pl.ds(chunk * NX, NX), 1].reshape(n_keys, HD).astype(F32)
        vt1[pl.ds(0, HD), :] = jnp.where(at < plen, v, 0.0).astype(BF).T
        lane = lax.broadcasted_iota(jnp.int32, (16, n_keys), 1) + chunk * n_keys
        vt1[pl.ds(HD, 16), :] = jnp.where(lane < plen, 1.0, 0.0).astype(BF)
        ahead_s = dot(kn, qnt[:, pl.ds(0, TILE)])
        for n in range(tiles):
            sl = pl.ds(n * TILE, TILE)
            s = ahead_s
            if n + 1 < tiles:
                ahead_s = dot(kn, qnt[:, pl.ds((n + 1) * TILE, TILE)])
            e = jnp.exp2(s * exp_scale)
            if n >= tiles_r:
                key = lax.broadcasted_iota(jnp.int32, s.shape, 0)
                lane = lax.broadcasted_iota(jnp.int32, s.shape, 1) + (n * TILE - rows_r)
                ahead = resp * (rows_p // 8) - chunk * n_keys
                e = jnp.where((key - ahead) * 8 <= lane, e, 0.0)
            e = e.astype(BF)
            e_ref[step, :, sl] = e
            ol[:, sl] += dot(vt1[...], e)
        return carry

    lax.fori_loop(0, NY, pass1, 0)

    for n in range(tiles):
        sl = pl.ds(n * TILE, TILE)
        rl = 1.0 / ol[pl.ds(HD, 1), sl]
        ds = (dt[:, sl] * rl).astype(BF)
        dst[:, sl] = ds
        delta = rl * jnp.sum(ds.astype(F32) * ol[pl.ds(0, HD), sl], axis=0, keepdims=True)
        delta_ref[:, sl] = jnp.broadcast_to(delta, (8, TILE))
    kterm[...] = jnp.zeros((8, HD), F32)

    def summed(slot, which):
        total = own[slot, which]
        for k in range(NX - 1):
            total = total + rx[slot, k, which].astype(F32)
        return total

    def along_y(slot):
        dy = (0, 1, 3, 2)[slot]
        wait_for(rx.at[slot], rx_got.at[slot])
        for which in range(2):
            ys[slot, which] = summed(slot, which).astype(BF)
        remote(ys.at[slot], ry.at[dy - 1], ry_sent, ry_got, y_peer(dy)).start()

    span = kall.shape[2]

    def pass2(back, carry):
        step = NY - 1 - back
        chunk = chunk_at(step)
        n_keys = NX * span
        v = kall[pl.ds(chunk * NX, NX), 1].reshape(n_keys, HD)
        gk = jnp.zeros((n_keys, HD), F32)
        ahead_dp = dot(v, dst[:, pl.ds(0, TILE)])
        for n in range(tiles):
            sl = pl.ds(n * TILE, TILE)
            dp = ahead_dp
            if n + 1 < tiles:
                ahead_dp = dot(v, dst[:, pl.ds((n + 1) * TILE, TILE)])
            e = e_ref[step, :, sl].astype(F32)
            gs = (e * (dp - delta_ref[pl.ds(0, 1), sl])).astype(BF)
            gs_ref[step, :, sl] = gs
            gk += dot(gs, qn[sl, :])
        at = lax.broadcasted_iota(jnp.int32, (n_keys, HD), 0) + chunk * n_keys
        gk = jnp.where(at < plen, gk * scale, 0.0)
        kn = kn_ref[step].astype(F32)
        kterm[...] += jnp.sum((gk * kn).reshape(n_keys // 8, 8, HD), axis=0)
        sums[step] = gk
        return carry

    lax.fori_loop(0, NY, pass2, 0)

    gkr = jnp.zeros((nkr, HD), F32)
    for n in range(tiles_r):
        sl = pl.ds(n * TILE, TILE)
        dp = dot(kvr[1], dst[:, sl])
        e = er_ref[:, sl].astype(F32)
        gs = (e * (dp - delta_ref[pl.ds(0, 1), sl])).astype(BF)
        gsr_ref[:, sl] = gs
        gkr += dot(gs, qn[sl, :])
    gkr = gkr * scale
    kn = knr[...].astype(F32)
    kterm[...] += jnp.sum((gkr * kn).reshape(nkr // 8, 8, HD), axis=0)

    stores = [
        pltpu.make_async_copy(dkvr_v, dkvr_out, out_sem.at[0]),
        pltpu.make_async_copy(dq_v.at[pl.ds(0, rows_r)], dqr_out, out_sem.at[1]),
        pltpu.make_async_copy(dq_v.at[pl.ds(rows_r, rows_p)], dqp_out, out_sem.at[2]),
        pltpu.make_async_copy(dkvp_v, dkvp_out, out_sem.at[3]),
        pltpu.make_async_copy(gsend.at[3, pl.ds(0, 2)], gains_out, out_sem.at[4]),
    ]
    term = jnp.sum(kterm[...], axis=0, keepdims=True)
    qterm = term / qg_ref[...]
    key_sum = term / kg_ref[...]
    which_row = lax.broadcasted_iota(jnp.int32, (8, HD), 0)
    gsend[0] = jnp.where(
        which_row == 0,
        jnp.broadcast_to(qterm, (8, HD)),
        jnp.where(which_row == 1, jnp.broadcast_to(key_sum, (8, HD)), 0.0),
    )

    def g_start(stage):
        for k in FARTHEST_FIRST:
            pltpu.make_async_remote_copy(
                src_ref=gsend.at[stage],
                dst_ref=grecv.at[stage, stage_at[stage]],
                send_sem=g_sent,
                recv_sem=g_got.at[stage],
                device_id=partner(stage, k),
                device_id_type=MESH,
            ).start()
        grecv[stage, stage_at[stage]] = gsend[stage]

    def g_finish(stage):
        wait_for(grecv.at[stage, pl.ds(0, 7)], g_got.at[stage])
        total = grecv[stage, 0]
        for k in range(1, 8):
            total = total + grecv[stage, k]
        gsend[stage + 1] = total


    @pl.when(grp < ngrp - 1)
    def _():
        pl.semaphore_wait(z_ready, ngrp - 1 - grp)

    g_start(0)

    def pass3(back, carry):
        step = NY - 1 - back
        n_keys = NX * span
        at = lax.broadcasted_iota(jnp.int32, (n_keys, HD), 0) + chunk_at(step) * n_keys
        gv = dot(e_ref[step], dst[...], NT)
        vsum[...] = jnp.where(at < plen, gv, 0.0)
        for k in range(NX):
            part[step, k, 0] = sums[step, pl.ds(k * span, span), :].astype(BF)
            part[step, k, 1] = vsum[pl.ds(k * span, span), :].astype(BF)
        own[step, 0] = sums[step, pl.ds(x * span, span), :]
        own[step, 1] = vsum[pl.ds(x * span, span), :]
        for dx in (2, 1, 3):
            remote(
                part.at[step, lax.rem(x + dx, NX)],
                rx.at[step, dx - 1],
                rx_sent,
                rx_got.at[step],
                x_peer(dx),
            ).start()
        return carry

    lax.fori_loop(0, NY, pass3, 0)

    gvr = dot(er_ref[...], dst[:, pl.ds(0, rows_r)], NT)
    ur = ukr[...]
    kf = kvr[0].astype(F32)
    inv = lax.rsqrt(jnp.mean(kf * kf, axis=-1, keepdims=True) + EPSILON)
    gu = gkr * kg_ref[...]
    dk = inv * (gu - ur * jnp.mean(gu * ur, axis=-1, keepdims=True))
    dkvr_v[0] = dk.astype(BF)
    dkvr_v[1] = gvr.astype(BF)
    stores[0].start()


    for n in range(tiles):
        sl = pl.ds(n * TILE, TILE)
        gq = dot(knt_ref[0], gs_ref[0, :, sl])
        for slot in range(1, NY):
            gq += dot(knt_ref[slot], gs_ref[slot, :, sl])
        if n < tiles_r:
            gq += dot(knrt[...], gsr_ref[:, sl])
        ut = unit_qt[:, sl]
        gu = gq * scale * gcol[...]
        back = inv_q[pl.ds(0, 1), sl] * (gu - ut * jnp.mean(gu * ut, axis=0, keepdims=True))
        dq_v[sl, :] = back.astype(BF).T
        if n < 2:
            along_y(3 - n)
    stores[1].start()
    stores[2].start()

    g_finish(0)
    g_start(1)
    along_y(1)
    wait_for(rx.at[0], rx_got.at[0])
    totals = [summed(0, which) for which in range(2)]
    kf = kall[resp, 0].astype(F32)
    inv = lax.rsqrt(jnp.mean(kf * kf, axis=-1, keepdims=True) + EPSILON)
    unit = kf * inv
    wait_for(kall.at[pl.ds(0, 15)], kv_sent)
    wait_for(rx, rx_sent)

    g_finish(1)
    g_start(2)

    wait_for(ry, ry_got)
    for which in range(2):
        for k in range(NY - 1):
            totals[which] = totals[which] + ry[k, which].astype(F32)
    gu = totals[0] * kg_ref[...]
    dk = inv * (gu - unit * jnp.mean(gu * unit, axis=-1, keepdims=True))
    dkvp_v[0] = dk.astype(BF)
    dkvp_v[1] = totals[1].astype(BF)
    stores[3].start()
    wait_for(ry, ry_sent)

    g_finish(2)
    stores[4].start()
    wait_for(grecv.at[:, pl.ds(0, 7)], g_sent)
    for store in stores:
        store.wait()


def hand_out(*refs):
    ins, outs, held = refs[:5], refs[5:10], refs[10:15]
    in_sem, out_sem = refs[15:]
    loads = [pltpu.make_async_copy(ins[n], held[n], in_sem.at[n]) for n in range(5)]
    stores = [pltpu.make_async_copy(held[n], outs[n], out_sem.at[n]) for n in range(5)]
    for load in loads:
        load.start()
    for load, store in zip(loads, stores):
        load.wait()
        store.start()
    for store in stores:
        store.wait()


def shards(
    q_prompt,
    q_resp,
    kv_prompt,
    kv_resp,
    dout_prompt,
    dout_resp,
    q_gain,
    k_gain,
    resp_len,
    prompt_len,
):
    span = q_prompt.shape[1]
    length = q_resp.shape[2]
    rows_r = length * 8
    rows_p = span * 8
    rows = rows_r + rows_p
    n_keys = NX * span
    any_spec = pl.BlockSpec(memory_space=pl.ANY)
    hbm = pl.BlockSpec(memory_space=pltpu.HBM)
    dma = pltpu.SemaphoreType.DMA
    out = pl.pallas_call(
        kernel,
        out_shape=(
            jax.ShapeDtypeStruct((rows_r, HD), BF),
            jax.ShapeDtypeStruct((rows_p, HD), BF),
            jax.ShapeDtypeStruct((2, span, HD), BF),
            jax.ShapeDtypeStruct((2, length, HD), BF),
            jax.ShapeDtypeStruct((2, HD), F32),
        ),
        in_specs=[hbm] * 10,
        out_specs=[any_spec] * 5,
        scratch_shapes=[
            pltpu.VMEM((1, HD), F32),
            pltpu.VMEM((1, HD), F32),
            pltpu.SMEM((1, 1), jnp.int32),
            pltpu.SMEM((1,), jnp.int32),
            pltpu.VMEM((rows, HD), BF),
            pltpu.VMEM((rows, HD), BF),
            pltpu.VMEM((2, length, HD), BF),
            pltpu.VMEM((NX * NY, 2, span, HD), BF),
            pltpu.VMEM((HD, rows), F32),
            pltpu.VMEM((8, rows), F32),
            pltpu.VMEM((HD, rows), BF),
            pltpu.VMEM((rows, HD), BF),
            pltpu.VMEM((HD, rows), F32),
            pltpu.VMEM((HD, rows), BF),
            pltpu.VMEM((8, rows), F32),
            pltpu.VMEM((HD, TILE), F32),
            pltpu.VMEM((NY, n_keys, HD), BF),
            pltpu.VMEM((NY, HD, n_keys), BF),
            pltpu.VMEM((HD + 16, n_keys), BF),
            pltpu.VMEM((length, HD), BF),
            pltpu.VMEM((HD, length), BF),
            pltpu.VMEM((length, HD), F32),
            pltpu.VMEM((NY, n_keys, rows), BF),
            pltpu.VMEM((length, rows_r), BF),
            pltpu.VMEM((NY, n_keys, rows), BF),
            pltpu.VMEM((length, rows_r), BF),
            pltpu.VMEM((HD + 16, rows), F32),
            pltpu.VMEM((NY, n_keys, HD), F32),
            pltpu.VMEM((n_keys, HD), F32),
            pltpu.VMEM((NY, NX, 2, span, HD), BF),
            pltpu.VMEM((NY, NX - 1, 2, span, HD), BF),
            pltpu.VMEM((NY, 2, span, HD), F32),
            pltpu.VMEM((NY, 2, span, HD), BF),
            pltpu.VMEM((NY - 1, 2, span, HD), BF),
            pltpu.VMEM((8, HD), F32),
            pltpu.VMEM((4, 8, HD), F32),
            pltpu.VMEM((3, 8, 8, HD), F32),
            pltpu.VMEM((rows, HD), BF),
            pltpu.VMEM((2, span, HD), BF),
            pltpu.VMEM((2, length, HD), BF),
            dma((10,)),
            dma((5,)),
            dma((NY,)),
            dma((NY - 1,)),
            dma,
            dma((NY,)),
            dma,
            dma,
            dma,
            dma((3,)),
            dma,
            pltpu.SemaphoreType.REGULAR,
        ],
        compiler_params=pltpu.CompilerParams(
            collective_id=0, has_side_effects=True, vmem_limit_bytes=62 * 2**20
        ),
        name="attention_grads",
    )(
        q_resp.reshape(rows_r, HD),
        q_prompt.reshape(rows_p, HD),
        kv_prompt.reshape(2, span, HD),
        kv_resp.reshape(2, length, HD),
        dout_resp.reshape(rows_r, HD),
        dout_prompt.reshape(rows_p, HD),
        q_gain.reshape(1, HD),
        k_gain.reshape(1, HD),
        resp_len,
        prompt_len,
    )
    out = pl.pallas_call(
        hand_out,
        out_shape=tuple(jax.ShapeDtypeStruct(a.shape, a.dtype) for a in out),
        in_specs=[any_spec] * 5,
        out_specs=[any_spec] * 5,
        scratch_shapes=[pltpu.VMEM(a.shape, a.dtype) for a in out] + [dma((5,))] * 2,
        name="hand_out",
    )(*out)
    return (
        out[1].reshape(q_prompt.shape),
        out[0].reshape(q_resp.shape),
        out[2].reshape(kv_prompt.shape),
        out[3].reshape(kv_resp.shape),
        out[4],
    )


def solution(mesh):
    return jax.shard_map(
        shards,
        mesh=mesh,
        in_specs=(
            P("grp", "resp", "head", None),
            P("grp", "resp", None, "head", None),
            P("grp", None, "resp", "head", None),
            P("grp", "resp", None, None, "head", None),
            P("grp", "resp", "head", None),
            P("grp", "resp", None, "head", None),
            P(),
            P(),
            P("grp", "resp"),
            P("grp"),
        ),
        out_specs=(
            P("grp", "resp", "head", None),
            P("grp", "resp", None, "head", None),
            P("grp", None, "resp", "head", None),
            P("grp", "resp", None, None, "head", None),
            P(),
        ),
        check_vma=False,
    )
```

```python
import functools
import math

import jax
import jax.numpy as jnp
from jax import lax
from jax.experimental import pallas as pl
from jax.experimental.pallas import tpu as pltpu
from jax.sharding import PartitionSpec as P

EPSILON = 1e-06
MESH = pl.DeviceIdType.MESH
HD = 128
BF = jnp.bfloat16
F32 = jnp.float32
NX = 4
NY = 4
TILE = 512
FARTHEST_FIRST = (4, 3, 5, 2, 6, 1, 7)
NT = (((1,), (1,)), ((), ()))
NN = (((1,), (0,)), ((), ()))


def dot(lhs, rhs, dims=NN):
    return lax.dot_general(lhs, rhs, dims, preferred_element_type=F32)


def order(step):
    return step + step // 2 - 2 * (step // 3)


def kernel(
    qr_in,
    qp_in,
    kvp_in,
    kvr_in,
    dr_in,
    dp_in,
    qg_in,
    kg_in,
    rlen_in,
    plen_in,
    dqr_out,
    dqp_out,
    dkvp_out,
    dkvr_out,
    gains_out,
    qg_ref,
    kg_ref,
    rlen_ref,
    plen_ref,
    q_nat,
    d_nat,
    kvr,
    kall,
    unit_qt,
    inv_q,
    qnt,
    qn,
    dt,
    dst,
    delta_ref,
    gcol,
    kn_ref,
    knt_ref,
    vt1,
    knr,
    knrt,
    ukr,
    e_ref,
    er_ref,
    gs_ref,
    gsr_ref,
    ol,
    sums,
    vsum,
    part,
    rx,
    own,
    ys,
    ry,
    kterm,
    gsend,
    grecv,
    dq_v,
    dkvp_v,
    dkvr_v,
    in_sem,
    out_sem,
    kvx_got,
    kvy_got,
    kv_sent,
    rx_got,
    rx_sent,
    ry_got,
    ry_sent,
    g_got,
    g_sent,
    z_ready,
):
    resp = lax.axis_index("resp")
    head = lax.axis_index("head")
    grp = lax.axis_index("grp")
    yh = resp // NX
    x = lax.rem(resp, NX)
    yl = head // 2
    core = lax.rem(head, 2)
    ngrp = 8
    y8 = 2 * yh + yl
    rows_r = qr_in.shape[0]
    rows_p = qp_in.shape[0]
    rows = rows_r + rows_p
    tiles = rows // TILE
    tiles_r = rows_r // TILE
    scale = HD**-0.5
    exp_scale = scale * math.log2(math.e)

    def partner(stage, k):
        if stage == 0:
            return {"grp": lax.rem(grp + k, ngrp)}
        if stage == 1:
            to = lax.rem(y8 + k, 8)
            return {"resp": (to // 2) * NX + x, "head": lax.rem(to, 2) * 2 + core}
        to = lax.rem(2 * x + core + k, 8)
        return {"resp": yh * NX + to // 2, "head": yl * 2 + lax.rem(to, 2)}

    stage_at = (grp, y8, 2 * x + core)

    loads = [
        pltpu.make_async_copy(kvp_in, kall.at[resp], in_sem.at[0]),
        pltpu.make_async_copy(qr_in, q_nat.at[pl.ds(0, rows_r)], in_sem.at[1]),
        pltpu.make_async_copy(qp_in, q_nat.at[pl.ds(rows_r, rows_p)], in_sem.at[2]),
        pltpu.make_async_copy(kvr_in, kvr, in_sem.at[3]),
        pltpu.make_async_copy(dr_in, d_nat.at[pl.ds(0, rows_r)], in_sem.at[4]),
        pltpu.make_async_copy(dp_in, d_nat.at[pl.ds(rows_r, rows_p)], in_sem.at[5]),
        pltpu.make_async_copy(qg_in, qg_ref, in_sem.at[6]),
        pltpu.make_async_copy(kg_in, kg_ref, in_sem.at[7]),
        pltpu.make_async_copy(rlen_in, rlen_ref, in_sem.at[8]),
        pltpu.make_async_copy(plen_in, plen_ref, in_sem.at[9]),
    ]
    loads[0].start()
    barrier = pltpu.get_barrier_semaphore()
    for k in FARTHEST_FIRST:
        for stage in (1, 2):
            pl.semaphore_signal(
                barrier, inc=1, device_id=partner(stage, k), device_id_type=MESH
            )
    for k in range(7, 0, -1):

        @pl.when(grp + k < ngrp)
        def _(k=k):
            pl.semaphore_signal(
                barrier, inc=1, device_id={"grp": grp + k}, device_id_type=MESH
            )

    loads[0].wait()
    pl.semaphore_wait(barrier, 14 + grp)

    def remote(src, dst, sent, got, to):
        return pltpu.make_async_remote_copy(
            src_ref=src,
            dst_ref=dst,
            send_sem=sent,
            recv_sem=got,
            device_id={"resp": to},
            device_id_type=MESH,
        )

    def wait_for(ref, sem):
        pltpu.make_async_copy(ref, ref, sem).wait()

    def x_peer(dx):
        return yh * NX + lax.rem(x + dx, NX)

    def y_peer(dy):
        return lax.rem(yh + dy, NY) * NX + x

    def chunk_at(slot):
        return lax.rem(yh + order(slot), NY)

    def along_x(slot):
        block = kall.at[chunk_at(slot) * NX + x]
        for dx in (2, 1, 3):
            remote(block, block, kv_sent, kvx_got.at[slot], x_peer(dx)).start()

    for dy in (2, 1, 3):
        remote(
            kall.at[resp], kall.at[resp], kv_sent, kvy_got.at[dy - 1], y_peer(dy)
        ).start()
    along_x(0)
    for load in loads[1:]:
        load.start()

    def forward(slot):
        dy = (0, 1, 3, 2)[slot]
        wait_for(kall.at[y_peer(dy)], kvy_got.at[(4 - dy) - 1])
        along_x(slot)

    for load in loads[6:]:
        load.wait()
    plen = plen_ref[0]
    rlen = rlen_ref[0, 0]

    gcol[...] = jnp.broadcast_to(qg_ref[...], (TILE, HD)).T
    loads[1].wait()
    loads[2].wait()
    for n in range(tiles):
        sl = pl.ds(n * TILE, TILE)
        xt = q_nat[sl, :].T.astype(F32)
        inv = lax.rsqrt(jnp.mean(xt * xt, axis=0, keepdims=True) + EPSILON)
        ut = xt * inv
        unit_qt[:, sl] = ut
        inv_q[:, sl] = jnp.broadcast_to(inv, (8, TILE))
        qt = (ut * gcol[...]).astype(BF)
        qnt[:, sl] = qt
        qn[sl, :] = qt.T

    forward(1)
    forward(2)
    for k in range(7, 0, -1):

        @pl.when(grp >= k)
        def _(k=k):
            pl.semaphore_signal(
                z_ready, inc=1, device_id={"grp": grp - k}, device_id_type=MESH
            )


    loads[4].wait()
    loads[5].wait()
    for n in range(tiles):
        sl = pl.ds(n * TILE, TILE)
        lane = lax.broadcasted_iota(jnp.int32, (HD, TILE), 1) + n * TILE
        if n < tiles_r:
            keep = lane < rlen * 8
        else:
            keep = lane - rows_r < (plen - rows_p // 8 * resp) * 8
        dt[:, sl] = jnp.where(keep, d_nat[sl, :].T.astype(F32), 0.0)

    loads[3].wait()
    kf = kvr[0].astype(F32)
    inv_kr = lax.rsqrt(jnp.mean(kf * kf, axis=-1, keepdims=True) + EPSILON)
    ur = kf * inv_kr
    ukr[...] = ur
    kr = (ur * kg_ref[...]).astype(BF)
    knr[...] = kr
    knrt[...] = kr.T
    nkr = kr.shape[0]
    vt1[pl.ds(0, HD), pl.ds(0, nkr)] = kvr[1].T
    vt1[pl.ds(HD, 16), pl.ds(0, nkr)] = jnp.ones((16, nkr), BF)
    for n in range(tiles):
        sl = pl.ds(n * TILE, TILE)
        if n < tiles_r:
            s = dot(knr[...], qnt[:, sl])
            at = lax.broadcasted_iota(jnp.int32, s.shape, 0)
            lane = lax.broadcasted_iota(jnp.int32, s.shape, 1) + n * TILE
            e = jnp.where(at * 8 <= lane, jnp.exp2(s * exp_scale), 0.0).astype(BF)
            er_ref[:, sl] = e
            ol[:, sl] = dot(vt1[:, pl.ds(0, nkr)], e)
        else:
            ol[:, sl] = jnp.zeros((HD + 16, TILE), F32)

    forward(3)

    def pass1(step, carry):
        chunk = chunk_at(step)
        wait_for(kall.at[pl.ds(0, NX - 1)], kvx_got.at[step])
        n_keys = NX * kall.shape[2]
        at = lax.broadcasted_iota(jnp.int32, (n_keys, HD), 0) + chunk * n_keys
        k_raw = kall[pl.ds(chunk * NX, NX), 0].reshape(n_keys, HD).astype(F32)
        inv = lax.rsqrt(jnp.mean(k_raw * k_raw, axis=-1, keepdims=True) + EPSILON)
        unit = k_raw * inv
        kf = unit * kg_ref[...]
        kn = kf.astype(BF)
        kn_ref[step] = kn
        knt_ref[step] = jnp.where(at < plen, kf, 0.0).astype(BF).T
        v = kall[pl.ds(chunk * NX, NX), 1].reshape(n_keys, HD).astype(F32)
        vt1[pl.ds(0, HD), :] = jnp.where(at < plen, v, 0.0).astype(BF).T
        lane = lax.broadcasted_iota(jnp.int32, (16, n_keys), 1) + chunk * n_keys
        vt1[pl.ds(HD, 16), :] = jnp.where(lane < plen, 1.0, 0.0).astype(BF)
        ahead_s = dot(kn, qnt[:, pl.ds(0, TILE)])
        for n in range(tiles):
            sl = pl.ds(n * TILE, TILE)
            s = ahead_s
            if n + 1 < tiles:
                ahead_s = dot(kn, qnt[:, pl.ds((n + 1) * TILE, TILE)])
            e = jnp.exp2(s * exp_scale)
            if n >= tiles_r:
                key = lax.broadcasted_iota(jnp.int32, s.shape, 0)
                lane = lax.broadcasted_iota(jnp.int32, s.shape, 1) + (n * TILE - rows_r)
                ahead = resp * (rows_p // 8) - chunk * n_keys
                e = jnp.where((key - ahead) * 8 <= lane, e, 0.0)
            e = e.astype(BF)
            e_ref[step, :, sl] = e
            ol[:, sl] += dot(vt1[...], e)
        return carry

    lax.fori_loop(0, NY, pass1, 0)

    for n in range(tiles):
        sl = pl.ds(n * TILE, TILE)
        rl = 1.0 / ol[pl.ds(HD, 1), sl]
        ds = (dt[:, sl] * rl).astype(BF)
        dst[:, sl] = ds
        delta = rl * jnp.sum(ds.astype(F32) * ol[pl.ds(0, HD), sl], axis=0, keepdims=True)
        delta_ref[:, sl] = jnp.broadcast_to(delta, (8, TILE))
    kterm[...] = jnp.zeros((8, HD), F32)

    def summed(slot, which):
        total = own[slot, which]
        for k in range(NX - 1):
            total = total + rx[slot, k, which].astype(F32)
        return total

    def along_y(slot):
        dy = (0, 1, 3, 2)[slot]
        wait_for(rx.at[slot], rx_got.at[slot])
        for which in range(2):
            ys[slot, which] = summed(slot, which).astype(BF)
        remote(ys.at[slot], ry.at[dy - 1], ry_sent, ry_got, y_peer(dy)).start()

    span = kall.shape[2]

    def value_sums(step):
        n_keys = NX * span
        at = lax.broadcasted_iota(jnp.int32, (n_keys, HD), 0) + chunk_at(step) * n_keys
        gv = dot(e_ref[step], dst[...], NT)
        vsum[...] = jnp.where(at < plen, gv, 0.0)
        for k in range(NX):
            part[step, k, 0] = sums[step, pl.ds(k * span, span), :].astype(BF)
            part[step, k, 1] = vsum[pl.ds(k * span, span), :].astype(BF)
        own[step, 0] = sums[step, pl.ds(x * span, span), :]
        own[step, 1] = vsum[pl.ds(x * span, span), :]
        for dx in (2, 1, 3):
            remote(
                part.at[step, lax.rem(x + dx, NX)],
                rx.at[step, dx - 1],
                rx_sent,
                rx_got.at[step],
                x_peer(dx),
            ).start()

    def pass2(back, carry):
        step = NY - 1 - back
        chunk = chunk_at(step)
        n_keys = NX * span
        v = kall[pl.ds(chunk * NX, NX), 1].reshape(n_keys, HD)
        gk = jnp.zeros((n_keys, HD), F32)
        ahead_dp = dot(v, dst[:, pl.ds(0, TILE)])
        for n in range(tiles):
            sl = pl.ds(n * TILE, TILE)
            dp = ahead_dp
            if n + 1 < tiles:
                ahead_dp = dot(v, dst[:, pl.ds((n + 1) * TILE, TILE)])
            e = e_ref[step, :, sl].astype(F32)
            gs = (e * (dp - delta_ref[pl.ds(0, 1), sl])).astype(BF)
            gs_ref[step, :, sl] = gs
            gk += dot(gs, qn[sl, :])
        at = lax.broadcasted_iota(jnp.int32, (n_keys, HD), 0) + chunk * n_keys
        gk = jnp.where(at < plen, gk * scale, 0.0)
        kn = kn_ref[step].astype(F32)
        kterm[...] += jnp.sum((gk * kn).reshape(n_keys // 8, 8, HD), axis=0)
        sums[step] = gk

        @pl.when(back < NY - 1)
        def _():
            value_sums(step)

        return carry

    lax.fori_loop(0, NY, pass2, 0)

    gkr = jnp.zeros((nkr, HD), F32)
    for n in range(tiles_r):
        sl = pl.ds(n * TILE, TILE)
        dp = dot(kvr[1], dst[:, sl])
        e = er_ref[:, sl].astype(F32)
        gs = (e * (dp - delta_ref[pl.ds(0, 1), sl])).astype(BF)
        gsr_ref[:, sl] = gs
        gkr += dot(gs, qn[sl, :])
    gkr = gkr * scale
    kn = knr[...].astype(F32)
    kterm[...] += jnp.sum((gkr * kn).reshape(nkr // 8, 8, HD), axis=0)

    stores = [
        pltpu.make_async_copy(dkvr_v, dkvr_out, out_sem.at[0]),
        pltpu.make_async_copy(dq_v.at[pl.ds(0, rows_r)], dqr_out, out_sem.at[1]),
        pltpu.make_async_copy(dq_v.at[pl.ds(rows_r, rows_p)], dqp_out, out_sem.at[2]),
        pltpu.make_async_copy(dkvp_v, dkvp_out, out_sem.at[3]),
        pltpu.make_async_copy(gsend.at[3, pl.ds(0, 2)], gains_out, out_sem.at[4]),
    ]
    term = jnp.sum(kterm[...], axis=0, keepdims=True)
    qterm = term / qg_ref[...]
    key_sum = term / kg_ref[...]
    which_row = lax.broadcasted_iota(jnp.int32, (8, HD), 0)
    gsend[0] = jnp.where(
        which_row == 0,
        jnp.broadcast_to(qterm, (8, HD)),
        jnp.where(which_row == 1, jnp.broadcast_to(key_sum, (8, HD)), 0.0),
    )

    def g_start(stage):
        for k in FARTHEST_FIRST:
            pltpu.make_async_remote_copy(
                src_ref=gsend.at[stage],
                dst_ref=grecv.at[stage, stage_at[stage]],
                send_sem=g_sent,
                recv_sem=g_got.at[stage],
                device_id=partner(stage, k),
                device_id_type=MESH,
            ).start()
        grecv[stage, stage_at[stage]] = gsend[stage]

    def g_finish(stage):
        wait_for(grecv.at[stage, pl.ds(0, 7)], g_got.at[stage])
        total = grecv[stage, 0]
        for k in range(1, 8):
            total = total + grecv[stage, k]
        gsend[stage + 1] = total


    @pl.when(grp < ngrp - 1)
    def _():
        pl.semaphore_wait(z_ready, ngrp - 1 - grp)

    g_start(0)

    value_sums(0)

    gvr = dot(er_ref[...], dst[:, pl.ds(0, rows_r)], NT)
    ur = ukr[...]
    kf = kvr[0].astype(F32)
    inv = lax.rsqrt(jnp.mean(kf * kf, axis=-1, keepdims=True) + EPSILON)
    gu = gkr * kg_ref[...]
    dk = inv * (gu - ur * jnp.mean(gu * ur, axis=-1, keepdims=True))
    dkvr_v[0] = dk.astype(BF)
    dkvr_v[1] = gvr.astype(BF)
    stores[0].start()


    for n in range(tiles):
        sl = pl.ds(n * TILE, TILE)
        gq = dot(knt_ref[0], gs_ref[0, :, sl])
        for slot in range(1, NY):
            gq += dot(knt_ref[slot], gs_ref[slot, :, sl])
        if n < tiles_r:
            gq += dot(knrt[...], gsr_ref[:, sl])
        ut = unit_qt[:, sl]
        gu = gq * scale * gcol[...]
        back = inv_q[pl.ds(0, 1), sl] * (gu - ut * jnp.mean(gu * ut, axis=0, keepdims=True))
        dq_v[sl, :] = back.astype(BF).T
        if n < 2:
            along_y(3 - n)
    stores[1].start()
    stores[2].start()

    g_finish(0)
    g_start(1)
    along_y(1)
    wait_for(rx.at[0], rx_got.at[0])
    totals = [summed(0, which) for which in range(2)]
    kf = kall[resp, 0].astype(F32)
    inv = lax.rsqrt(jnp.mean(kf * kf, axis=-1, keepdims=True) + EPSILON)
    unit = kf * inv
    wait_for(kall.at[pl.ds(0, 15)], kv_sent)
    wait_for(rx, rx_sent)

    g_finish(1)
    g_start(2)

    wait_for(ry, ry_got)
    for which in range(2):
        for k in range(NY - 1):
            totals[which] = totals[which] + ry[k, which].astype(F32)
    gu = totals[0] * kg_ref[...]
    dk = inv * (gu - unit * jnp.mean(gu * unit, axis=-1, keepdims=True))
    dkvp_v[0] = dk.astype(BF)
    dkvp_v[1] = totals[1].astype(BF)
    stores[3].start()
    wait_for(ry, ry_sent)

    g_finish(2)
    stores[4].start()
    wait_for(grecv.at[:, pl.ds(0, 7)], g_sent)
    for store in stores:
        store.wait()


def hand_out(*refs):
    ins, outs, held = refs[:5], refs[5:10], refs[10:15]
    in_sem, out_sem = refs[15:]
    loads = [pltpu.make_async_copy(ins[n], held[n], in_sem.at[n]) for n in range(5)]
    stores = [pltpu.make_async_copy(held[n], outs[n], out_sem.at[n]) for n in range(5)]
    for load in loads:
        load.start()
    for load, store in zip(loads, stores):
        load.wait()
        store.start()
    for store in stores:
        store.wait()


def shards(
    q_prompt,
    q_resp,
    kv_prompt,
    kv_resp,
    dout_prompt,
    dout_resp,
    q_gain,
    k_gain,
    resp_len,
    prompt_len,
):
    span = q_prompt.shape[1]
    length = q_resp.shape[2]
    rows_r = length * 8
    rows_p = span * 8
    rows = rows_r + rows_p
    n_keys = NX * span
    any_spec = pl.BlockSpec(memory_space=pl.ANY)
    hbm = pl.BlockSpec(memory_space=pltpu.HBM)
    dma = pltpu.SemaphoreType.DMA
    out = pl.pallas_call(
        kernel,
        out_shape=(
            jax.ShapeDtypeStruct((rows_r, HD), BF),
            jax.ShapeDtypeStruct((rows_p, HD), BF),
            jax.ShapeDtypeStruct((2, span, HD), BF),
            jax.ShapeDtypeStruct((2, length, HD), BF),
            jax.ShapeDtypeStruct((2, HD), F32),
        ),
        in_specs=[hbm] * 10,
        out_specs=[any_spec] * 5,
        scratch_shapes=[
            pltpu.VMEM((1, HD), F32),
            pltpu.VMEM((1, HD), F32),
            pltpu.SMEM((1, 1), jnp.int32),
            pltpu.SMEM((1,), jnp.int32),
            pltpu.VMEM((rows, HD), BF),
            pltpu.VMEM((rows, HD), BF),
            pltpu.VMEM((2, length, HD), BF),
            pltpu.VMEM((NX * NY, 2, span, HD), BF),
            pltpu.VMEM((HD, rows), F32),
            pltpu.VMEM((8, rows), F32),
            pltpu.VMEM((HD, rows), BF),
            pltpu.VMEM((rows, HD), BF),
            pltpu.VMEM((HD, rows), F32),
            pltpu.VMEM((HD, rows), BF),
            pltpu.VMEM((8, rows), F32),
            pltpu.VMEM((HD, TILE), F32),
            pltpu.VMEM((NY, n_keys, HD), BF),
            pltpu.VMEM((NY, HD, n_keys), BF),
            pltpu.VMEM((HD + 16, n_keys), BF),
            pltpu.VMEM((length, HD), BF),
            pltpu.VMEM((HD, length), BF),
            pltpu.VMEM((length, HD), F32),
            pltpu.VMEM((NY, n_keys, rows), BF),
            pltpu.VMEM((length, rows_r), BF),
            pltpu.VMEM((NY, n_keys, rows), BF),
            pltpu.VMEM((length, rows_r), BF),
            pltpu.VMEM((HD + 16, rows), F32),
            pltpu.VMEM((NY, n_keys, HD), F32),
            pltpu.VMEM((n_keys, HD), F32),
            pltpu.VMEM((NY, NX, 2, span, HD), BF),
            pltpu.VMEM((NY, NX - 1, 2, span, HD), BF),
            pltpu.VMEM((NY, 2, span, HD), F32),
            pltpu.VMEM((NY, 2, span, HD), BF),
            pltpu.VMEM((NY - 1, 2, span, HD), BF),
            pltpu.VMEM((8, HD), F32),
            pltpu.VMEM((4, 8, HD), F32),
            pltpu.VMEM((3, 8, 8, HD), F32),
            pltpu.VMEM((rows, HD), BF),
            pltpu.VMEM((2, span, HD), BF),
            pltpu.VMEM((2, length, HD), BF),
            dma((10,)),
            dma((5,)),
            dma((NY,)),
            dma((NY - 1,)),
            dma,
            dma((NY,)),
            dma,
            dma,
            dma,
            dma((3,)),
            dma,
            pltpu.SemaphoreType.REGULAR,
        ],
        compiler_params=pltpu.CompilerParams(
            collective_id=0, has_side_effects=True, vmem_limit_bytes=62 * 2**20
        ),
        name="attention_grads",
    )(
        q_resp.reshape(rows_r, HD),
        q_prompt.reshape(rows_p, HD),
        kv_prompt.reshape(2, span, HD),
        kv_resp.reshape(2, length, HD),
        dout_resp.reshape(rows_r, HD),
        dout_prompt.reshape(rows_p, HD),
        q_gain.reshape(1, HD),
        k_gain.reshape(1, HD),
        resp_len,
        prompt_len,
    )
    out = pl.pallas_call(
        hand_out,
        out_shape=tuple(jax.ShapeDtypeStruct(a.shape, a.dtype) for a in out),
        in_specs=[any_spec] * 5,
        out_specs=[any_spec] * 5,
        scratch_shapes=[pltpu.VMEM(a.shape, a.dtype) for a in out] + [dma((5,))] * 2,
        name="hand_out",
    )(*out)
    return (
        out[1].reshape(q_prompt.shape),
        out[0].reshape(q_resp.shape),
        out[2].reshape(kv_prompt.shape),
        out[3].reshape(kv_resp.shape),
        out[4],
    )


def solution(mesh):
    return jax.shard_map(
        shards,
        mesh=mesh,
        in_specs=(
            P("grp", "resp", "head", None),
            P("grp", "resp", None, "head", None),
            P("grp", None, "resp", "head", None),
            P("grp", "resp", None, None, "head", None),
            P("grp", "resp", "head", None),
            P("grp", "resp", None, "head", None),
            P(),
            P(),
            P("grp", "resp"),
            P("grp"),
        ),
        out_specs=(
            P("grp", "resp", "head", None),
            P("grp", "resp", None, "head", None),
            P("grp", None, "resp", "head", None),
            P("grp", "resp", None, None, "head", None),
            P(),
        ),
        check_vma=False,
    )
```

```python
import functools
import math

import jax
import jax.numpy as jnp
from jax import lax
from jax.experimental import pallas as pl
from jax.experimental.pallas import tpu as pltpu
from jax.sharding import PartitionSpec as P

EPSILON = 1e-06
MESH = pl.DeviceIdType.MESH
HD = 128
BF = jnp.bfloat16
F32 = jnp.float32
NX = 4
NY = 4
TILE = 512
FARTHEST_FIRST = (4, 3, 5, 2, 6, 1, 7)
NT = (((1,), (1,)), ((), ()))
NN = (((1,), (0,)), ((), ()))


def dot(lhs, rhs, dims=NN):
    return lax.dot_general(lhs, rhs, dims, preferred_element_type=F32)


def order(step):
    return step + step // 2 - 2 * (step // 3)


def kernel(
    qr_in,
    qp_in,
    kvp_in,
    kvr_in,
    dr_in,
    dp_in,
    qg_in,
    kg_in,
    rlen_in,
    plen_in,
    dqr_out,
    dqp_out,
    dkvp_out,
    dkvr_out,
    gains_out,
    qg_ref,
    kg_ref,
    rlen_ref,
    plen_ref,
    q_nat,
    d_nat,
    kvr,
    kall,
    unit_qt,
    inv_q,
    qnt,
    qn,
    dt,
    dst,
    delta_ref,
    gcol,
    kn_ref,
    knt_ref,
    vt1,
    knr,
    knrt,
    ukr,
    e_ref,
    er_ref,
    gs_ref,
    gsr_ref,
    ol,
    sums,
    vsum,
    part,
    rx,
    own,
    ys,
    ry,
    kterm,
    gsend,
    grecv,
    dq_v,
    dkvp_v,
    dkvr_v,
    in_sem,
    out_sem,
    kvx_got,
    kvy_got,
    kv_sent,
    rx_got,
    rx_sent,
    ry_got,
    ry_sent,
    g_got,
    g_sent,
    z_ready,
):
    resp = lax.axis_index("resp")
    head = lax.axis_index("head")
    grp = lax.axis_index("grp")
    yh = resp // NX
    x = lax.rem(resp, NX)
    yl = head // 2
    core = lax.rem(head, 2)
    ngrp = 8
    y8 = 2 * yh + yl
    rows_r = qr_in.shape[0]
    rows_p = qp_in.shape[0]
    rows = rows_r + rows_p
    tiles = rows // TILE
    tiles_r = rows_r // TILE
    scale = HD**-0.5
    exp_scale = scale * math.log2(math.e)

    def partner(stage, k):
        if stage == 0:
            to = lax.rem(y8 + k, 8)
            return {"resp": (to // 2) * NX + x, "head": lax.rem(to, 2) * 2 + core}
        if stage == 1:
            to = lax.rem(2 * x + core + k, 8)
            return {"resp": yh * NX + to // 2, "head": yl * 2 + lax.rem(to, 2)}
        return {"grp": lax.rem(grp + k, ngrp)}

    stage_at = (y8, 2 * x + core, grp)

    loads = [
        pltpu.make_async_copy(kvp_in, kall.at[resp], in_sem.at[0]),
        pltpu.make_async_copy(qr_in, q_nat.at[pl.ds(0, rows_r)], in_sem.at[1]),
        pltpu.make_async_copy(qp_in, q_nat.at[pl.ds(rows_r, rows_p)], in_sem.at[2]),
        pltpu.make_async_copy(kvr_in, kvr, in_sem.at[3]),
        pltpu.make_async_copy(dr_in, d_nat.at[pl.ds(0, rows_r)], in_sem.at[4]),
        pltpu.make_async_copy(dp_in, d_nat.at[pl.ds(rows_r, rows_p)], in_sem.at[5]),
        pltpu.make_async_copy(qg_in, qg_ref, in_sem.at[6]),
        pltpu.make_async_copy(kg_in, kg_ref, in_sem.at[7]),
        pltpu.make_async_copy(rlen_in, rlen_ref, in_sem.at[8]),
        pltpu.make_async_copy(plen_in, plen_ref, in_sem.at[9]),
    ]
    loads[0].start()
    barrier = pltpu.get_barrier_semaphore()
    for k in FARTHEST_FIRST:
        for stage in (0, 1):
            pl.semaphore_signal(
                barrier, inc=1, device_id=partner(stage, k), device_id_type=MESH
            )
    for k in range(7, 0, -1):

        @pl.when(grp + k < ngrp)
        def _(k=k):
            pl.semaphore_signal(
                barrier, inc=1, device_id={"grp": grp + k}, device_id_type=MESH
            )

    loads[0].wait()
    pl.semaphore_wait(barrier, 14 + grp)

    def remote(src, dst, sent, got, to):
        return pltpu.make_async_remote_copy(
            src_ref=src,
            dst_ref=dst,
            send_sem=sent,
            recv_sem=got,
            device_id={"resp": to},
            device_id_type=MESH,
        )

    def wait_for(ref, sem):
        pltpu.make_async_copy(ref, ref, sem).wait()

    def x_peer(dx):
        return yh * NX + lax.rem(x + dx, NX)

    def y_peer(dy):
        return lax.rem(yh + dy, NY) * NX + x

    def chunk_at(slot):
        return lax.rem(yh + order(slot), NY)

    def along_x(slot):
        block = kall.at[chunk_at(slot) * NX + x]
        for dx in (2, 1, 3):
            remote(block, block, kv_sent, kvx_got.at[slot], x_peer(dx)).start()

    for dy in (2, 1, 3):
        remote(
            kall.at[resp], kall.at[resp], kv_sent, kvy_got.at[dy - 1], y_peer(dy)
        ).start()
    along_x(0)
    for load in loads[1:]:
        load.start()

    def forward(slot):
        dy = (0, 1, 3, 2)[slot]
        wait_for(kall.at[y_peer(dy)], kvy_got.at[(4 - dy) - 1])
        along_x(slot)

    for load in loads[6:]:
        load.wait()
    plen = plen_ref[0]
    rlen = rlen_ref[0, 0]

    gcol[...] = jnp.broadcast_to(qg_ref[...], (TILE, HD)).T
    loads[1].wait()
    loads[2].wait()
    for n in range(tiles):
        sl = pl.ds(n * TILE, TILE)
        xt = q_nat[sl, :].T.astype(F32)
        inv = lax.rsqrt(jnp.mean(xt * xt, axis=0, keepdims=True) + EPSILON)
        ut = xt * inv
        unit_qt[:, sl] = ut
        inv_q[:, sl] = jnp.broadcast_to(inv, (8, TILE))
        qt = (ut * gcol[...]).astype(BF)
        qnt[:, sl] = qt
        qn[sl, :] = qt.T

    forward(1)
    forward(2)
    for k in range(7, 0, -1):

        @pl.when(grp >= k)
        def _(k=k):
            pl.semaphore_signal(
                z_ready, inc=1, device_id={"grp": grp - k}, device_id_type=MESH
            )


    loads[4].wait()
    loads[5].wait()
    for n in range(tiles):
        sl = pl.ds(n * TILE, TILE)
        lane = lax.broadcasted_iota(jnp.int32, (HD, TILE), 1) + n * TILE
        if n < tiles_r:
            keep = lane < rlen * 8
        else:
            keep = lane - rows_r < (plen - rows_p // 8 * resp) * 8
        dt[:, sl] = jnp.where(keep, d_nat[sl, :].T.astype(F32), 0.0)

    loads[3].wait()
    kf = kvr[0].astype(F32)
    inv_kr = lax.rsqrt(jnp.mean(kf * kf, axis=-1, keepdims=True) + EPSILON)
    ur = kf * inv_kr
    ukr[...] = ur
    kr = (ur * kg_ref[...]).astype(BF)
    knr[...] = kr
    knrt[...] = kr.T
    nkr = kr.shape[0]
    vt1[pl.ds(0, HD), pl.ds(0, nkr)] = kvr[1].T
    vt1[pl.ds(HD, 16), pl.ds(0, nkr)] = jnp.ones((16, nkr), BF)
    for n in range(tiles):
        sl = pl.ds(n * TILE, TILE)
        if n < tiles_r:
            s = dot(knr[...], qnt[:, sl])
            at = lax.broadcasted_iota(jnp.int32, s.shape, 0)
            lane = lax.broadcasted_iota(jnp.int32, s.shape, 1) + n * TILE
            e = jnp.where(at * 8 <= lane, jnp.exp2(s * exp_scale), 0.0).astype(BF)
            er_ref[:, sl] = e
            ol[:, sl] = dot(vt1[:, pl.ds(0, nkr)], e)
        else:
            ol[:, sl] = jnp.zeros((HD + 16, TILE), F32)

    forward(3)

    def pass1(step, carry):
        chunk = chunk_at(step)
        wait_for(kall.at[pl.ds(0, NX - 1)], kvx_got.at[step])
        n_keys = NX * kall.shape[2]
        at = lax.broadcasted_iota(jnp.int32, (n_keys, HD), 0) + chunk * n_keys
        k_raw = kall[pl.ds(chunk * NX, NX), 0].reshape(n_keys, HD).astype(F32)
        inv = lax.rsqrt(jnp.mean(k_raw * k_raw, axis=-1, keepdims=True) + EPSILON)
        unit = k_raw * inv
        kf = unit * kg_ref[...]
        kn = kf.astype(BF)
        kn_ref[step] = kn
        knt_ref[step] = jnp.where(at < plen, kf, 0.0).astype(BF).T
        v = kall[pl.ds(chunk * NX, NX), 1].reshape(n_keys, HD).astype(F32)
        vt1[pl.ds(0, HD), :] = jnp.where(at < plen, v, 0.0).astype(BF).T
        lane = lax.broadcasted_iota(jnp.int32, (16, n_keys), 1) + chunk * n_keys
        vt1[pl.ds(HD, 16), :] = jnp.where(lane < plen, 1.0, 0.0).astype(BF)
        ahead_s = dot(kn, qnt[:, pl.ds(0, TILE)])
        for n in range(tiles):
            sl = pl.ds(n * TILE, TILE)
            s = ahead_s
            if n + 1 < tiles:
                ahead_s = dot(kn, qnt[:, pl.ds((n + 1) * TILE, TILE)])
            e = jnp.exp2(s * exp_scale)
            if n >= tiles_r:
                key = lax.broadcasted_iota(jnp.int32, s.shape, 0)
                lane = lax.broadcasted_iota(jnp.int32, s.shape, 1) + (n * TILE - rows_r)
                ahead = resp * (rows_p // 8) - chunk * n_keys
                e = jnp.where((key - ahead) * 8 <= lane, e, 0.0)
            e = e.astype(BF)
            e_ref[step, :, sl] = e
            ol[:, sl] += dot(vt1[...], e)
        return carry

    lax.fori_loop(0, NY, pass1, 0)

    for n in range(tiles):
        sl = pl.ds(n * TILE, TILE)
        rl = 1.0 / ol[pl.ds(HD, 1), sl]
        ds = (dt[:, sl] * rl).astype(BF)
        dst[:, sl] = ds
        delta = rl * jnp.sum(ds.astype(F32) * ol[pl.ds(0, HD), sl], axis=0, keepdims=True)
        delta_ref[:, sl] = jnp.broadcast_to(delta, (8, TILE))
    kterm[...] = jnp.zeros((8, HD), F32)

    def summed(slot, which):
        total = own[slot, which]
        for k in range(NX - 1):
            total = total + rx[slot, k, which].astype(F32)
        return total

    def along_y(slot):
        dy = (0, 1, 3, 2)[slot]
        wait_for(rx.at[slot], rx_got.at[slot])
        for which in range(2):
            ys[slot, which] = summed(slot, which).astype(BF)
        remote(ys.at[slot], ry.at[dy - 1], ry_sent, ry_got, y_peer(dy)).start()

    span = kall.shape[2]

    def pass2(back, carry):
        step = NY - 1 - back
        chunk = chunk_at(step)
        n_keys = NX * span
        v = kall[pl.ds(chunk * NX, NX), 1].reshape(n_keys, HD)
        gk = jnp.zeros((n_keys, HD), F32)
        ahead_dp = dot(v, dst[:, pl.ds(0, TILE)])
        for n in range(tiles):
            sl = pl.ds(n * TILE, TILE)
            dp = ahead_dp
            if n + 1 < tiles:
                ahead_dp = dot(v, dst[:, pl.ds((n + 1) * TILE, TILE)])
            e = e_ref[step, :, sl].astype(F32)
            gs = (e * (dp - delta_ref[pl.ds(0, 1), sl])).astype(BF)
            gs_ref[step, :, sl] = gs
            gk += dot(gs, qn[sl, :])
        at = lax.broadcasted_iota(jnp.int32, (n_keys, HD), 0) + chunk * n_keys
        gk = jnp.where(at < plen, gk * scale, 0.0)
        kn = kn_ref[step].astype(F32)
        kterm[...] += jnp.sum((gk * kn).reshape(n_keys // 8, 8, HD), axis=0)
        sums[step] = gk
        return carry

    lax.fori_loop(0, NY, pass2, 0)

    gkr = jnp.zeros((nkr, HD), F32)
    for n in range(tiles_r):
        sl = pl.ds(n * TILE, TILE)
        dp = dot(kvr[1], dst[:, sl])
        e = er_ref[:, sl].astype(F32)
        gs = (e * (dp - delta_ref[pl.ds(0, 1), sl])).astype(BF)
        gsr_ref[:, sl] = gs
        gkr += dot(gs, qn[sl, :])
    gkr = gkr * scale
    kn = knr[...].astype(F32)
    kterm[...] += jnp.sum((gkr * kn).reshape(nkr // 8, 8, HD), axis=0)

    stores = [
        pltpu.make_async_copy(dkvr_v, dkvr_out, out_sem.at[0]),
        pltpu.make_async_copy(dq_v.at[pl.ds(0, rows_r)], dqr_out, out_sem.at[1]),
        pltpu.make_async_copy(dq_v.at[pl.ds(rows_r, rows_p)], dqp_out, out_sem.at[2]),
        pltpu.make_async_copy(dkvp_v, dkvp_out, out_sem.at[3]),
        pltpu.make_async_copy(gsend.at[3, pl.ds(0, 2)], gains_out, out_sem.at[4]),
    ]
    term = jnp.sum(kterm[...], axis=0, keepdims=True)
    qterm = term / qg_ref[...]
    key_sum = term / kg_ref[...]
    which_row = lax.broadcasted_iota(jnp.int32, (8, HD), 0)
    gsend[0] = jnp.where(
        which_row == 0,
        jnp.broadcast_to(qterm, (8, HD)),
        jnp.where(which_row == 1, jnp.broadcast_to(key_sum, (8, HD)), 0.0),
    )

    def g_start(stage):
        for k in FARTHEST_FIRST:
            pltpu.make_async_remote_copy(
                src_ref=gsend.at[stage],
                dst_ref=grecv.at[stage, stage_at[stage]],
                send_sem=g_sent,
                recv_sem=g_got.at[stage],
                device_id=partner(stage, k),
                device_id_type=MESH,
            ).start()
        grecv[stage, stage_at[stage]] = gsend[stage]

    def g_finish(stage):
        wait_for(grecv.at[stage, pl.ds(0, 7)], g_got.at[stage])
        total = grecv[stage, 0]
        for k in range(1, 8):
            total = total + grecv[stage, k]
        gsend[stage + 1] = total

    g_start(0)

    def pass3(back, carry):
        step = NY - 1 - back
        n_keys = NX * span
        at = lax.broadcasted_iota(jnp.int32, (n_keys, HD), 0) + chunk_at(step) * n_keys
        gv = dot(e_ref[step], dst[...], NT)
        vsum[...] = jnp.where(at < plen, gv, 0.0)
        for k in range(NX):
            part[step, k, 0] = sums[step, pl.ds(k * span, span), :].astype(BF)
            part[step, k, 1] = vsum[pl.ds(k * span, span), :].astype(BF)
        own[step, 0] = sums[step, pl.ds(x * span, span), :]
        own[step, 1] = vsum[pl.ds(x * span, span), :]
        for dx in (2, 1, 3):
            remote(
                part.at[step, lax.rem(x + dx, NX)],
                rx.at[step, dx - 1],
                rx_sent,
                rx_got.at[step],
                x_peer(dx),
            ).start()
        return carry

    lax.fori_loop(0, NY, pass3, 0)

    g_finish(0)
    g_start(1)

    gvr = dot(er_ref[...], dst[:, pl.ds(0, rows_r)], NT)
    ur = ukr[...]
    kf = kvr[0].astype(F32)
    inv = lax.rsqrt(jnp.mean(kf * kf, axis=-1, keepdims=True) + EPSILON)
    gu = gkr * kg_ref[...]
    dk = inv * (gu - ur * jnp.mean(gu * ur, axis=-1, keepdims=True))
    dkvr_v[0] = dk.astype(BF)
    dkvr_v[1] = gvr.astype(BF)
    stores[0].start()


    for n in range(tiles):
        sl = pl.ds(n * TILE, TILE)
        gq = dot(knt_ref[0], gs_ref[0, :, sl])
        for slot in range(1, NY):
            gq += dot(knt_ref[slot], gs_ref[slot, :, sl])
        if n < tiles_r:
            gq += dot(knrt[...], gsr_ref[:, sl])
        ut = unit_qt[:, sl]
        gu = gq * scale * gcol[...]
        back = inv_q[pl.ds(0, 1), sl] * (gu - ut * jnp.mean(gu * ut, axis=0, keepdims=True))
        dq_v[sl, :] = back.astype(BF).T
    stores[1].start()
    stores[2].start()

    g_finish(1)

    @pl.when(grp < ngrp - 1)
    def _():
        pl.semaphore_wait(z_ready, ngrp - 1 - grp)

    g_start(2)
    for slot in (3, 2, 1):
        along_y(slot)
    wait_for(rx.at[0], rx_got.at[0])
    totals = [summed(0, which) for which in range(2)]
    kf = kall[resp, 0].astype(F32)
    inv = lax.rsqrt(jnp.mean(kf * kf, axis=-1, keepdims=True) + EPSILON)
    unit = kf * inv
    wait_for(kall.at[pl.ds(0, 15)], kv_sent)
    wait_for(rx, rx_sent)

    wait_for(ry, ry_got)
    for which in range(2):
        for k in range(NY - 1):
            totals[which] = totals[which] + ry[k, which].astype(F32)
    gu = totals[0] * kg_ref[...]
    dk = inv * (gu - unit * jnp.mean(gu * unit, axis=-1, keepdims=True))
    dkvp_v[0] = dk.astype(BF)
    dkvp_v[1] = totals[1].astype(BF)
    stores[3].start()
    wait_for(ry, ry_sent)

    g_finish(2)
    stores[4].start()
    wait_for(grecv.at[:, pl.ds(0, 7)], g_sent)
    for store in stores:
        store.wait()


def hand_out(*refs):
    ins, outs, held = refs[:5], refs[5:10], refs[10:15]
    in_sem, out_sem = refs[15:]
    loads = [pltpu.make_async_copy(ins[n], held[n], in_sem.at[n]) for n in range(5)]
    stores = [pltpu.make_async_copy(held[n], outs[n], out_sem.at[n]) for n in range(5)]
    for load in loads:
        load.start()
    for load, store in zip(loads, stores):
        load.wait()
        store.start()
    for store in stores:
        store.wait()


def shards(
    q_prompt,
    q_resp,
    kv_prompt,
    kv_resp,
    dout_prompt,
    dout_resp,
    q_gain,
    k_gain,
    resp_len,
    prompt_len,
):
    span = q_prompt.shape[1]
    length = q_resp.shape[2]
    rows_r = length * 8
    rows_p = span * 8
    rows = rows_r + rows_p
    n_keys = NX * span
    any_spec = pl.BlockSpec(memory_space=pl.ANY)
    hbm = pl.BlockSpec(memory_space=pltpu.HBM)
    dma = pltpu.SemaphoreType.DMA
    out = pl.pallas_call(
        kernel,
        out_shape=(
            jax.ShapeDtypeStruct((rows_r, HD), BF),
            jax.ShapeDtypeStruct((rows_p, HD), BF),
            jax.ShapeDtypeStruct((2, span, HD), BF),
            jax.ShapeDtypeStruct((2, length, HD), BF),
            jax.ShapeDtypeStruct((2, HD), F32),
        ),
        in_specs=[hbm] * 10,
        out_specs=[any_spec] * 5,
        scratch_shapes=[
            pltpu.VMEM((1, HD), F32),
            pltpu.VMEM((1, HD), F32),
            pltpu.SMEM((1, 1), jnp.int32),
            pltpu.SMEM((1,), jnp.int32),
            pltpu.VMEM((rows, HD), BF),
            pltpu.VMEM((rows, HD), BF),
            pltpu.VMEM((2, length, HD), BF),
            pltpu.VMEM((NX * NY, 2, span, HD), BF),
            pltpu.VMEM((HD, rows), F32),
            pltpu.VMEM((8, rows), F32),
            pltpu.VMEM((HD, rows), BF),
            pltpu.VMEM((rows, HD), BF),
            pltpu.VMEM((HD, rows), F32),
            pltpu.VMEM((HD, rows), BF),
            pltpu.VMEM((8, rows), F32),
            pltpu.VMEM((HD, TILE), F32),
            pltpu.VMEM((NY, n_keys, HD), BF),
            pltpu.VMEM((NY, HD, n_keys), BF),
            pltpu.VMEM((HD + 16, n_keys), BF),
            pltpu.VMEM((length, HD), BF),
            pltpu.VMEM((HD, length), BF),
            pltpu.VMEM((length, HD), F32),
            pltpu.VMEM((NY, n_keys, rows), BF),
            pltpu.VMEM((length, rows_r), BF),
            pltpu.VMEM((NY, n_keys, rows), BF),
            pltpu.VMEM((length, rows_r), BF),
            pltpu.VMEM((HD + 16, rows), F32),
            pltpu.VMEM((NY, n_keys, HD), F32),
            pltpu.VMEM((n_keys, HD), F32),
            pltpu.VMEM((NY, NX, 2, span, HD), BF),
            pltpu.VMEM((NY, NX - 1, 2, span, HD), BF),
            pltpu.VMEM((NY, 2, span, HD), F32),
            pltpu.VMEM((NY, 2, span, HD), BF),
            pltpu.VMEM((NY - 1, 2, span, HD), BF),
            pltpu.VMEM((8, HD), F32),
            pltpu.VMEM((4, 8, HD), F32),
            pltpu.VMEM((3, 8, 8, HD), F32),
            pltpu.VMEM((rows, HD), BF),
            pltpu.VMEM((2, span, HD), BF),
            pltpu.VMEM((2, length, HD), BF),
            dma((10,)),
            dma((5,)),
            dma((NY,)),
            dma((NY - 1,)),
            dma,
            dma((NY,)),
            dma,
            dma,
            dma,
            dma((3,)),
            dma,
            pltpu.SemaphoreType.REGULAR,
        ],
        compiler_params=pltpu.CompilerParams(
            collective_id=0, has_side_effects=True, vmem_limit_bytes=62 * 2**20
        ),
        name="attention_grads",
    )(
        q_resp.reshape(rows_r, HD),
        q_prompt.reshape(rows_p, HD),
        kv_prompt.reshape(2, span, HD),
        kv_resp.reshape(2, length, HD),
        dout_resp.reshape(rows_r, HD),
        dout_prompt.reshape(rows_p, HD),
        q_gain.reshape(1, HD),
        k_gain.reshape(1, HD),
        resp_len,
        prompt_len,
    )
    out = pl.pallas_call(
        hand_out,
        out_shape=tuple(jax.ShapeDtypeStruct(a.shape, a.dtype) for a in out),
        in_specs=[any_spec] * 5,
        out_specs=[any_spec] * 5,
        scratch_shapes=[pltpu.VMEM(a.shape, a.dtype) for a in out] + [dma((5,))] * 2,
        name="hand_out",
    )(*out)
    return (
        out[1].reshape(q_prompt.shape),
        out[0].reshape(q_resp.shape),
        out[2].reshape(kv_prompt.shape),
        out[3].reshape(kv_resp.shape),
        out[4],
    )


def solution(mesh):
    return jax.shard_map(
        shards,
        mesh=mesh,
        in_specs=(
            P("grp", "resp", "head", None),
            P("grp", "resp", None, "head", None),
            P("grp", None, "resp", "head", None),
            P("grp", "resp", None, None, "head", None),
            P("grp", "resp", "head", None),
            P("grp", "resp", None, "head", None),
            P(),
            P(),
            P("grp", "resp"),
            P("grp"),
        ),
        out_specs=(
            P("grp", "resp", "head", None),
            P("grp", "resp", None, "head", None),
            P("grp", None, "resp", "head", None),
            P("grp", "resp", None, None, "head", None),
            P(),
        ),
        check_vma=False,
    )
```

```python
import functools
import math

import jax
import jax.numpy as jnp
from jax import lax
from jax.experimental import pallas as pl
from jax.experimental.pallas import tpu as pltpu
from jax.sharding import PartitionSpec as P

EPSILON = 1e-06
MESH = pl.DeviceIdType.MESH
HD = 128
BF = jnp.bfloat16
F32 = jnp.float32
NX = 4
NY = 4
TILE = 512
FARTHEST_FIRST = (4, 3, 5, 2, 6, 1, 7)
NT = (((1,), (1,)), ((), ()))
NN = (((1,), (0,)), ((), ()))


def dot(lhs, rhs, dims=NN):
    return lax.dot_general(lhs, rhs, dims, preferred_element_type=F32)


def order(step):
    return step + step // 2 - 2 * (step // 3)


def kernel(
    qr_in,
    qp_in,
    kvp_in,
    kvr_in,
    dr_in,
    dp_in,
    qg_in,
    kg_in,
    rlen_in,
    plen_in,
    dqr_out,
    dqp_out,
    dkvp_out,
    dkvr_out,
    gains_out,
    qg_ref,
    kg_ref,
    rlen_ref,
    plen_ref,
    q_nat,
    d_nat,
    kvr,
    kall,
    unit_qt,
    inv_q,
    qnt,
    qn,
    dt,
    dst,
    delta_ref,
    gcol,
    kn_ref,
    knt_ref,
    vt1,
    knr,
    knrt,
    ukr,
    e_ref,
    er_ref,
    gs_ref,
    gsr_ref,
    ol,
    sums,
    vsum,
    part,
    rx,
    own,
    ys,
    ry,
    kterm,
    gsend,
    grecv,
    dq_v,
    dkvp_v,
    dkvr_v,
    in_sem,
    out_sem,
    kvx_got,
    kvy_got,
    kv_sent,
    rx_got,
    rx_sent,
    ry_got,
    ry_sent,
    g_got,
    g_sent,
    z_ready,
):
    resp = lax.axis_index("resp")
    head = lax.axis_index("head")
    grp = lax.axis_index("grp")
    yh = resp // NX
    x = lax.rem(resp, NX)
    yl = head // 2
    core = lax.rem(head, 2)
    ngrp = 8
    y8 = 2 * yh + yl
    rows_r = qr_in.shape[0]
    rows_p = qp_in.shape[0]
    rows = rows_r + rows_p
    tiles = rows // TILE
    tiles_r = rows_r // TILE
    scale = HD**-0.5
    exp_scale = scale * math.log2(math.e)

    def partner(stage, k):
        if stage == 0:
            to = lax.rem(y8 + k, 8)
            return {"resp": (to // 2) * NX + x, "head": lax.rem(to, 2) * 2 + core}
        if stage == 1:
            to = lax.rem(2 * x + core + k, 8)
            return {"resp": yh * NX + to // 2, "head": yl * 2 + lax.rem(to, 2)}
        return {"grp": lax.rem(grp + k, ngrp)}

    stage_at = (y8, 2 * x + core, grp)

    loads = [
        pltpu.make_async_copy(kvp_in, kall.at[resp], in_sem.at[0]),
        pltpu.make_async_copy(qr_in, q_nat.at[pl.ds(0, rows_r)], in_sem.at[1]),
        pltpu.make_async_copy(qp_in, q_nat.at[pl.ds(rows_r, rows_p)], in_sem.at[2]),
        pltpu.make_async_copy(kvr_in, kvr, in_sem.at[3]),
        pltpu.make_async_copy(dr_in, d_nat.at[pl.ds(0, rows_r)], in_sem.at[4]),
        pltpu.make_async_copy(dp_in, d_nat.at[pl.ds(rows_r, rows_p)], in_sem.at[5]),
        pltpu.make_async_copy(qg_in, qg_ref, in_sem.at[6]),
        pltpu.make_async_copy(kg_in, kg_ref, in_sem.at[7]),
        pltpu.make_async_copy(rlen_in, rlen_ref, in_sem.at[8]),
        pltpu.make_async_copy(plen_in, plen_ref, in_sem.at[9]),
    ]
    loads[0].start()
    barrier = pltpu.get_barrier_semaphore()
    for k in FARTHEST_FIRST:
        for stage in (0, 1):
            pl.semaphore_signal(
                barrier, inc=1, device_id=partner(stage, k), device_id_type=MESH
            )
    for k in range(7, 0, -1):

        @pl.when(grp + k < ngrp)
        def _(k=k):
            pl.semaphore_signal(
                barrier, inc=1, device_id={"grp": grp + k}, device_id_type=MESH
            )

    loads[0].wait()
    pl.semaphore_wait(barrier, 14 + grp)

    def remote(src, dst, sent, got, to):
        return pltpu.make_async_remote_copy(
            src_ref=src,
            dst_ref=dst,
            send_sem=sent,
            recv_sem=got,
            device_id={"resp": to},
            device_id_type=MESH,
        )

    def wait_for(ref, sem):
        pltpu.make_async_copy(ref, ref, sem).wait()

    def x_peer(dx):
        return yh * NX + lax.rem(x + dx, NX)

    def y_peer(dy):
        return lax.rem(yh + dy, NY) * NX + x

    def chunk_at(slot):
        return lax.rem(yh + order(slot), NY)

    def along_x(slot):
        block = kall.at[chunk_at(slot) * NX + x]
        for dx in (2, 1, 3):
            remote(block, block, kv_sent, kvx_got.at[slot], x_peer(dx)).start()

    for dy in (2, 1, 3):
        remote(
            kall.at[resp], kall.at[resp], kv_sent, kvy_got.at[dy - 1], y_peer(dy)
        ).start()
    along_x(0)
    for load in loads[1:]:
        load.start()

    def forward(slot):
        dy = (0, 1, 3, 2)[slot]
        wait_for(kall.at[y_peer(dy)], kvy_got.at[(4 - dy) - 1])
        along_x(slot)

    forward(1)
    forward(2)

    for load in loads[6:]:
        load.wait()
    plen = plen_ref[0]
    rlen = rlen_ref[0, 0]

    gcol[...] = jnp.broadcast_to(qg_ref[...], (TILE, HD)).T
    loads[1].wait()
    loads[2].wait()
    for n in range(tiles):
        sl = pl.ds(n * TILE, TILE)
        xt = q_nat[sl, :].T.astype(F32)
        inv = lax.rsqrt(jnp.mean(xt * xt, axis=0, keepdims=True) + EPSILON)
        ut = xt * inv
        unit_qt[:, sl] = ut
        inv_q[:, sl] = jnp.broadcast_to(inv, (8, TILE))
        qt = (ut * gcol[...]).astype(BF)
        qnt[:, sl] = qt
        qn[sl, :] = qt.T

    for k in range(7, 0, -1):

        @pl.when(grp >= k)
        def _(k=k):
            pl.semaphore_signal(
                z_ready, inc=1, device_id={"grp": grp - k}, device_id_type=MESH
            )


    loads[4].wait()
    loads[5].wait()
    for n in range(tiles):
        sl = pl.ds(n * TILE, TILE)
        lane = lax.broadcasted_iota(jnp.int32, (HD, TILE), 1) + n * TILE
        if n < tiles_r:
            keep = lane < rlen * 8
        else:
            keep = lane - rows_r < (plen - rows_p // 8 * resp) * 8
        dt[:, sl] = jnp.where(keep, d_nat[sl, :].T.astype(F32), 0.0)

    forward(3)

    loads[3].wait()
    kf = kvr[0].astype(F32)
    inv_kr = lax.rsqrt(jnp.mean(kf * kf, axis=-1, keepdims=True) + EPSILON)
    ur = kf * inv_kr
    ukr[...] = ur
    kr = (ur * kg_ref[...]).astype(BF)
    knr[...] = kr
    knrt[...] = kr.T
    nkr = kr.shape[0]
    vt1[pl.ds(0, HD), pl.ds(0, nkr)] = kvr[1].T
    vt1[pl.ds(HD, 16), pl.ds(0, nkr)] = jnp.ones((16, nkr), BF)
    for n in range(tiles):
        sl = pl.ds(n * TILE, TILE)
        if n < tiles_r:
            s = dot(knr[...], qnt[:, sl])
            at = lax.broadcasted_iota(jnp.int32, s.shape, 0)
            lane = lax.broadcasted_iota(jnp.int32, s.shape, 1) + n * TILE
            e = jnp.where(at * 8 <= lane, jnp.exp2(s * exp_scale), 0.0).astype(BF)
            er_ref[:, sl] = e
            ol[:, sl] = dot(vt1[:, pl.ds(0, nkr)], e)
        else:
            ol[:, sl] = jnp.zeros((HD + 16, TILE), F32)

    def pass1(step, carry):
        chunk = chunk_at(step)
        wait_for(kall.at[pl.ds(0, NX - 1)], kvx_got.at[step])
        n_keys = NX * kall.shape[2]
        at = lax.broadcasted_iota(jnp.int32, (n_keys, HD), 0) + chunk * n_keys
        k_raw = kall[pl.ds(chunk * NX, NX), 0].reshape(n_keys, HD).astype(F32)
        inv = lax.rsqrt(jnp.mean(k_raw * k_raw, axis=-1, keepdims=True) + EPSILON)
        unit = k_raw * inv
        kf = unit * kg_ref[...]
        kn = kf.astype(BF)
        kn_ref[step] = kn
        knt_ref[step] = jnp.where(at < plen, kf, 0.0).astype(BF).T
        v = kall[pl.ds(chunk * NX, NX), 1].reshape(n_keys, HD).astype(F32)
        vt1[pl.ds(0, HD), :] = jnp.where(at < plen, v, 0.0).astype(BF).T
        lane = lax.broadcasted_iota(jnp.int32, (16, n_keys), 1) + chunk * n_keys
        vt1[pl.ds(HD, 16), :] = jnp.where(lane < plen, 1.0, 0.0).astype(BF)
        ahead_s = dot(kn, qnt[:, pl.ds(0, TILE)])
        for n in range(tiles):
            sl = pl.ds(n * TILE, TILE)
            s = ahead_s
            if n + 1 < tiles:
                ahead_s = dot(kn, qnt[:, pl.ds((n + 1) * TILE, TILE)])
            e = jnp.exp2(s * exp_scale)
            if n >= tiles_r:
                key = lax.broadcasted_iota(jnp.int32, s.shape, 0)
                lane = lax.broadcasted_iota(jnp.int32, s.shape, 1) + (n * TILE - rows_r)
                ahead = resp * (rows_p // 8) - chunk * n_keys
                e = jnp.where((key - ahead) * 8 <= lane, e, 0.0)
            e = e.astype(BF)
            e_ref[step, :, sl] = e
            ol[:, sl] += dot(vt1[...], e)
        return carry

    lax.fori_loop(0, NY, pass1, 0)

    for n in range(tiles):
        sl = pl.ds(n * TILE, TILE)
        rl = 1.0 / ol[pl.ds(HD, 1), sl]
        ds = (dt[:, sl] * rl).astype(BF)
        dst[:, sl] = ds
        delta = rl * jnp.sum(ds.astype(F32) * ol[pl.ds(0, HD), sl], axis=0, keepdims=True)
        delta_ref[:, sl] = jnp.broadcast_to(delta, (8, TILE))
    kterm[...] = jnp.zeros((8, HD), F32)

    def summed(slot, which):
        total = own[slot, which]
        for k in range(NX - 1):
            total = total + rx[slot, k, which].astype(F32)
        return total

    def along_y(slot):
        dy = (0, 1, 3, 2)[slot]
        wait_for(rx.at[slot], rx_got.at[slot])
        for which in range(2):
            ys[slot, which] = summed(slot, which).astype(BF)
        remote(ys.at[slot], ry.at[dy - 1], ry_sent, ry_got, y_peer(dy)).start()

    span = kall.shape[2]

    def pass2(back, carry):
        step = NY - 1 - back
        chunk = chunk_at(step)
        n_keys = NX * span
        v = kall[pl.ds(chunk * NX, NX), 1].reshape(n_keys, HD)
        gk = jnp.zeros((n_keys, HD), F32)
        ahead_dp = dot(v, dst[:, pl.ds(0, TILE)])
        for n in range(tiles):
            sl = pl.ds(n * TILE, TILE)
            dp = ahead_dp
            if n + 1 < tiles:
                ahead_dp = dot(v, dst[:, pl.ds((n + 1) * TILE, TILE)])
            e = e_ref[step, :, sl].astype(F32)
            gs = (e * (dp - delta_ref[pl.ds(0, 1), sl])).astype(BF)
            gs_ref[step, :, sl] = gs
            gk += dot(gs, qn[sl, :])
        at = lax.broadcasted_iota(jnp.int32, (n_keys, HD), 0) + chunk * n_keys
        gk = jnp.where(at < plen, gk * scale, 0.0)
        kn = kn_ref[step].astype(F32)
        kterm[...] += jnp.sum((gk * kn).reshape(n_keys // 8, 8, HD), axis=0)
        sums[step] = gk
        return carry

    lax.fori_loop(0, NY, pass2, 0)

    gkr = jnp.zeros((nkr, HD), F32)
    for n in range(tiles_r):
        sl = pl.ds(n * TILE, TILE)
        dp = dot(kvr[1], dst[:, sl])
        e = er_ref[:, sl].astype(F32)
        gs = (e * (dp - delta_ref[pl.ds(0, 1), sl])).astype(BF)
        gsr_ref[:, sl] = gs
        gkr += dot(gs, qn[sl, :])
    gkr = gkr * scale
    kn = knr[...].astype(F32)
    kterm[...] += jnp.sum((gkr * kn).reshape(nkr // 8, 8, HD), axis=0)

    stores = [
        pltpu.make_async_copy(dkvr_v, dkvr_out, out_sem.at[0]),
        pltpu.make_async_copy(dq_v.at[pl.ds(0, rows_r)], dqr_out, out_sem.at[1]),
        pltpu.make_async_copy(dq_v.at[pl.ds(rows_r, rows_p)], dqp_out, out_sem.at[2]),
        pltpu.make_async_copy(dkvp_v, dkvp_out, out_sem.at[3]),
        pltpu.make_async_copy(gsend.at[3, pl.ds(0, 2)], gains_out, out_sem.at[4]),
    ]
    term = jnp.sum(kterm[...], axis=0, keepdims=True)
    qterm = term / qg_ref[...]
    key_sum = term / kg_ref[...]
    which_row = lax.broadcasted_iota(jnp.int32, (8, HD), 0)
    gsend[0] = jnp.where(
        which_row == 0,
        jnp.broadcast_to(qterm, (8, HD)),
        jnp.where(which_row == 1, jnp.broadcast_to(key_sum, (8, HD)), 0.0),
    )

    def g_start(stage):
        for k in FARTHEST_FIRST:
            pltpu.make_async_remote_copy(
                src_ref=gsend.at[stage],
                dst_ref=grecv.at[stage, stage_at[stage]],
                send_sem=g_sent,
                recv_sem=g_got.at[stage],
                device_id=partner(stage, k),
                device_id_type=MESH,
            ).start()
        grecv[stage, stage_at[stage]] = gsend[stage]

    def g_finish(stage):
        wait_for(grecv.at[stage, pl.ds(0, 7)], g_got.at[stage])
        total = grecv[stage, 0]
        for k in range(1, 8):
            total = total + grecv[stage, k]
        gsend[stage + 1] = total

    g_start(0)

    def pass3(back, carry):
        step = NY - 1 - back
        n_keys = NX * span
        at = lax.broadcasted_iota(jnp.int32, (n_keys, HD), 0) + chunk_at(step) * n_keys
        gv = dot(e_ref[step], dst[...], NT)
        vsum[...] = jnp.where(at < plen, gv, 0.0)
        for k in range(NX):
            part[step, k, 0] = sums[step, pl.ds(k * span, span), :].astype(BF)
            part[step, k, 1] = vsum[pl.ds(k * span, span), :].astype(BF)
        own[step, 0] = sums[step, pl.ds(x * span, span), :]
        own[step, 1] = vsum[pl.ds(x * span, span), :]
        for dx in (2, 1, 3):
            remote(
                part.at[step, lax.rem(x + dx, NX)],
                rx.at[step, dx - 1],
                rx_sent,
                rx_got.at[step],
                x_peer(dx),
            ).start()
        return carry

    lax.fori_loop(0, NY, pass3, 0)

    g_finish(0)
    g_start(1)

    gvr = dot(er_ref[...], dst[:, pl.ds(0, rows_r)], NT)
    ur = ukr[...]
    kf = kvr[0].astype(F32)
    inv = lax.rsqrt(jnp.mean(kf * kf, axis=-1, keepdims=True) + EPSILON)
    gu = gkr * kg_ref[...]
    dk = inv * (gu - ur * jnp.mean(gu * ur, axis=-1, keepdims=True))
    dkvr_v[0] = dk.astype(BF)
    dkvr_v[1] = gvr.astype(BF)
    stores[0].start()


    for n in range(tiles):
        sl = pl.ds(n * TILE, TILE)
        gq = dot(knt_ref[0], gs_ref[0, :, sl])
        for slot in range(1, NY):
            gq += dot(knt_ref[slot], gs_ref[slot, :, sl])
        if n < tiles_r:
            gq += dot(knrt[...], gsr_ref[:, sl])
        ut = unit_qt[:, sl]
        gu = gq * scale * gcol[...]
        back = inv_q[pl.ds(0, 1), sl] * (gu - ut * jnp.mean(gu * ut, axis=0, keepdims=True))
        dq_v[sl, :] = back.astype(BF).T
    stores[1].start()
    stores[2].start()

    g_finish(1)

    @pl.when(grp < ngrp - 1)
    def _():
        pl.semaphore_wait(z_ready, ngrp - 1 - grp)

    g_start(2)
    for slot in (3, 2, 1):
        along_y(slot)
    wait_for(rx.at[0], rx_got.at[0])
    totals = [summed(0, which) for which in range(2)]
    kf = kall[resp, 0].astype(F32)
    inv = lax.rsqrt(jnp.mean(kf * kf, axis=-1, keepdims=True) + EPSILON)
    unit = kf * inv
    wait_for(kall.at[pl.ds(0, 15)], kv_sent)
    wait_for(rx, rx_sent)

    wait_for(ry, ry_got)
    for which in range(2):
        for k in range(NY - 1):
            totals[which] = totals[which] + ry[k, which].astype(F32)
    gu = totals[0] * kg_ref[...]
    dk = inv * (gu - unit * jnp.mean(gu * unit, axis=-1, keepdims=True))
    dkvp_v[0] = dk.astype(BF)
    dkvp_v[1] = totals[1].astype(BF)
    stores[3].start()
    wait_for(ry, ry_sent)

    g_finish(2)
    stores[4].start()
    wait_for(grecv.at[:, pl.ds(0, 7)], g_sent)
    for store in stores:
        store.wait()


def hand_out(*refs):
    ins, outs, held = refs[:5], refs[5:10], refs[10:15]
    in_sem, out_sem = refs[15:]
    loads = [pltpu.make_async_copy(ins[n], held[n], in_sem.at[n]) for n in range(5)]
    stores = [pltpu.make_async_copy(held[n], outs[n], out_sem.at[n]) for n in range(5)]
    for load in loads:
        load.start()
    for load, store in zip(loads, stores):
        load.wait()
        store.start()
    for store in stores:
        store.wait()


def shards(
    q_prompt,
    q_resp,
    kv_prompt,
    kv_resp,
    dout_prompt,
    dout_resp,
    q_gain,
    k_gain,
    resp_len,
    prompt_len,
):
    span = q_prompt.shape[1]
    length = q_resp.shape[2]
    rows_r = length * 8
    rows_p = span * 8
    rows = rows_r + rows_p
    n_keys = NX * span
    any_spec = pl.BlockSpec(memory_space=pl.ANY)
    hbm = pl.BlockSpec(memory_space=pltpu.HBM)
    dma = pltpu.SemaphoreType.DMA
    out = pl.pallas_call(
        kernel,
        out_shape=(
            jax.ShapeDtypeStruct((rows_r, HD), BF),
            jax.ShapeDtypeStruct((rows_p, HD), BF),
            jax.ShapeDtypeStruct((2, span, HD), BF),
            jax.ShapeDtypeStruct((2, length, HD), BF),
            jax.ShapeDtypeStruct((2, HD), F32),
        ),
        in_specs=[hbm] * 10,
        out_specs=[any_spec] * 5,
        scratch_shapes=[
            pltpu.VMEM((1, HD), F32),
            pltpu.VMEM((1, HD), F32),
            pltpu.SMEM((1, 1), jnp.int32),
            pltpu.SMEM((1,), jnp.int32),
            pltpu.VMEM((rows, HD), BF),
            pltpu.VMEM((rows, HD), BF),
            pltpu.VMEM((2, length, HD), BF),
            pltpu.VMEM((NX * NY, 2, span, HD), BF),
            pltpu.VMEM((HD, rows), F32),
            pltpu.VMEM((8, rows), F32),
            pltpu.VMEM((HD, rows), BF),
            pltpu.VMEM((rows, HD), BF),
            pltpu.VMEM((HD, rows), F32),
            pltpu.VMEM((HD, rows), BF),
            pltpu.VMEM((8, rows), F32),
            pltpu.VMEM((HD, TILE), F32),
            pltpu.VMEM((NY, n_keys, HD), BF),
            pltpu.VMEM((NY, HD, n_keys), BF),
            pltpu.VMEM((HD + 16, n_keys), BF),
            pltpu.VMEM((length, HD), BF),
            pltpu.VMEM((HD, length), BF),
            pltpu.VMEM((length, HD), F32),
            pltpu.VMEM((NY, n_keys, rows), BF),
            pltpu.VMEM((length, rows_r), BF),
            pltpu.VMEM((NY, n_keys, rows), BF),
            pltpu.VMEM((length, rows_r), BF),
            pltpu.VMEM((HD + 16, rows), F32),
            pltpu.VMEM((NY, n_keys, HD), F32),
            pltpu.VMEM((n_keys, HD), F32),
            pltpu.VMEM((NY, NX, 2, span, HD), BF),
            pltpu.VMEM((NY, NX - 1, 2, span, HD), BF),
            pltpu.VMEM((NY, 2, span, HD), F32),
            pltpu.VMEM((NY, 2, span, HD), BF),
            pltpu.VMEM((NY - 1, 2, span, HD), BF),
            pltpu.VMEM((8, HD), F32),
            pltpu.VMEM((4, 8, HD), F32),
            pltpu.VMEM((3, 8, 8, HD), F32),
            pltpu.VMEM((rows, HD), BF),
            pltpu.VMEM((2, span, HD), BF),
            pltpu.VMEM((2, length, HD), BF),
            dma((10,)),
            dma((5,)),
            dma((NY,)),
            dma((NY - 1,)),
            dma,
            dma((NY,)),
            dma,
            dma,
            dma,
            dma((3,)),
            dma,
            pltpu.SemaphoreType.REGULAR,
        ],
        compiler_params=pltpu.CompilerParams(
            collective_id=0, has_side_effects=True, vmem_limit_bytes=62 * 2**20
        ),
        name="attention_grads",
    )(
        q_resp.reshape(rows_r, HD),
        q_prompt.reshape(rows_p, HD),
        kv_prompt.reshape(2, span, HD),
        kv_resp.reshape(2, length, HD),
        dout_resp.reshape(rows_r, HD),
        dout_prompt.reshape(rows_p, HD),
        q_gain.reshape(1, HD),
        k_gain.reshape(1, HD),
        resp_len,
        prompt_len,
    )
    out = pl.pallas_call(
        hand_out,
        out_shape=tuple(jax.ShapeDtypeStruct(a.shape, a.dtype) for a in out),
        in_specs=[any_spec] * 5,
        out_specs=[any_spec] * 5,
        scratch_shapes=[pltpu.VMEM(a.shape, a.dtype) for a in out] + [dma((5,))] * 2,
        name="hand_out",
    )(*out)
    return (
        out[1].reshape(q_prompt.shape),
        out[0].reshape(q_resp.shape),
        out[2].reshape(kv_prompt.shape),
        out[3].reshape(kv_resp.shape),
        out[4],
    )


def solution(mesh):
    return jax.shard_map(
        shards,
        mesh=mesh,
        in_specs=(
            P("grp", "resp", "head", None),
            P("grp", "resp", None, "head", None),
            P("grp", None, "resp", "head", None),
            P("grp", "resp", None, None, "head", None),
            P("grp", "resp", "head", None),
            P("grp", "resp", None, "head", None),
            P(),
            P(),
            P("grp", "resp"),
            P("grp"),
        ),
        out_specs=(
            P("grp", "resp", "head", None),
            P("grp", "resp", None, "head", None),
            P("grp", None, "resp", "head", None),
            P("grp", "resp", None, None, "head", None),
            P(),
        ),
        check_vma=False,
    )
```

```python
import functools
import math

import jax
import jax.numpy as jnp
from jax import lax
from jax.experimental import pallas as pl
from jax.experimental.pallas import tpu as pltpu
from jax.sharding import PartitionSpec as P

EPSILON = 1e-06
MESH = pl.DeviceIdType.MESH
HD = 128
BF = jnp.bfloat16
F32 = jnp.float32
NX = 4
NY = 4
TILE = 512
FARTHEST_FIRST = (4, 3, 5, 2, 6, 1, 7)
NT = (((1,), (1,)), ((), ()))
NN = (((1,), (0,)), ((), ()))


def dot(lhs, rhs, dims=NN):
    return lax.dot_general(lhs, rhs, dims, preferred_element_type=F32)


def order(step):
    return step + step // 2 - 2 * (step // 3)


def kernel(
    qr_in,
    qp_in,
    kvp_in,
    kvr_in,
    dr_in,
    dp_in,
    qg_in,
    kg_in,
    rlen_in,
    plen_in,
    dqr_out,
    dqp_out,
    dkvp_out,
    dkvr_out,
    gains_out,
    qg_ref,
    kg_ref,
    rlen_ref,
    plen_ref,
    q_nat,
    d_nat,
    kvr,
    kall,
    unit_qt,
    inv_q,
    qnt,
    qn,
    dt,
    dst,
    delta_ref,
    gcol,
    kn_ref,
    knt_ref,
    vt1,
    knr,
    knrt,
    ukr,
    e_ref,
    er_ref,
    gs_ref,
    gsr_ref,
    ol,
    sums,
    vsum,
    part,
    rx,
    own,
    ys,
    ry,
    kterm,
    gsend,
    grecv,
    dq_v,
    dkvp_v,
    dkvr_v,
    in_sem,
    out_sem,
    kvx_got,
    kvy_got,
    kv_sent,
    rx_got,
    rx_sent,
    ry_got,
    ry_sent,
    g_got,
    g_sent,
    z_ready,
):
    resp = lax.axis_index("resp")
    head = lax.axis_index("head")
    grp = lax.axis_index("grp")
    yh = resp // NX
    x = lax.rem(resp, NX)
    yl = head // 2
    core = lax.rem(head, 2)
    ngrp = 8
    y8 = 2 * yh + yl
    rows_r = qr_in.shape[0]
    rows_p = qp_in.shape[0]
    rows = rows_r + rows_p
    tiles = rows // TILE
    tiles_r = rows_r // TILE
    scale = HD**-0.5
    exp_scale = scale * math.log2(math.e)

    def partner(stage, k):
        if stage == 0:
            to = lax.rem(y8 + k, 8)
            return {"resp": (to // 2) * NX + x, "head": lax.rem(to, 2) * 2 + core}
        if stage == 1:
            to = lax.rem(2 * x + core + k, 8)
            return {"resp": yh * NX + to // 2, "head": yl * 2 + lax.rem(to, 2)}
        return {"grp": lax.rem(grp + k, ngrp)}

    stage_at = (y8, 2 * x + core, grp)

    loads = [
        pltpu.make_async_copy(kvp_in, kall.at[resp], in_sem.at[0]),
        pltpu.make_async_copy(qr_in, q_nat.at[pl.ds(0, rows_r)], in_sem.at[1]),
        pltpu.make_async_copy(qp_in, q_nat.at[pl.ds(rows_r, rows_p)], in_sem.at[2]),
        pltpu.make_async_copy(kvr_in, kvr, in_sem.at[3]),
        pltpu.make_async_copy(dr_in, d_nat.at[pl.ds(0, rows_r)], in_sem.at[4]),
        pltpu.make_async_copy(dp_in, d_nat.at[pl.ds(rows_r, rows_p)], in_sem.at[5]),
        pltpu.make_async_copy(qg_in, qg_ref, in_sem.at[6]),
        pltpu.make_async_copy(kg_in, kg_ref, in_sem.at[7]),
        pltpu.make_async_copy(rlen_in, rlen_ref, in_sem.at[8]),
        pltpu.make_async_copy(plen_in, plen_ref, in_sem.at[9]),
    ]
    loads[0].start()
    barrier = pltpu.get_barrier_semaphore()
    for k in FARTHEST_FIRST:
        for stage in (0, 1):
            pl.semaphore_signal(
                barrier, inc=1, device_id=partner(stage, k), device_id_type=MESH
            )
    for k in range(7, 0, -1):

        @pl.when(grp + k < ngrp)
        def _(k=k):
            pl.semaphore_signal(
                barrier, inc=1, device_id={"grp": grp + k}, device_id_type=MESH
            )

    loads[0].wait()
    pl.semaphore_wait(barrier, 14 + grp)

    def remote(src, dst, sent, got, to):
        return pltpu.make_async_remote_copy(
            src_ref=src,
            dst_ref=dst,
            send_sem=sent,
            recv_sem=got,
            device_id={"resp": to},
            device_id_type=MESH,
        )

    def wait_for(ref, sem):
        pltpu.make_async_copy(ref, ref, sem).wait()

    def x_peer(dx):
        return yh * NX + lax.rem(x + dx, NX)

    def y_peer(dy):
        return lax.rem(yh + dy, NY) * NX + x

    def chunk_at(slot):
        return lax.rem(yh + order(slot), NY)

    def along_x(slot):
        block = kall.at[chunk_at(slot) * NX + x]
        for dx in (2, 1, 3):
            remote(block, block, kv_sent, kvx_got.at[slot], x_peer(dx)).start()

    for dy in (2, 1, 3):
        remote(
            kall.at[resp], kall.at[resp], kv_sent, kvy_got.at[dy - 1], y_peer(dy)
        ).start()
    along_x(0)
    for load in loads[1:]:
        load.start()

    def forward(slot):
        dy = (0, 1, 3, 2)[slot]
        wait_for(kall.at[y_peer(dy)], kvy_got.at[(4 - dy) - 1])
        along_x(slot)

    for load in loads[6:]:
        load.wait()
    plen = plen_ref[0]
    rlen = rlen_ref[0, 0]

    gcol[...] = jnp.broadcast_to(qg_ref[...], (TILE, HD)).T
    loads[1].wait()
    loads[2].wait()
    for n in range(tiles):
        sl = pl.ds(n * TILE, TILE)
        xt = q_nat[sl, :].T.astype(F32)
        inv = lax.rsqrt(jnp.mean(xt * xt, axis=0, keepdims=True) + EPSILON)
        ut = xt * inv
        unit_qt[:, sl] = ut
        inv_q[:, sl] = jnp.broadcast_to(inv, (8, TILE))
        qt = (ut * gcol[...]).astype(BF)
        qnt[:, sl] = qt
        qn[sl, :] = qt.T

    forward(1)
    forward(2)
    for k in range(7, 0, -1):

        @pl.when(grp >= k)
        def _(k=k):
            pl.semaphore_signal(
                z_ready, inc=1, device_id={"grp": grp - k}, device_id_type=MESH
            )


    loads[4].wait()
    loads[5].wait()
    for n in range(tiles):
        sl = pl.ds(n * TILE, TILE)
        lane = lax.broadcasted_iota(jnp.int32, (HD, TILE), 1) + n * TILE
        if n < tiles_r:
            keep = lane < rlen * 8
        else:
            keep = lane - rows_r < (plen - rows_p // 8 * resp) * 8
        dt[:, sl] = jnp.where(keep, d_nat[sl, :].T.astype(F32), 0.0)

    loads[3].wait()
    kf = kvr[0].astype(F32)
    inv_kr = lax.rsqrt(jnp.mean(kf * kf, axis=-1, keepdims=True) + EPSILON)
    ur = kf * inv_kr
    ukr[...] = ur
    kr = (ur * kg_ref[...]).astype(BF)
    knr[...] = kr
    knrt[...] = kr.T
    nkr = kr.shape[0]
    vt1[pl.ds(0, HD), pl.ds(0, nkr)] = kvr[1].T
    vt1[pl.ds(HD, 16), pl.ds(0, nkr)] = jnp.ones((16, nkr), BF)
    for n in range(tiles):
        sl = pl.ds(n * TILE, TILE)
        if n < tiles_r:
            s = dot(knr[...], qnt[:, sl])
            at = lax.broadcasted_iota(jnp.int32, s.shape, 0)
            lane = lax.broadcasted_iota(jnp.int32, s.shape, 1) + n * TILE
            e = jnp.where(at * 8 <= lane, jnp.exp2(s * exp_scale), 0.0).astype(BF)
            er_ref[:, sl] = e
            ol[:, sl] = dot(vt1[:, pl.ds(0, nkr)], e)
        else:
            ol[:, sl] = jnp.zeros((HD + 16, TILE), F32)

    forward(3)

    def pass1(step, carry):
        chunk = chunk_at(step)
        wait_for(kall.at[pl.ds(0, NX - 1)], kvx_got.at[step])
        n_keys = NX * kall.shape[2]
        at = lax.broadcasted_iota(jnp.int32, (n_keys, HD), 0) + chunk * n_keys
        k_raw = kall[pl.ds(chunk * NX, NX), 0].reshape(n_keys, HD).astype(F32)
        inv = lax.rsqrt(jnp.mean(k_raw * k_raw, axis=-1, keepdims=True) + EPSILON)
        unit = k_raw * inv
        kf = unit * kg_ref[...]
        kn = kf.astype(BF)
        kn_ref[step] = kn
        knt_ref[step] = jnp.where(at < plen, kf, 0.0).astype(BF).T
        v = kall[pl.ds(chunk * NX, NX), 1].reshape(n_keys, HD).astype(F32)
        vt1[pl.ds(0, HD), :] = jnp.where(at < plen, v, 0.0).astype(BF).T
        lane = lax.broadcasted_iota(jnp.int32, (16, n_keys), 1) + chunk * n_keys
        vt1[pl.ds(HD, 16), :] = jnp.where(lane < plen, 1.0, 0.0).astype(BF)
        ahead_s = dot(kn, qnt[:, pl.ds(0, TILE)])
        for n in range(tiles):
            sl = pl.ds(n * TILE, TILE)
            s = ahead_s
            if n + 1 < tiles:
                ahead_s = dot(kn, qnt[:, pl.ds((n + 1) * TILE, TILE)])
            e = jnp.exp2(s * exp_scale)
            if n >= tiles_r:
                key = lax.broadcasted_iota(jnp.int32, s.shape, 0)
                lane = lax.broadcasted_iota(jnp.int32, s.shape, 1) + (n * TILE - rows_r)
                ahead = resp * (rows_p // 8) - chunk * n_keys
                e = jnp.where((key - ahead) * 8 <= lane, e, 0.0)
            e = e.astype(BF)
            e_ref[step, :, sl] = e
            ol[:, sl] += dot(vt1[...], e)
        return carry

    lax.fori_loop(0, NY, pass1, 0)

    for n in range(tiles):
        sl = pl.ds(n * TILE, TILE)
        rl = 1.0 / ol[pl.ds(HD, 1), sl]
        ds = (dt[:, sl] * rl).astype(BF)
        dst[:, sl] = ds
        delta = rl * jnp.sum(ds.astype(F32) * ol[pl.ds(0, HD), sl], axis=0, keepdims=True)
        delta_ref[:, sl] = jnp.broadcast_to(delta, (8, TILE))
    kterm[...] = jnp.zeros((8, HD), F32)

    def summed(slot, which):
        total = own[slot, which]
        for k in range(NX - 1):
            total = total + rx[slot, k, which].astype(F32)
        return total

    def along_y(slot):
        dy = (0, 1, 3, 2)[slot]
        wait_for(rx.at[slot], rx_got.at[slot])
        for which in range(2):
            ys[slot, which] = summed(slot, which).astype(BF)
        remote(ys.at[slot], ry.at[dy - 1], ry_sent, ry_got, y_peer(dy)).start()

    span = kall.shape[2]

    def pass2(back, carry):
        step = NY - 1 - back
        chunk = chunk_at(step)
        n_keys = NX * span
        v = kall[pl.ds(chunk * NX, NX), 1].reshape(n_keys, HD)
        gk = jnp.zeros((n_keys, HD), F32)
        ahead_dp = dot(v, dst[:, pl.ds(0, TILE)])
        for n in range(tiles):
            sl = pl.ds(n * TILE, TILE)
            dp = ahead_dp
            if n + 1 < tiles:
                ahead_dp = dot(v, dst[:, pl.ds((n + 1) * TILE, TILE)])
            e = e_ref[step, :, sl].astype(F32)
            gs = (e * (dp - delta_ref[pl.ds(0, 1), sl])).astype(BF)
            gs_ref[step, :, sl] = gs
            gk += dot(gs, qn[sl, :])
        at = lax.broadcasted_iota(jnp.int32, (n_keys, HD), 0) + chunk * n_keys
        gk = jnp.where(at < plen, gk * scale, 0.0)
        kn = kn_ref[step].astype(F32)
        kterm[...] += jnp.sum((gk * kn).reshape(n_keys // 8, 8, HD), axis=0)
        sums[step] = gk
        return carry

    lax.fori_loop(0, NY, pass2, 0)

    gkr = jnp.zeros((nkr, HD), F32)
    for n in range(tiles_r):
        sl = pl.ds(n * TILE, TILE)
        dp = dot(kvr[1], dst[:, sl])
        e = er_ref[:, sl].astype(F32)
        gs = (e * (dp - delta_ref[pl.ds(0, 1), sl])).astype(BF)
        gsr_ref[:, sl] = gs
        gkr += dot(gs, qn[sl, :])
    gkr = gkr * scale
    kn = knr[...].astype(F32)
    kterm[...] += jnp.sum((gkr * kn).reshape(nkr // 8, 8, HD), axis=0)

    stores = [
        pltpu.make_async_copy(dkvr_v, dkvr_out, out_sem.at[0]),
        pltpu.make_async_copy(dq_v.at[pl.ds(0, rows_r)], dqr_out, out_sem.at[1]),
        pltpu.make_async_copy(dq_v.at[pl.ds(rows_r, rows_p)], dqp_out, out_sem.at[2]),
        pltpu.make_async_copy(dkvp_v, dkvp_out, out_sem.at[3]),
        pltpu.make_async_copy(gsend.at[3, pl.ds(0, 2)], gains_out, out_sem.at[4]),
    ]
    term = jnp.sum(kterm[...], axis=0, keepdims=True)
    qterm = term / qg_ref[...]
    key_sum = term / kg_ref[...]
    which_row = lax.broadcasted_iota(jnp.int32, (8, HD), 0)
    gsend[0] = jnp.where(
        which_row == 0,
        jnp.broadcast_to(qterm, (8, HD)),
        jnp.where(which_row == 1, jnp.broadcast_to(key_sum, (8, HD)), 0.0),
    )

    def g_start(stage):
        for k in FARTHEST_FIRST:
            pltpu.make_async_remote_copy(
                src_ref=gsend.at[stage],
                dst_ref=grecv.at[stage, stage_at[stage]],
                send_sem=g_sent,
                recv_sem=g_got.at[stage],
                device_id=partner(stage, k),
                device_id_type=MESH,
            ).start()
        grecv[stage, stage_at[stage]] = gsend[stage]

    def g_finish(stage):
        wait_for(grecv.at[stage, pl.ds(0, 7)], g_got.at[stage])
        total = grecv[stage, 0]
        for k in range(1, 8):
            total = total + grecv[stage, k]
        gsend[stage + 1] = total

    g_start(0)

    def pass3(back, carry):
        step = NY - 1 - back
        n_keys = NX * span
        at = lax.broadcasted_iota(jnp.int32, (n_keys, HD), 0) + chunk_at(step) * n_keys
        gv = dot(e_ref[step], dst[...], NT)
        vsum[...] = jnp.where(at < plen, gv, 0.0)
        for k in range(NX):
            part[step, k, 0] = sums[step, pl.ds(k * span, span), :].astype(BF)
            part[step, k, 1] = vsum[pl.ds(k * span, span), :].astype(BF)
        own[step, 0] = sums[step, pl.ds(x * span, span), :]
        own[step, 1] = vsum[pl.ds(x * span, span), :]
        for dx in (2, 1, 3):
            remote(
                part.at[step, lax.rem(x + dx, NX)],
                rx.at[step, dx - 1],
                rx_sent,
                rx_got.at[step],
                x_peer(dx),
            ).start()
        return carry

    pass3(0, 0)

    g_finish(0)
    g_start(1)
    pass3(1, 0)

    g_finish(1)

    @pl.when(grp < ngrp - 1)
    def _():
        pl.semaphore_wait(z_ready, ngrp - 1 - grp)

    g_start(2)
    lax.fori_loop(2, NY, pass3, 0)

    gvr = dot(er_ref[...], dst[:, pl.ds(0, rows_r)], NT)
    ur = ukr[...]
    kf = kvr[0].astype(F32)
    inv = lax.rsqrt(jnp.mean(kf * kf, axis=-1, keepdims=True) + EPSILON)
    gu = gkr * kg_ref[...]
    dk = inv * (gu - ur * jnp.mean(gu * ur, axis=-1, keepdims=True))
    dkvr_v[0] = dk.astype(BF)
    dkvr_v[1] = gvr.astype(BF)
    stores[0].start()


    for n in range(tiles):
        sl = pl.ds(n * TILE, TILE)
        gq = dot(knt_ref[0], gs_ref[0, :, sl])
        for slot in range(1, NY):
            gq += dot(knt_ref[slot], gs_ref[slot, :, sl])
        if n < tiles_r:
            gq += dot(knrt[...], gsr_ref[:, sl])
        ut = unit_qt[:, sl]
        gu = gq * scale * gcol[...]
        back = inv_q[pl.ds(0, 1), sl] * (gu - ut * jnp.mean(gu * ut, axis=0, keepdims=True))
        dq_v[sl, :] = back.astype(BF).T
    stores[1].start()
    stores[2].start()

    for slot in (3, 2, 1):
        along_y(slot)
    wait_for(rx.at[0], rx_got.at[0])
    totals = [summed(0, which) for which in range(2)]
    kf = kall[resp, 0].astype(F32)
    inv = lax.rsqrt(jnp.mean(kf * kf, axis=-1, keepdims=True) + EPSILON)
    unit = kf * inv
    wait_for(kall.at[pl.ds(0, 15)], kv_sent)
    wait_for(rx, rx_sent)

    wait_for(ry, ry_got)
    for which in range(2):
        for k in range(NY - 1):
            totals[which] = totals[which] + ry[k, which].astype(F32)
    gu = totals[0] * kg_ref[...]
    dk = inv * (gu - unit * jnp.mean(gu * unit, axis=-1, keepdims=True))
    dkvp_v[0] = dk.astype(BF)
    dkvp_v[1] = totals[1].astype(BF)
    stores[3].start()
    wait_for(ry, ry_sent)

    g_finish(2)
    stores[4].start()
    wait_for(grecv.at[:, pl.ds(0, 7)], g_sent)
    for store in stores:
        store.wait()


def hand_out(*refs):
    ins, outs, held = refs[:5], refs[5:10], refs[10:15]
    in_sem, out_sem = refs[15:]
    loads = [pltpu.make_async_copy(ins[n], held[n], in_sem.at[n]) for n in range(5)]
    stores = [pltpu.make_async_copy(held[n], outs[n], out_sem.at[n]) for n in range(5)]
    for load in loads:
        load.start()
    for load, store in zip(loads, stores):
        load.wait()
        store.start()
    for store in stores:
        store.wait()


def shards(
    q_prompt,
    q_resp,
    kv_prompt,
    kv_resp,
    dout_prompt,
    dout_resp,
    q_gain,
    k_gain,
    resp_len,
    prompt_len,
):
    span = q_prompt.shape[1]
    length = q_resp.shape[2]
    rows_r = length * 8
    rows_p = span * 8
    rows = rows_r + rows_p
    n_keys = NX * span
    any_spec = pl.BlockSpec(memory_space=pl.ANY)
    hbm = pl.BlockSpec(memory_space=pltpu.HBM)
    dma = pltpu.SemaphoreType.DMA
    out = pl.pallas_call(
        kernel,
        out_shape=(
            jax.ShapeDtypeStruct((rows_r, HD), BF),
            jax.ShapeDtypeStruct((rows_p, HD), BF),
            jax.ShapeDtypeStruct((2, span, HD), BF),
            jax.ShapeDtypeStruct((2, length, HD), BF),
            jax.ShapeDtypeStruct((2, HD), F32),
        ),
        in_specs=[hbm] * 10,
        out_specs=[any_spec] * 5,
        scratch_shapes=[
            pltpu.VMEM((1, HD), F32),
            pltpu.VMEM((1, HD), F32),
            pltpu.SMEM((1, 1), jnp.int32),
            pltpu.SMEM((1,), jnp.int32),
            pltpu.VMEM((rows, HD), BF),
            pltpu.VMEM((rows, HD), BF),
            pltpu.VMEM((2, length, HD), BF),
            pltpu.VMEM((NX * NY, 2, span, HD), BF),
            pltpu.VMEM((HD, rows), F32),
            pltpu.VMEM((8, rows), F32),
            pltpu.VMEM((HD, rows), BF),
            pltpu.VMEM((rows, HD), BF),
            pltpu.VMEM((HD, rows), F32),
            pltpu.VMEM((HD, rows), BF),
            pltpu.VMEM((8, rows), F32),
            pltpu.VMEM((HD, TILE), F32),
            pltpu.VMEM((NY, n_keys, HD), BF),
            pltpu.VMEM((NY, HD, n_keys), BF),
            pltpu.VMEM((HD + 16, n_keys), BF),
            pltpu.VMEM((length, HD), BF),
            pltpu.VMEM((HD, length), BF),
            pltpu.VMEM((length, HD), F32),
            pltpu.VMEM((NY, n_keys, rows), BF),
            pltpu.VMEM((length, rows_r), BF),
            pltpu.VMEM((NY, n_keys, rows), BF),
            pltpu.VMEM((length, rows_r), BF),
            pltpu.VMEM((HD + 16, rows), F32),
            pltpu.VMEM((NY, n_keys, HD), F32),
            pltpu.VMEM((n_keys, HD), F32),
            pltpu.VMEM((NY, NX, 2, span, HD), BF),
            pltpu.VMEM((NY, NX - 1, 2, span, HD), BF),
            pltpu.VMEM((NY, 2, span, HD), F32),
            pltpu.VMEM((NY, 2, span, HD), BF),
            pltpu.VMEM((NY - 1, 2, span, HD), BF),
            pltpu.VMEM((8, HD), F32),
            pltpu.VMEM((4, 8, HD), F32),
            pltpu.VMEM((3, 8, 8, HD), F32),
            pltpu.VMEM((rows, HD), BF),
            pltpu.VMEM((2, span, HD), BF),
            pltpu.VMEM((2, length, HD), BF),
            dma((10,)),
            dma((5,)),
            dma((NY,)),
            dma((NY - 1,)),
            dma,
            dma((NY,)),
            dma,
            dma,
            dma,
            dma((3,)),
            dma,
            pltpu.SemaphoreType.REGULAR,
        ],
        compiler_params=pltpu.CompilerParams(
            collective_id=0, has_side_effects=True, vmem_limit_bytes=62 * 2**20
        ),
        name="attention_grads",
    )(
        q_resp.reshape(rows_r, HD),
        q_prompt.reshape(rows_p, HD),
        kv_prompt.reshape(2, span, HD),
        kv_resp.reshape(2, length, HD),
        dout_resp.reshape(rows_r, HD),
        dout_prompt.reshape(rows_p, HD),
        q_gain.reshape(1, HD),
        k_gain.reshape(1, HD),
        resp_len,
        prompt_len,
    )
    out = pl.pallas_call(
        hand_out,
        out_shape=tuple(jax.ShapeDtypeStruct(a.shape, a.dtype) for a in out),
        in_specs=[any_spec] * 5,
        out_specs=[any_spec] * 5,
        scratch_shapes=[pltpu.VMEM(a.shape, a.dtype) for a in out] + [dma((5,))] * 2,
        name="hand_out",
    )(*out)
    return (
        out[1].reshape(q_prompt.shape),
        out[0].reshape(q_resp.shape),
        out[2].reshape(kv_prompt.shape),
        out[3].reshape(kv_resp.shape),
        out[4],
    )


def solution(mesh):
    return jax.shard_map(
        shards,
        mesh=mesh,
        in_specs=(
            P("grp", "resp", "head", None),
            P("grp", "resp", None, "head", None),
            P("grp", None, "resp", "head", None),
            P("grp", "resp", None, None, "head", None),
            P("grp", "resp", "head", None),
            P("grp", "resp", None, "head", None),
            P(),
            P(),
            P("grp", "resp"),
            P("grp"),
        ),
        out_specs=(
            P("grp", "resp", "head", None),
            P("grp", "resp", None, "head", None),
            P("grp", None, "resp", "head", None),
            P("grp", "resp", None, None, "head", None),
            P(),
        ),
        check_vma=False,
    )
```

```python
import functools
import math

import jax
import jax.numpy as jnp
from jax import lax
from jax.experimental import pallas as pl
from jax.experimental.pallas import tpu as pltpu
from jax.sharding import PartitionSpec as P

EPSILON = 1e-06
MESH = pl.DeviceIdType.MESH
HD = 128
BF = jnp.bfloat16
F32 = jnp.float32
NX = 4
NY = 4
TILE = 512
FARTHEST_FIRST = (4, 3, 5, 2, 6, 1, 7)
NT = (((1,), (1,)), ((), ()))
NN = (((1,), (0,)), ((), ()))


def dot(lhs, rhs, dims=NN):
    return lax.dot_general(lhs, rhs, dims, preferred_element_type=F32)


def order(step):
    return step + step // 2 - 2 * (step // 3)


def kernel(
    qr_in,
    qp_in,
    kvp_in,
    kvr_in,
    dr_in,
    dp_in,
    qg_in,
    kg_in,
    rlen_in,
    plen_in,
    dqr_out,
    dqp_out,
    dkvp_out,
    dkvr_out,
    gains_out,
    qg_ref,
    kg_ref,
    rlen_ref,
    plen_ref,
    q_nat,
    d_nat,
    kvr,
    kall,
    unit_qt,
    inv_q,
    qnt,
    qn,
    dt,
    dst,
    delta_ref,
    gcol,
    kn_ref,
    knt_ref,
    vt1,
    knr,
    knrt,
    ukr,
    e_ref,
    er_ref,
    gs_ref,
    gsr_ref,
    ol,
    sums,
    vsum,
    part,
    rx,
    own,
    ys,
    ry,
    kterm,
    gsend,
    grecv,
    dq_v,
    dkvp_v,
    dkvr_v,
    in_sem,
    out_sem,
    kvx_got,
    kvy_got,
    kv_sent,
    rx_got,
    rx_sent,
    ry_got,
    ry_sent,
    g_got,
    g_sent,
    z_ready,
):
    resp = lax.axis_index("resp")
    head = lax.axis_index("head")
    grp = lax.axis_index("grp")
    yh = resp // NX
    x = lax.rem(resp, NX)
    yl = head // 2
    core = lax.rem(head, 2)
    ngrp = 8
    y8 = 2 * yh + yl
    rows_r = qr_in.shape[0]
    rows_p = qp_in.shape[0]
    rows = rows_r + rows_p
    tiles = rows // TILE
    tiles_r = rows_r // TILE
    scale = HD**-0.5
    exp_scale = scale * math.log2(math.e)

    def partner(stage, k):
        if stage == 0:
            to = lax.rem(y8 + k, 8)
            return {"resp": (to // 2) * NX + x, "head": lax.rem(to, 2) * 2 + core}
        if stage == 1:
            to = lax.rem(2 * x + core + k, 8)
            return {"resp": yh * NX + to // 2, "head": yl * 2 + lax.rem(to, 2)}
        return {"grp": lax.rem(grp + k, ngrp)}

    stage_at = (y8, 2 * x + core, grp)

    loads = [
        pltpu.make_async_copy(kvp_in, kall.at[resp], in_sem.at[0]),
        pltpu.make_async_copy(qr_in, q_nat.at[pl.ds(0, rows_r)], in_sem.at[1]),
        pltpu.make_async_copy(qp_in, q_nat.at[pl.ds(rows_r, rows_p)], in_sem.at[2]),
        pltpu.make_async_copy(kvr_in, kvr, in_sem.at[3]),
        pltpu.make_async_copy(dr_in, d_nat.at[pl.ds(0, rows_r)], in_sem.at[4]),
        pltpu.make_async_copy(dp_in, d_nat.at[pl.ds(rows_r, rows_p)], in_sem.at[5]),
        pltpu.make_async_copy(qg_in, qg_ref, in_sem.at[6]),
        pltpu.make_async_copy(kg_in, kg_ref, in_sem.at[7]),
        pltpu.make_async_copy(rlen_in, rlen_ref, in_sem.at[8]),
        pltpu.make_async_copy(plen_in, plen_ref, in_sem.at[9]),
    ]
    loads[0].start()
    barrier = pltpu.get_barrier_semaphore()
    for k in FARTHEST_FIRST:
        for stage in (0, 1):
            pl.semaphore_signal(
                barrier, inc=1, device_id=partner(stage, k), device_id_type=MESH
            )
    for k in range(7, 0, -1):

        @pl.when(grp + k < ngrp)
        def _(k=k):
            pl.semaphore_signal(
                barrier, inc=1, device_id={"grp": grp + k}, device_id_type=MESH
            )

    loads[0].wait()
    pl.semaphore_wait(barrier, 14 + grp)

    def remote(src, dst, sent, got, to):
        return pltpu.make_async_remote_copy(
            src_ref=src,
            dst_ref=dst,
            send_sem=sent,
            recv_sem=got,
            device_id={"resp": to},
            device_id_type=MESH,
        )

    def wait_for(ref, sem):
        pltpu.make_async_copy(ref, ref, sem).wait()

    def x_peer(dx):
        return yh * NX + lax.rem(x + dx, NX)

    def y_peer(dy):
        return lax.rem(yh + dy, NY) * NX + x

    def chunk_at(slot):
        return lax.rem(yh + order(slot), NY)

    def along_x(slot):
        block = kall.at[chunk_at(slot) * NX + x]
        for dx in (2, 1, 3):
            remote(block, block, kv_sent, kvx_got.at[slot], x_peer(dx)).start()

    for dy in (2, 1, 3):
        remote(
            kall.at[resp], kall.at[resp], kv_sent, kvy_got.at[dy - 1], y_peer(dy)
        ).start()
    along_x(0)
    for load in loads[1:]:
        load.start()

    def forward(slot):
        dy = (0, 1, 3, 2)[slot]
        wait_for(kall.at[y_peer(dy)], kvy_got.at[(4 - dy) - 1])
        along_x(slot)

    for load in loads[6:]:
        load.wait()
    plen = plen_ref[0]
    rlen = rlen_ref[0, 0]

    gcol[...] = jnp.broadcast_to(qg_ref[...], (TILE, HD)).T
    loads[1].wait()
    loads[2].wait()
    for n in range(tiles):
        sl = pl.ds(n * TILE, TILE)
        xt = q_nat[sl, :].T.astype(F32)
        inv = lax.rsqrt(jnp.mean(xt * xt, axis=0, keepdims=True) + EPSILON)
        ut = xt * inv
        unit_qt[:, sl] = ut
        inv_q[:, sl] = jnp.broadcast_to(inv, (8, TILE))
        qt = (ut * gcol[...]).astype(BF)
        qnt[:, sl] = qt
        qn[sl, :] = qt.T

    forward(1)
    forward(2)
    for k in range(7, 0, -1):

        @pl.when(grp >= k)
        def _(k=k):
            pl.semaphore_signal(
                z_ready, inc=1, device_id={"grp": grp - k}, device_id_type=MESH
            )


    loads[4].wait()
    loads[5].wait()
    for n in range(tiles):
        sl = pl.ds(n * TILE, TILE)
        lane = lax.broadcasted_iota(jnp.int32, (HD, TILE), 1) + n * TILE
        if n < tiles_r:
            keep = lane < rlen * 8
        else:
            keep = lane - rows_r < (plen - rows_p // 8 * resp) * 8
        dt[:, sl] = jnp.where(keep, d_nat[sl, :].T.astype(F32), 0.0)

    loads[3].wait()
    kf = kvr[0].astype(F32)
    inv_kr = lax.rsqrt(jnp.mean(kf * kf, axis=-1, keepdims=True) + EPSILON)
    ur = kf * inv_kr
    ukr[...] = ur
    kr = (ur * kg_ref[...]).astype(BF)
    knr[...] = kr
    knrt[...] = kr.T
    nkr = kr.shape[0]
    vt1[pl.ds(0, HD), pl.ds(0, nkr)] = kvr[1].T
    vt1[pl.ds(HD, 16), pl.ds(0, nkr)] = jnp.ones((16, nkr), BF)
    for n in range(tiles):
        sl = pl.ds(n * TILE, TILE)
        if n < tiles_r:
            s = dot(knr[...], qnt[:, sl])
            at = lax.broadcasted_iota(jnp.int32, s.shape, 0)
            lane = lax.broadcasted_iota(jnp.int32, s.shape, 1) + n * TILE
            e = jnp.where(at * 8 <= lane, jnp.exp2(s * exp_scale), 0.0).astype(BF)
            er_ref[:, sl] = e
            ol[:, sl] = dot(vt1[:, pl.ds(0, nkr)], e)
        else:
            ol[:, sl] = jnp.zeros((HD + 16, TILE), F32)

    forward(3)

    def pass1(step, carry):
        chunk = chunk_at(step)
        wait_for(kall.at[pl.ds(0, NX - 1)], kvx_got.at[step])
        n_keys = NX * kall.shape[2]
        at = lax.broadcasted_iota(jnp.int32, (n_keys, HD), 0) + chunk * n_keys
        k_raw = kall[pl.ds(chunk * NX, NX), 0].reshape(n_keys, HD).astype(F32)
        inv = lax.rsqrt(jnp.mean(k_raw * k_raw, axis=-1, keepdims=True) + EPSILON)
        unit = k_raw * inv
        kf = unit * kg_ref[...]
        kn = kf.astype(BF)
        kn_ref[step] = kn
        knt_ref[step] = jnp.where(at < plen, kf, 0.0).astype(BF).T
        v = kall[pl.ds(chunk * NX, NX), 1].reshape(n_keys, HD).astype(F32)
        vt1[pl.ds(0, HD), :] = jnp.where(at < plen, v, 0.0).astype(BF).T
        lane = lax.broadcasted_iota(jnp.int32, (16, n_keys), 1) + chunk * n_keys
        vt1[pl.ds(HD, 16), :] = jnp.where(lane < plen, 1.0, 0.0).astype(BF)
        ahead_s = dot(kn, qnt[:, pl.ds(0, TILE)])
        for n in range(tiles):
            sl = pl.ds(n * TILE, TILE)
            s = ahead_s
            if n + 1 < tiles:
                ahead_s = dot(kn, qnt[:, pl.ds((n + 1) * TILE, TILE)])
            e = jnp.exp2(s * exp_scale)
            if n >= tiles_r:
                key = lax.broadcasted_iota(jnp.int32, s.shape, 0)
                lane = lax.broadcasted_iota(jnp.int32, s.shape, 1) + (n * TILE - rows_r)
                ahead = resp * (rows_p // 8) - chunk * n_keys
                e = jnp.where((key - ahead) * 8 <= lane, e, 0.0)
            e = e.astype(BF)
            e_ref[step, :, sl] = e
            ol[:, sl] += dot(vt1[...], e)
        return carry

    lax.fori_loop(0, NY, pass1, 0)

    for n in range(tiles):
        sl = pl.ds(n * TILE, TILE)
        rl = 1.0 / ol[pl.ds(HD, 1), sl]
        ds = (dt[:, sl] * rl).astype(BF)
        dst[:, sl] = ds
        delta = rl * jnp.sum(ds.astype(F32) * ol[pl.ds(0, HD), sl], axis=0, keepdims=True)
        delta_ref[:, sl] = jnp.broadcast_to(delta, (8, TILE))
    kterm[...] = jnp.zeros((8, HD), F32)

    def summed(slot, which):
        total = own[slot, which]
        for k in range(NX - 1):
            total = total + rx[slot, k, which].astype(F32)
        return total

    def along_y(slot):
        dy = (0, 1, 3, 2)[slot]
        wait_for(rx.at[slot], rx_got.at[slot])
        for which in range(2):
            ys[slot, which] = summed(slot, which).astype(BF)
        remote(ys.at[slot], ry.at[dy - 1], ry_sent, ry_got, y_peer(dy)).start()

    span = kall.shape[2]

    def pass2(back, carry):
        step = NY - 1 - back
        chunk = chunk_at(step)
        n_keys = NX * span
        v = kall[pl.ds(chunk * NX, NX), 1].reshape(n_keys, HD)
        gk = jnp.zeros((n_keys, HD), F32)
        ahead_dp = dot(v, dst[:, pl.ds(0, TILE)])
        for n in range(tiles):
            sl = pl.ds(n * TILE, TILE)
            dp = ahead_dp
            if n + 1 < tiles:
                ahead_dp = dot(v, dst[:, pl.ds((n + 1) * TILE, TILE)])
            e = e_ref[step, :, sl].astype(F32)
            gs = (e * (dp - delta_ref[pl.ds(0, 1), sl])).astype(BF)
            gs_ref[step, :, sl] = gs
            gk += dot(gs, qn[sl, :])
        at = lax.broadcasted_iota(jnp.int32, (n_keys, HD), 0) + chunk * n_keys
        gk = jnp.where(at < plen, gk * scale, 0.0)
        kn = kn_ref[step].astype(F32)
        kterm[...] += jnp.sum((gk * kn).reshape(n_keys // 8, 8, HD), axis=0)
        sums[step] = gk
        return carry

    lax.fori_loop(0, NY, pass2, 0, unroll=2)

    gkr = jnp.zeros((nkr, HD), F32)
    for n in range(tiles_r):
        sl = pl.ds(n * TILE, TILE)
        dp = dot(kvr[1], dst[:, sl])
        e = er_ref[:, sl].astype(F32)
        gs = (e * (dp - delta_ref[pl.ds(0, 1), sl])).astype(BF)
        gsr_ref[:, sl] = gs
        gkr += dot(gs, qn[sl, :])
    gkr = gkr * scale
    kn = knr[...].astype(F32)
    kterm[...] += jnp.sum((gkr * kn).reshape(nkr // 8, 8, HD), axis=0)

    stores = [
        pltpu.make_async_copy(dkvr_v, dkvr_out, out_sem.at[0]),
        pltpu.make_async_copy(dq_v.at[pl.ds(0, rows_r)], dqr_out, out_sem.at[1]),
        pltpu.make_async_copy(dq_v.at[pl.ds(rows_r, rows_p)], dqp_out, out_sem.at[2]),
        pltpu.make_async_copy(dkvp_v, dkvp_out, out_sem.at[3]),
        pltpu.make_async_copy(gsend.at[3, pl.ds(0, 2)], gains_out, out_sem.at[4]),
    ]
    term = jnp.sum(kterm[...], axis=0, keepdims=True)
    qterm = term / qg_ref[...]
    key_sum = term / kg_ref[...]
    which_row = lax.broadcasted_iota(jnp.int32, (8, HD), 0)
    gsend[0] = jnp.where(
        which_row == 0,
        jnp.broadcast_to(qterm, (8, HD)),
        jnp.where(which_row == 1, jnp.broadcast_to(key_sum, (8, HD)), 0.0),
    )

    def g_start(stage):
        for k in FARTHEST_FIRST:
            pltpu.make_async_remote_copy(
                src_ref=gsend.at[stage],
                dst_ref=grecv.at[stage, stage_at[stage]],
                send_sem=g_sent,
                recv_sem=g_got.at[stage],
                device_id=partner(stage, k),
                device_id_type=MESH,
            ).start()
        grecv[stage, stage_at[stage]] = gsend[stage]

    def g_finish(stage):
        wait_for(grecv.at[stage, pl.ds(0, 7)], g_got.at[stage])
        total = grecv[stage, 0]
        for k in range(1, 8):
            total = total + grecv[stage, k]
        gsend[stage + 1] = total

    g_start(0)

    def pass3(back, carry):
        step = NY - 1 - back
        n_keys = NX * span
        at = lax.broadcasted_iota(jnp.int32, (n_keys, HD), 0) + chunk_at(step) * n_keys
        gv = dot(e_ref[step], dst[...], NT)
        vsum[...] = jnp.where(at < plen, gv, 0.0)
        for k in range(NX):
            part[step, k, 0] = sums[step, pl.ds(k * span, span), :].astype(BF)
            part[step, k, 1] = vsum[pl.ds(k * span, span), :].astype(BF)
        own[step, 0] = sums[step, pl.ds(x * span, span), :]
        own[step, 1] = vsum[pl.ds(x * span, span), :]
        for dx in (2, 1, 3):
            remote(
                part.at[step, lax.rem(x + dx, NX)],
                rx.at[step, dx - 1],
                rx_sent,
                rx_got.at[step],
                x_peer(dx),
            ).start()
        return carry

    lax.fori_loop(0, NY, pass3, 0)

    g_finish(0)
    g_start(1)

    gvr = dot(er_ref[...], dst[:, pl.ds(0, rows_r)], NT)
    ur = ukr[...]
    kf = kvr[0].astype(F32)
    inv = lax.rsqrt(jnp.mean(kf * kf, axis=-1, keepdims=True) + EPSILON)
    gu = gkr * kg_ref[...]
    dk = inv * (gu - ur * jnp.mean(gu * ur, axis=-1, keepdims=True))
    dkvr_v[0] = dk.astype(BF)
    dkvr_v[1] = gvr.astype(BF)
    stores[0].start()


    for n in range(tiles):
        sl = pl.ds(n * TILE, TILE)
        gq = dot(knt_ref[0], gs_ref[0, :, sl])
        for slot in range(1, NY):
            gq += dot(knt_ref[slot], gs_ref[slot, :, sl])
        if n < tiles_r:
            gq += dot(knrt[...], gsr_ref[:, sl])
        ut = unit_qt[:, sl]
        gu = gq * scale * gcol[...]
        back = inv_q[pl.ds(0, 1), sl] * (gu - ut * jnp.mean(gu * ut, axis=0, keepdims=True))
        dq_v[sl, :] = back.astype(BF).T
    stores[1].start()
    stores[2].start()

    g_finish(1)

    @pl.when(grp < ngrp - 1)
    def _():
        pl.semaphore_wait(z_ready, ngrp - 1 - grp)

    g_start(2)
    for slot in (3, 2, 1):
        along_y(slot)
    wait_for(rx.at[0], rx_got.at[0])
    totals = [summed(0, which) for which in range(2)]
    kf = kall[resp, 0].astype(F32)
    inv = lax.rsqrt(jnp.mean(kf * kf, axis=-1, keepdims=True) + EPSILON)
    unit = kf * inv
    wait_for(kall.at[pl.ds(0, 15)], kv_sent)
    wait_for(rx, rx_sent)

    wait_for(ry, ry_got)
    for which in range(2):
        for k in range(NY - 1):
            totals[which] = totals[which] + ry[k, which].astype(F32)
    gu = totals[0] * kg_ref[...]
    dk = inv * (gu - unit * jnp.mean(gu * unit, axis=-1, keepdims=True))
    dkvp_v[0] = dk.astype(BF)
    dkvp_v[1] = totals[1].astype(BF)
    stores[3].start()
    wait_for(ry, ry_sent)

    g_finish(2)
    stores[4].start()
    wait_for(grecv.at[:, pl.ds(0, 7)], g_sent)
    for store in stores:
        store.wait()


def hand_out(*refs):
    ins, outs, held = refs[:5], refs[5:10], refs[10:15]
    in_sem, out_sem = refs[15:]
    loads = [pltpu.make_async_copy(ins[n], held[n], in_sem.at[n]) for n in range(5)]
    stores = [pltpu.make_async_copy(held[n], outs[n], out_sem.at[n]) for n in range(5)]
    for load in loads:
        load.start()
    for load, store in zip(loads, stores):
        load.wait()
        store.start()
    for store in stores:
        store.wait()


def shards(
    q_prompt,
    q_resp,
    kv_prompt,
    kv_resp,
    dout_prompt,
    dout_resp,
    q_gain,
    k_gain,
    resp_len,
    prompt_len,
):
    span = q_prompt.shape[1]
    length = q_resp.shape[2]
    rows_r = length * 8
    rows_p = span * 8
    rows = rows_r + rows_p
    n_keys = NX * span
    any_spec = pl.BlockSpec(memory_space=pl.ANY)
    hbm = pl.BlockSpec(memory_space=pltpu.HBM)
    dma = pltpu.SemaphoreType.DMA
    out = pl.pallas_call(
        kernel,
        out_shape=(
            jax.ShapeDtypeStruct((rows_r, HD), BF),
            jax.ShapeDtypeStruct((rows_p, HD), BF),
            jax.ShapeDtypeStruct((2, span, HD), BF),
            jax.ShapeDtypeStruct((2, length, HD), BF),
            jax.ShapeDtypeStruct((2, HD), F32),
        ),
        in_specs=[hbm] * 10,
        out_specs=[any_spec] * 5,
        scratch_shapes=[
            pltpu.VMEM((1, HD), F32),
            pltpu.VMEM((1, HD), F32),
            pltpu.SMEM((1, 1), jnp.int32),
            pltpu.SMEM((1,), jnp.int32),
            pltpu.VMEM((rows, HD), BF),
            pltpu.VMEM((rows, HD), BF),
            pltpu.VMEM((2, length, HD), BF),
            pltpu.VMEM((NX * NY, 2, span, HD), BF),
            pltpu.VMEM((HD, rows), F32),
            pltpu.VMEM((8, rows), F32),
            pltpu.VMEM((HD, rows), BF),
            pltpu.VMEM((rows, HD), BF),
            pltpu.VMEM((HD, rows), F32),
            pltpu.VMEM((HD, rows), BF),
            pltpu.VMEM((8, rows), F32),
            pltpu.VMEM((HD, TILE), F32),
            pltpu.VMEM((NY, n_keys, HD), BF),
            pltpu.VMEM((NY, HD, n_keys), BF),
            pltpu.VMEM((HD + 16, n_keys), BF),
            pltpu.VMEM((length, HD), BF),
            pltpu.VMEM((HD, length), BF),
            pltpu.VMEM((length, HD), F32),
            pltpu.VMEM((NY, n_keys, rows), BF),
            pltpu.VMEM((length, rows_r), BF),
            pltpu.VMEM((NY, n_keys, rows), BF),
            pltpu.VMEM((length, rows_r), BF),
            pltpu.VMEM((HD + 16, rows), F32),
            pltpu.VMEM((NY, n_keys, HD), F32),
            pltpu.VMEM((n_keys, HD), F32),
            pltpu.VMEM((NY, NX, 2, span, HD), BF),
            pltpu.VMEM((NY, NX - 1, 2, span, HD), BF),
            pltpu.VMEM((NY, 2, span, HD), F32),
            pltpu.VMEM((NY, 2, span, HD), BF),
            pltpu.VMEM((NY - 1, 2, span, HD), BF),
            pltpu.VMEM((8, HD), F32),
            pltpu.VMEM((4, 8, HD), F32),
            pltpu.VMEM((3, 8, 8, HD), F32),
            pltpu.VMEM((rows, HD), BF),
            pltpu.VMEM((2, span, HD), BF),
            pltpu.VMEM((2, length, HD), BF),
            dma((10,)),
            dma((5,)),
            dma((NY,)),
            dma((NY - 1,)),
            dma,
            dma((NY,)),
            dma,
            dma,
            dma,
            dma((3,)),
            dma,
            pltpu.SemaphoreType.REGULAR,
        ],
        compiler_params=pltpu.CompilerParams(
            collective_id=0, has_side_effects=True, vmem_limit_bytes=62 * 2**20
        ),
        name="attention_grads",
    )(
        q_resp.reshape(rows_r, HD),
        q_prompt.reshape(rows_p, HD),
        kv_prompt.reshape(2, span, HD),
        kv_resp.reshape(2, length, HD),
        dout_resp.reshape(rows_r, HD),
        dout_prompt.reshape(rows_p, HD),
        q_gain.reshape(1, HD),
        k_gain.reshape(1, HD),
        resp_len,
        prompt_len,
    )
    out = pl.pallas_call(
        hand_out,
        out_shape=tuple(jax.ShapeDtypeStruct(a.shape, a.dtype) for a in out),
        in_specs=[any_spec] * 5,
        out_specs=[any_spec] * 5,
        scratch_shapes=[pltpu.VMEM(a.shape, a.dtype) for a in out] + [dma((5,))] * 2,
        name="hand_out",
    )(*out)
    return (
        out[1].reshape(q_prompt.shape),
        out[0].reshape(q_resp.shape),
        out[2].reshape(kv_prompt.shape),
        out[3].reshape(kv_resp.shape),
        out[4],
    )


def solution(mesh):
    return jax.shard_map(
        shards,
        mesh=mesh,
        in_specs=(
            P("grp", "resp", "head", None),
            P("grp", "resp", None, "head", None),
            P("grp", None, "resp", "head", None),
            P("grp", "resp", None, None, "head", None),
            P("grp", "resp", "head", None),
            P("grp", "resp", None, "head", None),
            P(),
            P(),
            P("grp", "resp"),
            P("grp"),
        ),
        out_specs=(
            P("grp", "resp", "head", None),
            P("grp", "resp", None, "head", None),
            P("grp", None, "resp", "head", None),
            P("grp", "resp", None, None, "head", None),
            P(),
        ),
        check_vma=False,
    )
```
